32 devices in a mesh: dp: 8 (over y, x, core), seq: 4 (over z).
Axes of the slice: x: 2, y: 2, z: 4, core: 2. Of those that a mesh axis runs over, the one named last changes fastest.
Arguments:
- tokens: bfloat16 [8, 2048, 768], P('dp', 'seq'), may hold values from -6 to 6
- cell_lengths: int32 [8, 8], P('dp'), may hold values from 0 to 2048, as said below
- ln1_gain: float32 [768], replicated, may hold values from 0.25 to 1.75
- ln1_shift: float32 [768], replicated, may hold values from -3 to 3
- w_qkv: bfloat16 [768, 2304], replicated, may hold values from -0.21875 to 0.21875
- b_query: float32 [768], replicated, may hold values from -3 to 3
- b_value: float32 [768], replicated, may hold values from -3 to 3
- w_out: bfloat16 [768, 768], replicated, may hold values from -2.5 to 2.5
- b_out: float32 [768], replicated, may hold values from -3 to 3
- ln2_gain: float32 [768], replicated, may hold values from 0.25 to 1.75
- ln2_shift: float32 [768], replicated, may hold values from -3 to 3
- w_up: bfloat16 [768, 3072], replicated, may hold values from -0.21875 to 0.21875
- b_up: float32 [3072], replicated, may hold values from -3 to 3
- w_down: bfloat16 [3072, 768], replicated, may hold values from -0.109375 to 0.109375
- b_down: float32 [768], replicated, may hold values from -3 to 3
- cotangent: bfloat16 [8, 2048, 768], P('dp', 'seq'), may hold values from -6 to 6
Outputs:
- layer_out: bfloat16 [8, 2048, 768], P('dp', 'seq')
- tokens_grad: bfloat16 [8, 2048, 768], P('dp', 'seq')
- ln1_gain_grad: float32 [768], P('dp')
- ln1_shift_grad: float32 [768], P('dp')
- w_qkv_grad: float32 [768, 2304], P('dp')
- b_query_grad: float32 [768], P('dp')
- b_value_grad: float32 [768], P('dp')
- w_out_grad: float32 [768, 768], P('dp')
- b_out_grad: float32 [768], P('dp')
- ln2_gain_grad: float32 [768], P('dp')
- ln2_shift_grad: float32 [768], P('dp')
- w_up_grad: float32 [768, 3072], P('dp')
- b_up_grad: float32 [3072], P('dp')
- w_down_grad: float32 [3072, 768], P('dp')
- b_down_grad: float32 [768], P('dp')
The draws below stay inside these ranges and needn't reach their ends.
Inputs may be any that keep to these rules, and one draw needn't show every extreme that they name: `cell_lengths`: each row lists, in slot order, the lengths of the cells packed into one bucket of 2048 slots, and sums to 2048; an entry of 0 is an unused cell place.
All inputs are finite; a program needn't handle non-finite values.
Results may differ from the reference program's by a relative error of at most 0.015.
Values may be sent and summed in bfloat16 or wider, within the bound.
A program may use at most 192 MiB of HBM per device.

```python
import jax
import jax.numpy as jnp
from jax import lax

D = 768
HEADS = 12
HEAD = 64
FF = 3072
SLOTS = 2048
CELLS = 8
BUCKETS_ALL = 8
SEQ_SLOTS = 512


def draw_cell_lengths(key, part):
    key = jax.random.fold_in(key, 11)
    subkeys = jax.random.split(key, 5)
    bucket_rows = BUCKETS_ALL
    span_len = jax.random.randint(subkeys[0], (bucket_rows,), SLOTS - 2 * SEQ_SLOTS + 2, SLOTS + 1)
    longest = jax.random.randint(subkeys[1], (), 0, bucket_rows)
    span_len = jnp.where(jnp.arange(bucket_rows) == longest, SLOTS, span_len)
    remain = SLOTS - span_len
    lowest = jnp.maximum(0, SLOTS - SEQ_SLOTS + 1 - span_len)
    highest = jnp.minimum(remain, SEQ_SLOTS - 1)
    fraction = jax.random.randint(subkeys[2], (bucket_rows,), 0, 1 << 20)
    before = lowest + fraction * (highest - lowest + 1) // (1 << 20)
    behind = remain - before
    split_at = jax.random.randint(subkeys[3], (bucket_rows, 1), 1, CELLS - 1)
    scores = jax.random.randint(subkeys[4], (bucket_rows, CELLS - 1), 1, 1000)
    places = jnp.arange(CELLS - 1)[None, :]
    in_front = places < split_at
    front_cum = jnp.cumsum(jnp.where(in_front, scores, 0), axis=1)
    back_cum = jnp.cumsum(jnp.where(in_front, 0, scores), axis=1)
    front_edges = before[:, None] * front_cum // jnp.maximum(front_cum[:, -1:], 1)
    back_edges = behind[:, None] * back_cum // jnp.maximum(back_cum[:, -1:], 1)
    zero_col = jnp.zeros((bucket_rows, 1), front_edges.dtype)
    pieces = jnp.diff(front_edges, axis=1, prepend=zero_col) + jnp.diff(back_edges, axis=1, prepend=zero_col)
    shifted = jnp.concatenate([zero_col, pieces], axis=1)
    stretched = jnp.concatenate([pieces, zero_col], axis=1)
    cell_places = jnp.arange(CELLS)[None, :]
    lengths = jnp.where(cell_places < split_at, stretched, jnp.where(cell_places == split_at, span_len[:, None], shifted))
    return lengths.astype(jnp.int32)


def with_spikes(entries, stream_key, source, target, shards_of, factor):
    def block_of(position):
        return (jnp.arange(entries.shape[position]) // (entries.shape[position] // shards_of)).reshape((-1,) + (1,) * (entries.ndim - 1 - position))

    first = jax.random.permutation(stream_key, shards_of)[block_of(target)]
    other_side = (block_of(target) + shards_of // 2) % shards_of
    return jnp.where((block_of(source) == first) | (block_of(source) == other_side), factor * entries, entries)


def steps_of(rng, shape, cuts, least, high):
    level = 1.0
    for position, blocks in cuts:
        steps = jax.random.uniform(jax.random.fold_in(jax.random.fold_in(rng, 6), position), (blocks,), jnp.float32, least / len(cuts), high / len(cuts))
        level = level * jnp.repeat(jnp.exp(steps), shape[position] // blocks).reshape((-1,) + (1,) * (len(shape) - 1 - position))
    return level


def scatter_about(key, extent, spread, most, cuts=(), kind=jnp.bfloat16):
    level = steps_of(key, extent, cuts, -0.22, 0.18) if cuts else 1.0
    entries = jax.random.normal(key, extent, jnp.float32) * spread * level
    return jnp.minimum(jnp.maximum(entries, -most), most).astype(kind)


def noise_with(stream_key, dims, deviation, limit, cuts, heavy, kind=jnp.bfloat16):
    entries = deviation * jax.random.normal(stream_key, dims, jnp.float32)
    if cuts:
        entries = entries * steps_of(stream_key, dims, cuts, -0.22, 0.18)
    return jnp.clip(with_spikes(entries, jax.random.fold_in(stream_key, 3), *heavy), -limit, limit).astype(kind)


def setup_inputs(seed: int = 0) -> dict:
    splits = jax.random.split(jax.random.key(seed), 17)
    return {
        "tokens": scatter_about(splits[0], (BUCKETS_ALL, SLOTS, D), 1.0, 6.0, ((0, 8), (1, 4))),
        "cell_lengths": draw_cell_lengths(jax.random.fold_in(splits[16], 71), 0),
        "ln1_gain": jnp.clip(1.0 + 0.15 * jax.random.normal(splits[2], (D,), jnp.float32), 0.25, 1.75),
        "ln1_shift": scatter_about(splits[3], (D,), 0.3, 3.0, (), jnp.float32),
        "w_qkv": scatter_about(splits[4], (D, 3 * D), D ** -0.5, 0.21875),
        "b_query": scatter_about(splits[5], (D,), 0.3, 3.0, (), jnp.float32),
        "b_value": scatter_about(splits[6], (D,), 0.3, 3.0, (), jnp.float32),
        "w_out": scatter_about(splits[7], (D, D), (max(D // 128, 1)) ** -0.5, 2.5),
        "b_out": scatter_about(splits[8], (D,), 0.3, 3.0, (), jnp.float32),
        "ln2_gain": jnp.clip(1.0 + 0.15 * jax.random.normal(splits[9], (D,), jnp.float32), 0.25, 1.75),
        "ln2_shift": scatter_about(splits[10], (D,), 0.3, 3.0, (), jnp.float32),
        "w_up": scatter_about(splits[11], (D, FF), D ** -0.5, 0.21875),
        "b_up": scatter_about(splits[12], (FF,), 0.3, 3.0, (), jnp.float32),
        "w_down": scatter_about(splits[13], (FF, D), FF ** -0.5, 0.109375),
        "b_down": scatter_about(splits[14], (D,), 0.3, 3.0, (), jnp.float32),
        "cotangent": noise_with(splits[15], (BUCKETS_ALL, SLOTS, D), 1.0, 6.0, ((0, 8), (1, 4)), (0, 2, 8, 2.0)),
    }


EPS = 1e-05
ROOT_HALF = 0.7071067811865476
HIGH = lax.Precision.HIGHEST

@jax.custom_vjp
def low(v):
    return lax.optimization_barrier(v.astype(jnp.bfloat16)).astype(jnp.float32)

@jax.custom_vjp
def low_back(v):
    return v

def low_keep(v):
    return (low(v), None)

def low_pass(kept, grad):
    return (grad,)

def back_keep(v):
    return (v, None)

def back_low(kept, grad):
    return (low(grad),)
low.defvjp(low_keep, low_pass)
low_back.defvjp(back_keep, back_low)

def normalize(values, gain, shift):
    average = lax.optimization_barrier(jnp.mean(values, axis=-1, keepdims=True))
    centred = values - average
    variance = lax.optimization_barrier(jnp.mean(centred * centred, axis=-1, keepdims=True))
    return centred * lax.rsqrt(variance + EPS) * gain + shift

def gelu_exact(values):
    return 0.5 * values * (1.0 + jax.scipy.special.erf(values * ROOT_HALF))

def segments_of(lengths, slot_count):
    cell_ends = jnp.cumsum(lengths, axis=-1).astype(jnp.int32)
    places = jnp.arange(slot_count, dtype=jnp.int32)
    return lax.optimization_barrier(jnp.sum((places[:, None] >= cell_ends[..., None, :]).astype(jnp.int32), axis=-1))

def bucket_forward(params, block_tokens, segment):
    ln1_gain, ln1_shift, w_qkv, b_query, b_value, w_out, b_out, ln2_gain, ln2_shift, w_up, b_up, w_down, b_down = params
    normed_one = low(normalize(block_tokens, ln1_gain, ln1_shift))
    projected = jnp.dot(normed_one, w_qkv, precision=HIGH).reshape(SLOTS, HEADS, 3, HEAD)
    queries = low_back(low(projected[:, :, 0] + b_query.reshape(HEADS, HEAD)))
    key_part = low_back(low(projected[:, :, 1]))
    value_part = low_back(low(projected[:, :, 2] + b_value.reshape(HEADS, HEAD)))
    block_rows = min(512, SLOTS)
    scaling = HEAD ** (-0.5)

    def attend_block(block_start):
        q_block = lax.dynamic_slice_in_dim(queries, block_start, block_rows, 0)
        seg_block = lax.dynamic_slice_in_dim(segment, block_start, block_rows, 0)
        scores = low_back(jnp.einsum('qhe,khe->hqk', q_block, key_part, precision=HIGH) * scaling)
        allowed = seg_block[:, None] == segment[None, :]
        scores = jnp.where(allowed[None], scores, -1e+30)
        highest = lax.optimization_barrier(jnp.max(scores, axis=-1, keepdims=True))
        raised = jnp.exp(scores - highest)
        weights = low(raised / lax.optimization_barrier(jnp.sum(raised, axis=-1, keepdims=True)))
        return low_back(low(jnp.einsum('hqk,khe->qhe', weights, value_part, precision=HIGH)))
    starts = jnp.arange(SLOTS // block_rows, dtype=jnp.int32) * block_rows
    attended = lax.map(jax.checkpoint(attend_block), starts).reshape(SLOTS, HEADS * HEAD)
    middle = block_tokens + low_back(jnp.dot(attended, w_out, precision=HIGH) + b_out)
    normed_two = low(normalize(middle, ln2_gain, ln2_shift))
    upper = low_back(jnp.dot(normed_two, w_up, precision=HIGH) + b_up)
    hidden = low(gelu_exact(upper))
    return middle + jnp.dot(hidden, w_down, precision=HIGH) + b_down

def reference(tokens, cell_lengths, ln1_gain, ln1_shift, w_qkv, b_query, b_value, w_out, b_out, ln2_gain, ln2_shift, w_up, b_up, w_down, b_down, cotangent):
    params = (ln1_gain.astype(jnp.float32), ln1_shift.astype(jnp.float32), w_qkv.astype(jnp.float32), b_query.astype(jnp.float32), b_value.astype(jnp.float32), w_out.astype(jnp.float32), b_out.astype(jnp.float32), ln2_gain.astype(jnp.float32), ln2_shift.astype(jnp.float32), w_up.astype(jnp.float32), b_up.astype(jnp.float32), w_down.astype(jnp.float32), b_down.astype(jnp.float32))

    def one_bucket(totals, inputs):
        block_tokens, lengths, block_cot = inputs
        segment = segments_of(lengths, SLOTS)

        def forward(weights_all, inputs_f):
            return bucket_forward(weights_all, inputs_f, segment)
        result, pullback = jax.vjp(forward, params, block_tokens.astype(jnp.float32))
        param_grads, token_grads = pullback(block_cot.astype(jnp.float32))
        totals = jax.tree.map(jnp.add, totals, param_grads)
        return (totals, (result.astype(jnp.bfloat16), token_grads.astype(jnp.bfloat16)))
    zero_grads = jax.tree.map(jnp.zeros_like, params)
    totals, outputs = lax.scan(one_bucket, zero_grads, (tokens, cell_lengths, cotangent))
    return (outputs[0], outputs[1], totals[0], totals[1], totals[2], totals[3], totals[4], totals[5], totals[6], totals[7], totals[8], totals[9], totals[10], totals[11], totals[12])
```

```python
from functools import partial

import jax
import jax.numpy as jnp
from jax import lax
from jax.experimental import pallas as pl
from jax.experimental.pallas import tpu as pltpu
from jax.sharding import PartitionSpec as P

HEADS = 12
HEAD = 64
PAIRS = 6
EPS = 1e-05
ROOT_HALF = 0.7071067811865476
BIG = 1e30
MESH = pl.DeviceIdType.MESH
F32 = jnp.float32
BF = jnp.bfloat16
MIB = 1024 * 1024


def normalize(values, gain, shift):
    average = jnp.mean(values, axis=-1, keepdims=True)
    centred = values - average
    variance = jnp.mean(centred * centred, axis=-1, keepdims=True)
    return centred * lax.rsqrt(variance + EPS) * gain + shift


def gelu_exact(values):
    return 0.5 * values * (1.0 + jax.scipy.special.erf(values * ROOT_HALF))


def mm(a, b):
    return jnp.dot(a, b, preferred_element_type=F32)


def mm_nt(a, b):
    return lax.dot_general(a, b, (((1,), (1,)), ((), ())), preferred_element_type=F32)


def cell_bounds(lens_ref, index):
    start = jnp.zeros(index.shape, jnp.int32)
    end = jnp.zeros(index.shape, jnp.int32)
    at = jnp.int32(0)
    for c in range(lens_ref.shape[1]):
        after = at + lens_ref[0, c]
        start = jnp.where(index == c, at, start)
        end = jnp.where(index == c, after, end)
        at = after
    return start, end


def key_codes(lens_ref, block, rows):
    lane = lax.broadcasted_iota(jnp.int32, (1, 128), 1) % 64
    start, end = cell_bounds(lens_ref, lane)
    ones = ((lane >= 8) & (lane < 11)).astype(F32)
    slot = lax.broadcasted_iota(jnp.int32, (rows, 128), 0) + block * rows
    hot = jnp.where((slot >= start) & (slot < end), 1.0, 0.0)
    return (hot + ones).astype(BF)


def query_codes(lens_ref, block, rows):
    cell = lax.broadcasted_iota(jnp.int32, (64, 1), 0)
    start, end = cell_bounds(lens_ref, cell)
    slot = lax.broadcasted_iota(jnp.int32, (64, rows), 1) + block * rows
    inside = (slot >= start) & (slot < end)
    return jnp.where(inside | (cell >= 8), 0.0, -BIG)


def lane_halves():
    lane = lax.broadcasted_iota(jnp.int32, (1, 128), 1)
    low = jnp.where(lane < 64, 1.0, 0.0).astype(BF)
    high = jnp.where(lane < 64, 0.0, 1.0).astype(BF)
    return low, high


def sort_weights(w_ref, wp):
    depth = w_ref.shape[0]
    lane = lax.broadcasted_iota(jnp.int32, (depth, 128), 1)
    low = lane < 64
    for i in range(PAIRS):
        t0, t1, t2 = (w_ref[:, 384 * i + 128 * j : 384 * i + 128 * (j + 1)].astype(F32) for j in range(3))
        at = slice(128 * i, 128 * (i + 1))
        wp[0, :, at] = jnp.where(low, t0, t1).astype(BF)
        wp[1, :, at] = pltpu.roll(jnp.where(low, t2, t0), 64, 1).astype(BF)
        wp[2, :, at] = jnp.where(low, t1, t2).astype(BF)


def gather_kernel(
    tok, lens, gain, shift, w, bq, bv,
    kn_o, vn_o, kt_o, xt_o, qn_o, qt_o, wp_o, att_f, att_o, lse_o,
    xg, wp, kn, vn, kt, xt, qn, qt, qta, vta, acc, top, send, recv, out_sem,
):
    rows, width = tok.shape
    seq = lax.axis_size("seq")
    me = lax.axis_index("seq")
    has_left, has_right = me > 0, me < seq - 1

    barrier = pltpu.get_barrier_semaphore()

    @pl.when(has_left)
    def _():
        pl.semaphore_signal(barrier, inc=1, device_id={"seq": me - 1}, device_id_type=MESH)

    @pl.when(has_right)
    def _():
        pl.semaphore_signal(barrier, inc=1, device_id={"seq": me + 1}, device_id_type=MESH)

    xg[me] = normalize(tok[...].astype(F32), gain[...], shift[...]).astype(BF)

    @pl.when(has_left & has_right)
    def _():
        pl.semaphore_wait(barrier, 2)

    @pl.when(~(has_left & has_right))
    def _():
        pl.semaphore_wait(barrier, 1)

    def copy(way, hop, block):
        return pltpu.make_async_remote_copy(
            src_ref=xg.at[block],
            dst_ref=xg.at[block],
            send_sem=send.at[way, hop],
            recv_sem=recv.at[way, hop],
            device_id={"seq": me - 1 if way == 0 else me + 1},
            device_id_type=MESH,
        )

    def can_send(way):
        return has_left if way == 0 else has_right

    def holds(way, hop):
        return me + hop < seq if way == 0 else me - hop >= 0

    def block_of(way, hop):
        return me + hop if way == 0 else me - hop

    for way in range(2):
        @pl.when(can_send(way))
        def _():
            copy(way, 0, me).start()

    sort_weights(w, wp)
    keep_w = pltpu.make_async_copy(wp, wp_o, out_sem.at[0])
    keep_w.start()
    codes = query_codes(lens, me, rows).astype(BF)
    q = ((mm(xg[me], wp[0]) + bq[...]).astype(BF).astype(F32) * (HEAD**-0.5)).astype(BF)
    for i in range(PAIRS):
        pair = q[:, 128 * i : 128 * (i + 1)]
        qn[i] = pair
        turned = pair.T
        qt[i] = turned
        qta[2 * i, :64] = turned[:64]
        qta[2 * i, 64:] = codes
        qta[2 * i + 1, :64] = codes
        qta[2 * i + 1, 64:] = turned[64:]
    keep_q = pltpu.make_async_copy(qn, qn_o, out_sem.at[1])
    keep_q.start()
    keep_qt = pltpu.make_async_copy(qt, qt_o, out_sem.at[2])
    keep_qt.start()
    row16 = lax.broadcasted_iota(jnp.int32, (16, rows), 0)
    for h in range(HEADS):
        vta[h, 64:] = jnp.where(row16 == 0, 1.0, 0.0).astype(BF)
    acc[...] = jnp.zeros_like(acc)
    top[...] = jnp.full_like(top, -3e38)
    low, high = lane_halves()
    at_end = (me == 0) | (me == seq - 1)

    def keeps(block, step):
        return [
            pltpu.make_async_copy(kn.at[block], kn_o.at[block], out_sem.at[3 + 4 * step]),
            pltpu.make_async_copy(vn.at[block], vn_o.at[block], out_sem.at[4 + 4 * step]),
            pltpu.make_async_copy(kt.at[block], kt_o.at[block], out_sem.at[5 + 4 * step]),
            pltpu.make_async_copy(xt.at[block], xt_o.at[block], out_sem.at[6 + 4 * step]),
        ]

    def block_at(step):
        from_end = jnp.where(me == 0, step, seq - 1 - step)
        from_mid = jnp.where(step == 0, me, jnp.where(step == 1, me + 1, jnp.where(step == 2, me - 1, jnp.where(me == 1, seq - 1, 0))))
        return jnp.where(at_end, from_end, from_mid)

    def one_step(step, carry):
        for hop in range(1, 4):
            due = step == jnp.where(at_end, hop, 2 * hop - 1)
            for way in range(2):
                @pl.when(due & holds(way, hop))
                def _():
                    copy(way, hop - 1, block_of(way, hop)).wait_recv()

                    @pl.when(can_send(way))
                    def _():
                        copy(way, hop, block_of(way, hop)).start()

        block = block_at(step)
        x = xg[block]
        keys = mm(x, wp[1]).astype(BF)
        values = (mm(x, wp[2]) + bv[...]).astype(BF)
        hot = key_codes(lens, block, rows)
        hot_low, hot_high = hot * low, hot * high
        xt[block] = x.T
        for i in range(PAIRS):
            at = slice(128 * i, 128 * (i + 1))
            kn[block, i] = keys[:, at]
            kt[block, i] = keys[:, at].T
            vn[block, i] = values[:, at]
            turned = values[:, at].T
            vta[2 * i, :64] = turned[:64]
            vta[2 * i + 1, :64] = turned[64:]
        for c in keeps(block, step):
            c.start()

        def one_pair(i, carry):
            pair = kn[block, i]
            scores = [
                mm(pair * low + hot_high, qta[2 * i]),
                mm(pair * high + hot_low, qta[2 * i + 1]),
            ]
            for j in range(2):
                h = 2 * i + j
                before = top[h]
                now = jnp.maximum(before, jnp.max(scores[j], axis=0, keepdims=True))
                raised = jnp.exp(scores[j] - now).astype(BF)
                top[h] = now
                acc[h] = acc[h] * jnp.exp(before - now) + mm(vta[h], raised)
            return carry

        lax.fori_loop(0, PAIRS, one_pair, 0)
        return carry

    lax.fori_loop(0, seq, one_step, 0)

    lse_o[...] = jnp.zeros_like(lse_o)
    for h in range(HEADS):
        total = acc[h, 64:65]
        lse_o[h : h + 1] = top[h] + jnp.log(total)
        att_f[64 * h : 64 * (h + 1)] = acc[h, :64] / total
    att_o[...] = att_f[...].T.astype(BF)

    for way in range(2):
        for hop in range(3):
            @pl.when(can_send(way) & holds(way, hop))
            def _():
                copy(way, hop, block_of(way, hop)).wait_send()

    keep_w.wait()
    keep_q.wait()
    keep_qt.wait()
    for step in range(4):
        for c in keeps(block_at(step), step):
            c.wait()


def gather_attend(tokens, lens, gain, shift, w, bq, bv, seq):
    rows, width = tokens.shape
    any_spec = pl.BlockSpec(memory_space=pl.ANY)
    vmem = pl.BlockSpec(memory_space=pltpu.VMEM)
    sds = jax.ShapeDtypeStruct
    outs = [
        sds((seq, PAIRS, rows, 128), BF),
        sds((seq, PAIRS, rows, 128), BF),
        sds((seq, PAIRS, 128, rows), BF),
        sds((seq, width, rows), BF),
        sds((PAIRS, rows, 128), BF),
        sds((PAIRS, 128, rows), BF),
        sds((3, width, width), BF),
        sds((width, rows), F32),
        sds((rows, width), BF),
        sds((16, rows), F32),
    ]
    return pl.pallas_call(
        gather_kernel,
        out_shape=outs,
        in_specs=[vmem, pl.BlockSpec(memory_space=pltpu.SMEM)] + [vmem] * 5,
        out_specs=[any_spec] * 7 + [vmem] * 3,
        scratch_shapes=[
            pltpu.VMEM((seq, rows, width), BF),
            pltpu.VMEM((3, width, width), BF),
            pltpu.VMEM((seq, PAIRS, rows, 128), BF),
            pltpu.VMEM((seq, PAIRS, rows, 128), BF),
            pltpu.VMEM((seq, PAIRS, 128, rows), BF),
            pltpu.VMEM((seq, width, rows), BF),
            pltpu.VMEM((PAIRS, rows, 128), BF),
            pltpu.VMEM((PAIRS, 128, rows), BF),
            pltpu.VMEM((HEADS, 128, rows), BF),
            pltpu.VMEM((HEADS, 80, rows), BF),
            pltpu.VMEM((HEADS, 80, rows), F32),
            pltpu.VMEM((HEADS, 1, rows), F32),
            pltpu.SemaphoreType.DMA((2, 4)),
            pltpu.SemaphoreType.DMA((2, 4)),
            pltpu.SemaphoreType.DMA((20,)),
        ],
        compiler_params=pltpu.CompilerParams(
            collective_id=0, has_side_effects=True, vmem_limit_bytes=56 * MIB
        ),
        name="gather_attend",
    )(tokens, lens, gain, shift, w, bq, bv)


def three_parts(values):
    high = values.astype(BF).astype(F32)
    middle = (values - high).astype(BF).astype(F32)
    return high, middle, values - high - middle


def attend_back_kernel(
    kn_h, vn_h, kt_h, xt_h, qn, qt, d_att, d_att_t, delta, lse, wp, lens,
    dx_o, gw_o, gbias_o,
    kn, vn, kt, xt, qta, dta, qh, dh, dqt, gk, gv, dk, dv, in_sem,
):
    rows, width = d_att.shape
    seq = lax.axis_size("seq")
    me = lax.axis_index("seq")

    def block_at(step):
        b0 = jnp.where(me < 2, seq - 1, 0)
        b1 = jnp.where(me < 2, seq - 2, 1)
        b2 = jnp.where(me == 0, 1, jnp.where(me == 1, 0, jnp.where(me == 2, 3, 2)))
        return jnp.where(step == 0, b0, jnp.where(step == 1, b1, jnp.where(step == 2, b2, me)))

    def loads(step):
        block = block_at(step)
        return [
            pltpu.make_async_copy(kn_h.at[block], kn.at[step], in_sem.at[step, 0]),
            pltpu.make_async_copy(vn_h.at[block], vn.at[step], in_sem.at[step, 1]),
            pltpu.make_async_copy(kt_h.at[block], kt.at[step], in_sem.at[step, 2]),
            pltpu.make_async_copy(xt_h.at[block], xt.at[step], in_sem.at[step, 3]),
        ]

    for step in range(4):
        for c in loads(step):
            c.start()

    low, high = lane_halves()
    codes = query_codes(lens, me, rows)
    row64 = lax.broadcasted_iota(jnp.int32, (64, rows), 0)
    for h in range(HEADS):
        i, j = h // 2, h % 2
        own, other = (slice(0, 64), slice(64, 128)) if j == 0 else (slice(64, 128), slice(0, 64))
        extra = codes
        for r, part in enumerate(three_parts(-lse[h : h + 1])):
            extra = jnp.where(row64 == 8 + r, part, extra)
        qta[h, own] = qt[i, own]
        qta[h, other] = extra.astype(BF)
        extra = jnp.zeros((64, rows), F32)
        for r, part in enumerate(three_parts(-delta[h : h + 1])):
            extra = jnp.where(row64 == r, part, extra)
        dta[h, own] = d_att_t[64 * h : 64 * (h + 1)]
        dta[h, other] = extra.astype(BF)
        half = low if j == 0 else high
        qh[h] = qn[i] * half
        dh[h] = d_att[:, 128 * i : 128 * (i + 1)] * half
    dqt[...] = jnp.zeros_like(dqt)
    gk[...] = jnp.zeros_like(gk)
    gv[...] = jnp.zeros_like(gv)
    gbias_o[...] = jnp.zeros_like(gbias_o)
    lane = lax.broadcasted_iota(jnp.int32, (1, 128), 1)
    v_low = jnp.where(lane < 3, 1.0, 0.0).astype(BF)
    v_high = jnp.where((lane >= 64) & (lane < 67), 1.0, 0.0).astype(BF)

    def one_step(step, carry):
        for c in loads(step):
            c.wait()
        block = block_at(step)
        hot = key_codes(lens, block, rows)
        hot_low, hot_high = hot * low, hot * high

        def one_pair(i, carry):
            keys, values = kn[step, i], vn[step, i]
            scores = [
                mm(keys * low + hot_high, qta[2 * i]),
                mm(keys * high + hot_low, qta[2 * i + 1]),
            ]
            slopes = [
                mm(values * low + v_high, dta[2 * i]),
                mm(values * high + v_low, dta[2 * i + 1]),
            ]
            d_keys = jnp.zeros((rows, 128), F32)
            d_values = jnp.zeros((rows, 128), F32)
            for j in range(2):
                h = 2 * i + j
                probs = jnp.exp(scores[j])
                d_scores = (probs * slopes[j]).astype(BF)
                d_values = d_values + mm(probs.astype(BF), dh[h])
                d_keys = d_keys + mm(d_scores, qh[h])
                dqt[h] += mm(kt[step, i, 64 * j : 64 * (j + 1)], d_scores)
            at = pl.ds(pl.multiple_of(i * 128, 128), 128)
            dk[:, at] = d_keys.astype(BF)
            dv[:, at] = d_values.astype(BF)
            return carry

        lax.fori_loop(0, PAIRS, one_pair, 0)
        dx = mm_nt(dk[...], wp[1]) + mm_nt(dv[...], wp[2])
        gk[...] += mm(xt[step], dk[...])
        gv[...] += mm(xt[step], dv[...])
        gbias_o[1:2] += jnp.sum(dv[...].astype(F32), axis=0, keepdims=True)

        @pl.when(step < seq - 1)
        def _():
            dx_o[block] = dx.astype(BF)

        @pl.when(step == seq - 1)
        def _():
            turned = (dqt[...] * (HEAD**-0.5)).reshape(width, rows).T
            dq = turned.astype(BF)
            dx_o[block] = (dx + mm_nt(dq, wp[0])).astype(BF)
            gbias_o[0:1] = jnp.sum(dq.astype(F32), axis=0, keepdims=True)
            gq = mm(xt[step], dq)
            lane_w = lax.broadcasted_iota(jnp.int32, (width, 128), 1)
            lo = lane_w < 64
            for i in range(PAIRS):
                at = slice(128 * i, 128 * (i + 1))
                k_turned = pltpu.roll(gk[:, at], 64, 1)
                t0 = jnp.where(lo, gq[:, at], k_turned)
                t1 = jnp.where(lo, gv[:, at], gq[:, at])
                t2 = jnp.where(lo, k_turned, gv[:, at])
                for j, t in enumerate((t0, t1, t2)):
                    gw_o[:, 384 * i + 128 * j : 384 * i + 128 * (j + 1)] = t.astype(BF)

        return carry

    lax.fori_loop(0, seq, one_step, 0)


def attend_back(kn, vn, kt, xt, qn, qt, d_att, d_att_t, delta, lse, wp, lens):
    seq, _, rows, _ = kn.shape
    width = wp.shape[1]
    any_spec = pl.BlockSpec(memory_space=pl.ANY)
    vmem = pl.BlockSpec(memory_space=pltpu.VMEM)
    sds = jax.ShapeDtypeStruct
    return pl.pallas_call(
        attend_back_kernel,
        out_shape=[
            sds((seq, rows, width), BF),
            sds((width, 3 * width), BF),
            sds((8, width), F32),
        ],
        in_specs=[any_spec] * 4 + [vmem] * 7 + [pl.BlockSpec(memory_space=pltpu.SMEM)],
        out_specs=[vmem] * 3,
        scratch_shapes=[
            pltpu.VMEM((seq, PAIRS, rows, 128), BF),
            pltpu.VMEM((seq, PAIRS, rows, 128), BF),
            pltpu.VMEM((seq, PAIRS, 128, rows), BF),
            pltpu.VMEM((seq, width, rows), BF),
            pltpu.VMEM((HEADS, 128, rows), BF),
            pltpu.VMEM((HEADS, 128, rows), BF),
            pltpu.VMEM((HEADS, rows, 128), BF),
            pltpu.VMEM((HEADS, rows, 128), BF),
            pltpu.VMEM((HEADS, HEAD, rows), F32),
            pltpu.VMEM((width, width), F32),
            pltpu.VMEM((width, width), F32),
            pltpu.VMEM((rows, width), BF),
            pltpu.VMEM((rows, width), BF),
            pltpu.SemaphoreType.DMA((4, 4)),
        ],
        compiler_params=pltpu.CompilerParams(vmem_limit_bytes=58 * MIB),
        name="attend_back",
    )(kn, vn, kt, xt, qn, qt, d_att, d_att_t, delta, lse, wp, lens)


def local(
    tokens, cell_lengths, ln1_gain, ln1_shift, w_qkv, b_query, b_value, w_out, b_out,
    ln2_gain, ln2_shift, w_up, b_up, w_down, b_down, cotangent,
):
    bucket_count, local_slots, width = tokens.shape
    seq_count = lax.axis_size("seq")
    dp_count = lax.axis_size("dp")
    rows = bucket_count * local_slots
    flat = tokens.reshape(rows, width)
    flat_tokens = flat.astype(F32)

    def row(v):
        return v.reshape(1, -1)

    kn, vn, kt, xt, qn, qt, wp, att_t, attended, lse = gather_attend(
        flat, cell_lengths, row(ln1_gain), row(ln1_shift), w_qkv, row(b_query), row(b_value), seq_count
    )
    middle = flat_tokens + mm(attended, w_out) + b_out
    normed_two = normalize(middle, ln2_gain, ln2_shift).astype(BF)
    upper = mm(normed_two, w_up) + b_up
    hidden = gelu_exact(upper).astype(BF)
    layer_out = middle + mm(hidden, w_down) + b_down
    layer_out = layer_out.astype(BF).reshape(tokens.shape)
    d_output = cotangent.reshape(rows, width)
    g_w_down = mm(hidden.T, d_output).astype(BF)
    g_b_down = jnp.sum(d_output, axis=0, dtype=F32)
    d_hidden = mm(d_output, w_down.T)
    gelu_pull = jax.vjp(gelu_exact, upper)[1]
    d_upper = gelu_pull(d_hidden)[0].astype(BF)
    g_w_up = mm(normed_two.T, d_upper).astype(BF)
    g_b_up = jnp.sum(d_upper, axis=0, dtype=F32)
    d_normed_two = mm(d_upper, w_up.T)
    second_pull = jax.vjp(normalize, middle, ln2_gain, ln2_shift)[1]
    d_middle, g_ln2_gain, g_ln2_shift = second_pull(d_normed_two)
    d_middle = d_middle + d_output.astype(F32)
    d_branch = d_middle.astype(BF)
    g_w_out = mm(attended.T, d_branch).astype(BF)
    g_b_out = jnp.sum(d_branch, axis=0, dtype=F32)
    d_att = mm(d_branch, w_out.T).astype(BF)
    d_att_t = d_att.T
    delta = jnp.sum((d_att_t.astype(F32) * att_t).reshape(HEADS, HEAD, rows), axis=1)
    delta = jnp.pad(delta, ((0, 4), (0, 0)))
    dx, g_w_qkv, g_bias = attend_back(kn, vn, kt, xt, qn, qt, d_att, d_att_t, delta, lse, wp, cell_lengths)
    d_normed_one = lax.psum_scatter(dx, "seq", scatter_dimension=0, tiled=True).reshape(rows, width).astype(F32)
    first_pull = jax.vjp(normalize, flat_tokens, ln1_gain, ln1_shift)[1]
    d_tokens, g_ln1_gain, g_ln1_shift = first_pull(d_normed_one)
    tokens_grad = (d_tokens + d_middle).astype(BF).reshape(tokens.shape)

    def summed(g):
        share = lax.psum_scatter(g, "dp", scatter_dimension=0, tiled=True)
        return lax.psum(share, "seq").astype(F32)

    g_w_down, g_w_up, g_w_out, g_w_qkv = summed(g_w_down), summed(g_w_up), summed(g_w_out), summed(g_w_qkv)
    vectors = (g_ln1_gain, g_ln1_shift, g_bias[0], g_bias[1], g_b_out, g_ln2_gain, g_ln2_shift, g_b_up, g_b_down)
    packed = jnp.concatenate([v.reshape(dp_count, -1) for v in vectors], axis=1)
    packed = lax.psum(packed, ("dp", "seq"))
    mine = lax.dynamic_index_in_dim(packed, lax.axis_index("dp"), 0, keepdims=False)
    parts, at = [], 0
    for v in vectors:
        size = v.shape[0] // dp_count
        parts.append(mine[at : at + size])
        at += size
    return (
        layer_out, tokens_grad, parts[0], parts[1], g_w_qkv, parts[2], parts[3], g_w_out, parts[4],
        parts[5], parts[6], g_w_up, parts[7], g_w_down, parts[8],
    )


def solution(mesh):
    token_spec = P("dp", "seq", None)
    vector, matrix = P("dp"), P("dp", None)
    placed = (token_spec, P("dp", None)) + (P(),) * 13 + (token_spec,)
    return jax.shard_map(
        local,
        mesh=mesh,
        in_specs=placed,
        out_specs=(
            token_spec, token_spec, vector, vector, matrix, vector, vector, matrix, vector,
            vector, vector, matrix, vector, matrix, vector,
        ),
        check_vma=False,
    )
```

```python
from functools import partial

import jax
import jax.numpy as jnp
from jax import lax
from jax.experimental import pallas as pl
from jax.experimental.pallas import tpu as pltpu
from jax.sharding import PartitionSpec as P

HEADS = 12
HEAD = 64
PAIRS = 6
EPS = 1e-05
ROOT_HALF = 0.7071067811865476
BIG = 1e30
MESH = pl.DeviceIdType.MESH
F32 = jnp.float32
BF = jnp.bfloat16
MIB = 1024 * 1024


def normalize(values, gain, shift):
    average = jnp.mean(values, axis=-1, keepdims=True)
    centred = values - average
    variance = jnp.mean(centred * centred, axis=-1, keepdims=True)
    return centred * lax.rsqrt(variance + EPS) * gain + shift


def gelu_exact(values):
    return 0.5 * values * (1.0 + jax.scipy.special.erf(values * ROOT_HALF))


def mm(a, b):
    return jnp.dot(a, b, preferred_element_type=F32)


def mm_nt(a, b):
    return lax.dot_general(a, b, (((1,), (1,)), ((), ())), preferred_element_type=F32)


def cell_bounds(lens_ref, index):
    start = jnp.zeros(index.shape, jnp.int32)
    end = jnp.zeros(index.shape, jnp.int32)
    at = jnp.int32(0)
    for c in range(lens_ref.shape[1]):
        after = at + lens_ref[0, c]
        start = jnp.where(index == c, at, start)
        end = jnp.where(index == c, after, end)
        at = after
    return start, end


def key_codes(lens_ref, block, rows):
    lane = lax.broadcasted_iota(jnp.int32, (1, 128), 1) % 64
    start, end = cell_bounds(lens_ref, lane)
    ones = ((lane >= 8) & (lane < 11)).astype(F32)
    slot = lax.broadcasted_iota(jnp.int32, (rows, 128), 0) + block * rows
    hot = jnp.where((slot >= start) & (slot < end), 1.0, 0.0)
    return (hot + ones).astype(BF)


def query_codes(lens_ref, block, rows):
    cell = lax.broadcasted_iota(jnp.int32, (64, 1), 0)
    start, end = cell_bounds(lens_ref, cell)
    slot = lax.broadcasted_iota(jnp.int32, (64, rows), 1) + block * rows
    inside = (slot >= start) & (slot < end)
    return jnp.where(inside | (cell >= 8), 0.0, -BIG)


def lane_halves():
    lane = lax.broadcasted_iota(jnp.int32, (1, 128), 1)
    low = jnp.where(lane < 64, 1.0, 0.0).astype(BF)
    high = jnp.where(lane < 64, 0.0, 1.0).astype(BF)
    return low, high


def sort_weights(w_ref, wp):
    depth = w_ref.shape[0]
    lane = lax.broadcasted_iota(jnp.int32, (depth, 128), 1)
    low = lane < 64
    for i in range(PAIRS):
        t0, t1, t2 = (w_ref[:, 384 * i + 128 * j : 384 * i + 128 * (j + 1)].astype(F32) for j in range(3))
        at = slice(128 * i, 128 * (i + 1))
        wp[0, :, at] = jnp.where(low, t0, t1).astype(BF)
        wp[1, :, at] = pltpu.roll(jnp.where(low, t2, t0), 64, 1).astype(BF)
        wp[2, :, at] = jnp.where(low, t1, t2).astype(BF)


def gather_kernel(
    tok, lens, gain, shift, w, bq, bv,
    kn_o, vn_o, kt_o, xt_o, qn_o, qt_o, wp_o, att_f, att_o, lse_o,
    xg, wp, kn, vn, kt, xt, qn, qt, qta, vta, acc, top, send, recv, out_sem,
):
    rows, width = tok.shape
    seq = lax.axis_size("seq")
    me = lax.axis_index("seq")
    has_left, has_right = me > 0, me < seq - 1

    barrier = pltpu.get_barrier_semaphore()

    @pl.when(has_left)
    def _():
        pl.semaphore_signal(barrier, inc=1, device_id={"seq": me - 1}, device_id_type=MESH)

    @pl.when(has_right)
    def _():
        pl.semaphore_signal(barrier, inc=1, device_id={"seq": me + 1}, device_id_type=MESH)

    xg[me] = normalize(tok[...].astype(F32), gain[...].reshape(1, -1), shift[...].reshape(1, -1)).astype(BF)

    @pl.when(has_left & has_right)
    def _():
        pl.semaphore_wait(barrier, 2)

    @pl.when(~(has_left & has_right))
    def _():
        pl.semaphore_wait(barrier, 1)

    def copy(way, hop, block):
        return pltpu.make_async_remote_copy(
            src_ref=xg.at[block],
            dst_ref=xg.at[block],
            send_sem=send.at[way, hop],
            recv_sem=recv.at[way, hop],
            device_id={"seq": me - 1 if way == 0 else me + 1},
            device_id_type=MESH,
        )

    def can_send(way):
        return has_left if way == 0 else has_right

    def holds(way, hop):
        return me + hop < seq if way == 0 else me - hop >= 0

    def block_of(way, hop):
        return me + hop if way == 0 else me - hop

    for way in range(2):
        @pl.when(can_send(way))
        def _():
            copy(way, 0, me).start()

    sort_weights(w, wp)
    keep_w = pltpu.make_async_copy(wp, wp_o, out_sem.at[0])
    keep_w.start()
    codes = query_codes(lens, me, rows).astype(BF)
    q = ((mm(xg[me], wp[0]) + bq[...].reshape(1, -1)).astype(BF).astype(F32) * (HEAD**-0.5)).astype(BF)
    for i in range(PAIRS):
        pair = q[:, 128 * i : 128 * (i + 1)]
        qn[i] = pair
        turned = pair.T
        qt[i] = turned
        qta[2 * i, :64] = turned[:64]
        qta[2 * i, 64:] = codes
        qta[2 * i + 1, :64] = codes
        qta[2 * i + 1, 64:] = turned[64:]
    keep_q = pltpu.make_async_copy(qn, qn_o, out_sem.at[1])
    keep_q.start()
    keep_qt = pltpu.make_async_copy(qt, qt_o, out_sem.at[2])
    keep_qt.start()
    row16 = lax.broadcasted_iota(jnp.int32, (16, rows), 0)
    for h in range(HEADS):
        vta[h, 64:] = jnp.where(row16 == 0, 1.0, 0.0).astype(BF)
    acc[...] = jnp.zeros_like(acc)
    top[...] = jnp.full_like(top, -3e38)
    low, high = lane_halves()
    at_end = (me == 0) | (me == seq - 1)

    def keeps(block, step):
        return [
            pltpu.make_async_copy(kn.at[block], kn_o.at[block], out_sem.at[3 + 4 * step]),
            pltpu.make_async_copy(vn.at[block], vn_o.at[block], out_sem.at[4 + 4 * step]),
            pltpu.make_async_copy(kt.at[block], kt_o.at[block], out_sem.at[5 + 4 * step]),
            pltpu.make_async_copy(xt.at[block], xt_o.at[block], out_sem.at[6 + 4 * step]),
        ]

    def block_at(step):
        from_end = jnp.where(me == 0, step, seq - 1 - step)
        from_mid = jnp.where(step == 0, me, jnp.where(step == 1, me + 1, jnp.where(step == 2, me - 1, jnp.where(me == 1, seq - 1, 0))))
        return jnp.where(at_end, from_end, from_mid)

    def one_step(step, carry):
        for hop in range(1, 4):
            due = step == jnp.where(at_end, hop, 2 * hop - 1)
            for way in range(2):
                @pl.when(due & holds(way, hop))
                def _():
                    copy(way, hop - 1, block_of(way, hop)).wait_recv()

                    @pl.when(can_send(way))
                    def _():
                        copy(way, hop, block_of(way, hop)).start()

        block = block_at(step)
        x = xg[block]
        keys = mm(x, wp[1]).astype(BF)
        values = (mm(x, wp[2]) + bv[...].reshape(1, -1)).astype(BF)
        hot = key_codes(lens, block, rows)
        hot_low, hot_high = hot * low, hot * high
        xt[block] = x.T
        for i in range(PAIRS):
            at = slice(128 * i, 128 * (i + 1))
            kn[block, i] = keys[:, at]
            kt[block, i] = keys[:, at].T
            vn[block, i] = values[:, at]
            turned = values[:, at].T
            vta[2 * i, :64] = turned[:64]
            vta[2 * i + 1, :64] = turned[64:]
        for c in keeps(block, step):
            c.start()

        def one_pair(i, carry):
            pair = kn[block, i]
            scores = [
                mm(pair * low + hot_high, qta[2 * i]),
                mm(pair * high + hot_low, qta[2 * i + 1]),
            ]
            for j in range(2):
                h = 2 * i + j
                before = top[h]
                now = jnp.maximum(before, jnp.max(scores[j], axis=0, keepdims=True))
                raised = jnp.exp(scores[j] - now).astype(BF)
                top[h] = now
                acc[h] = acc[h] * jnp.exp(before - now) + mm(vta[h], raised)
            return carry

        lax.fori_loop(0, PAIRS, one_pair, 0)
        return carry

    lax.fori_loop(0, seq, one_step, 0)

    lse_o[...] = jnp.zeros_like(lse_o)
    for h in range(HEADS):
        total = acc[h, 64:65]
        lse_o[h : h + 1] = top[h] + jnp.log(total)
        att_f[64 * h : 64 * (h + 1)] = acc[h, :64] / total
    att_o[...] = att_f[...].T.astype(BF)

    for way in range(2):
        for hop in range(3):
            @pl.when(can_send(way) & holds(way, hop))
            def _():
                copy(way, hop, block_of(way, hop)).wait_send()

    keep_w.wait()
    keep_q.wait()
    keep_qt.wait()
    for step in range(4):
        for c in keeps(block_at(step), step):
            c.wait()


def gather_attend(tokens, lens, gain, shift, w, bq, bv, seq):
    rows, width = tokens.shape
    any_spec = pl.BlockSpec(memory_space=pl.ANY)
    vmem = pl.BlockSpec(memory_space=pltpu.VMEM)
    sds = jax.ShapeDtypeStruct
    outs = [
        sds((seq, PAIRS, rows, 128), BF),
        sds((seq, PAIRS, rows, 128), BF),
        sds((seq, PAIRS, 128, rows), BF),
        sds((seq, width, rows), BF),
        sds((PAIRS, rows, 128), BF),
        sds((PAIRS, 128, rows), BF),
        sds((3, width, width), BF),
        sds((width, rows), F32),
        sds((rows, width), BF),
        sds((16, rows), F32),
    ]
    return pl.pallas_call(
        gather_kernel,
        out_shape=outs,
        in_specs=[vmem, pl.BlockSpec(memory_space=pltpu.SMEM)] + [vmem] * 5,
        out_specs=[any_spec] * 7 + [vmem] * 3,
        scratch_shapes=[
            pltpu.VMEM((seq, rows, width), BF),
            pltpu.VMEM((3, width, width), BF),
            pltpu.VMEM((seq, PAIRS, rows, 128), BF),
            pltpu.VMEM((seq, PAIRS, rows, 128), BF),
            pltpu.VMEM((seq, PAIRS, 128, rows), BF),
            pltpu.VMEM((seq, width, rows), BF),
            pltpu.VMEM((PAIRS, rows, 128), BF),
            pltpu.VMEM((PAIRS, 128, rows), BF),
            pltpu.VMEM((HEADS, 128, rows), BF),
            pltpu.VMEM((HEADS, 80, rows), BF),
            pltpu.VMEM((HEADS, 80, rows), F32),
            pltpu.VMEM((HEADS, 1, rows), F32),
            pltpu.SemaphoreType.DMA((2, 4)),
            pltpu.SemaphoreType.DMA((2, 4)),
            pltpu.SemaphoreType.DMA((20,)),
        ],
        compiler_params=pltpu.CompilerParams(
            collective_id=0, has_side_effects=True, vmem_limit_bytes=56 * MIB
        ),
        name="gather_attend",
    )(tokens, lens, gain, shift, w, bq, bv)


def three_parts(values):
    high = values.astype(BF).astype(F32)
    middle = (values - high).astype(BF).astype(F32)
    return high, middle, values - high - middle


def dp_place():
    dp = lax.axis_index("dp")
    core, x, y = dp % 2, (dp // 2) % 2, dp // 4
    return (core, x, y), (dp + 1 - 2 * core, dp + 2 - 4 * x, dp + 4 - 8 * y)


class DpSum:
    def __init__(self, first, stage, one, two, three, send, recv):
        self.first, self.stage, self.one, self.two, self.three = first, stage, one, two, three
        (self.core, self.x, self.y), (self.to_core, self.to_x, self.to_y) = dp_place()
        self.send, self.recv = send, recv

    def copy(self, phase):
        x_first = self.first == "x"
        if phase == 0:
            src, dst, to = self.stage.at[:, :, 1 - self.core], self.one, self.to_core
        elif phase == 1:
            src = self.one.at[:, 1 - self.x] if x_first else self.one.at[1 - self.y]
            dst, to = self.two, self.to_x if x_first else self.to_y
        else:
            src = self.two.at[1 - self.y] if x_first else self.two.at[1 - self.x]
            dst, to = self.three, self.to_y if x_first else self.to_x
        return pltpu.make_async_remote_copy(
            src_ref=src, dst_ref=dst, send_sem=self.send.at[phase], recv_sem=self.recv.at[phase],
            device_id={"dp": to}, device_id_type=MESH,
        )

    def start(self, phase):
        self.copy(phase).start()

    def finish(self, phase):
        self.copy(phase).wait_recv()
        x_first = self.first == "x"
        if phase == 0:
            for y in range(2):
                for x in range(2):
                    self.one[y, x] = self.one[y, x] + self.stage[y, x, self.core]
        elif phase == 1:
            for other in range(2):
                kept = self.one[other, self.x] if x_first else self.one[self.y, other]
                self.two[other] = self.two[other] + kept
        else:
            kept = self.two[self.y] if x_first else self.two[self.x]
            self.three[...] = self.three[...] + kept

    def wait_sends(self, phases):
        for phase in phases:
            self.copy(phase).wait_send()


class SeqSum:
    def __init__(self, part, from_end, swapped, total, send, recv):
        self.part, self.from_end, self.swapped, self.total = part, from_end, swapped, total
        self.send, self.recv = send, recv
        me = lax.axis_index("seq")
        self.end = (me == 0) | (me == 3)
        self.partner = jnp.where(me < 2, 1 - me, 5 - me)
        self.other = 3 - me

    def copy(self, phase):
        src, dst, to = (
            (self.part, self.from_end, self.partner),
            (self.part, self.swapped, self.other),
            (self.total, self.total, self.partner),
        )[phase]
        return pltpu.make_async_remote_copy(
            src_ref=src, dst_ref=dst, send_sem=self.send.at[phase], recv_sem=self.recv.at[phase],
            device_id={"seq": to}, device_id_type=MESH,
        )

    def ends_send(self):
        @pl.when(self.end)
        def _():
            self.copy(0).start()

    def middles_swap(self):
        @pl.when(~self.end)
        def _():
            self.copy(0).wait_recv()
            self.part[...] = self.part[...] + self.from_end[...]
            self.copy(1).start()

    def middles_send(self):
        @pl.when(~self.end)
        def _():
            self.copy(1).wait_recv()
            self.total[...] = self.part[...] + self.swapped[...]
            self.copy(2).start()

    def finish(self):
        @pl.when(self.end)
        def _():
            self.copy(0).wait_send()
            self.copy(2).wait_recv()

        @pl.when(~self.end)
        def _():
            self.copy(1).wait_send()
            self.copy(2).wait_send()


CHUNKS = 3
GROUPS = 8


def chunk_columns(ff, c, d):
    return (ff // GROUPS) * d + 128 * c


def feed_forward_kernel(fast, *refs):
    (
        tok, att, att_f, cot, w_out, b_out, gain, shift, b_up, b_down, w_up_h, w_down_h,
        layer_o, d_mid_o, d_att_o, d_att_t_o, delta_o, vec_o, vec_up_o, gd_o, gu_o, go_o, *refs,
    ) = refs
    if fast:
        d3_o, u3_o, *refs = refs
    wu, wd, stage_d, stage_u, stage_o, *refs = refs
    if fast:
        one_d, one_u, one_o, two_d, two_u, three_d, three_u, send, recv, *refs = refs
    in_sem, out_sem = refs
    rows, width = tok.shape
    ff = w_up_h.shape[1]
    span = GROUPS * 128

    def loads(c):
        found = []
        for d in range(GROUPS):
            at = pl.ds(chunk_columns(ff, c, d), 128)
            to = pl.ds(128 * d, 128)
            found.append(pltpu.make_async_copy(w_up_h.at[:, at], wu.at[c, :, to], in_sem.at[0, c, d]))
            found.append(pltpu.make_async_copy(w_down_h.at[at], wd.at[c, to], in_sem.at[1, c, d]))
        return found

    for c in range(CHUNKS):
        for copy in loads(c):
            copy.start()
    if fast:
        barrier = pltpu.get_barrier_semaphore()
        for to in dp_place()[1]:
            pl.semaphore_signal(barrier, inc=1, device_id={"dp": to}, device_id_type=MESH)
        pl.semaphore_wait(barrier, 3)
        sums_d = [
            DpSum("x", stage_d.at[c], one_d.at[c], two_d, three_d, send.at[c], recv.at[c]) for c in range(CHUNKS)
        ]
        sums_u = [
            DpSum("y", stage_u.at[c], one_u.at[c], two_u, three_u, send.at[3 + c], recv.at[3 + c]) for c in range(CHUNKS)
        ]
        sum_o = DpSum("x", stage_o, one_o, None, None, send.at[6], recv.at[6])

    def per_row(ref):
        return ref[...].reshape(1, -1)

    middle = tok[...].astype(F32) + mm(att[...], w_out[...]) + per_row(b_out)
    average = jnp.mean(middle, axis=-1, keepdims=True)
    centred = middle - average
    scale = lax.rsqrt(jnp.mean(centred * centred, axis=-1, keepdims=True) + EPS)
    unit = centred * scale
    normed = (unit * per_row(gain) + per_row(shift)).astype(BF)
    normed_t = normed.T
    d_out = cot[...]
    up_bias = b_up[...].reshape(1, -1)
    total = middle + per_row(b_down)
    d_normed = jnp.zeros((rows, width), F32)
    vec_up_o[...] = jnp.zeros_like(vec_up_o)
    vec_o[...] = jnp.zeros_like(vec_o)

    for c in range(CHUNKS):
        for copy in loads(c):
            copy.wait()
        bias = jnp.concatenate(
            [up_bias[:, chunk_columns(ff, c, d) : chunk_columns(ff, c, d) + 128] for d in range(GROUPS)], axis=1
        )
        upper = mm(normed, wu[c]) + bias
        cdf = 0.5 * (1.0 + lax.erf(upper * ROOT_HALF))
        hidden = (upper * cdf).astype(BF)
        slope = cdf + upper * (jnp.exp(-0.5 * upper * upper) * 0.3989422804014327)
        d_upper_f = mm_nt(d_out, wd[c]) * slope
        d_upper = d_upper_f.astype(BF)
        vec_up_o[c : c + 1] = jnp.sum(d_upper.astype(F32), axis=0, keepdims=True)
        if fast and c == 1:
            for unit_sum in (sums_d[0], sums_u[0]):
                unit_sum.finish(0)
                unit_sum.start(1)
        if fast and c == 2:
            for unit_sum in (sums_d[0], sums_u[0]):
                unit_sum.finish(1)
                unit_sum.start(2)
            for unit_sum in (sums_d[1], sums_u[1]):
                unit_sum.finish(0)
        total = total + mm(hidden, wd[c])
        d_normed = d_normed + mm_nt(d_upper, wu[c])
        g_down = mm(hidden.T, d_out).astype(BF)
        g_up = mm(normed_t, d_upper).astype(BF)
        for d in range(GROUPS):
            y, x, core = d // 4, (d // 2) % 2, d % 2
            stage_d[c, y, x, core] = g_down[128 * d : 128 * (d + 1)]
            stage_u[c, y, x, core] = g_up[96 * d : 96 * (d + 1)]
        if fast:
            sums_d[c].start(0)
            sums_u[c].start(0)
    layer_o[...] = total.astype(BF)
    vec_o[3:4] = jnp.sum(d_out.astype(F32), axis=0, keepdims=True)
    vec_o[1:2] = jnp.sum(d_normed * unit, axis=0, keepdims=True)
    vec_o[2:3] = jnp.sum(d_normed, axis=0, keepdims=True)
    scaled = d_normed * per_row(gain)
    d_middle = d_out.astype(F32) + scale * (
        scaled
        - jnp.mean(scaled, axis=-1, keepdims=True)
        - unit * jnp.mean(scaled * unit, axis=-1, keepdims=True)
    )
    d_mid_o[...] = d_middle
    d_branch = d_middle.astype(BF)
    vec_o[0:1] = jnp.sum(d_branch.astype(F32), axis=0, keepdims=True)
    g_out = mm(att_f[...].astype(BF), d_branch).astype(BF)
    for d in range(GROUPS):
        stage_o[d // 4, (d // 2) % 2, d % 2] = g_out[96 * d : 96 * (d + 1)]
    if fast:
        sum_o.start(0)
        for unit_sum in (sums_d[2], sums_u[2]):
            unit_sum.finish(0)
    d_att = mm_nt(d_branch, w_out[...]).astype(BF)
    d_att_o[...] = d_att
    d_att_t = d_att.T
    d_att_t_o[...] = d_att_t
    product = d_att_t.astype(F32) * att_f[...]
    delta_o[...] = jnp.zeros_like(delta_o)
    for h in range(HEADS):
        delta_o[h : h + 1] = jnp.sum(product[64 * h : 64 * (h + 1)], axis=0, keepdims=True)
    if fast:
        keep = [
            pltpu.make_async_copy(one_d.at[pl.ds(1, 2)], gd_o, out_sem.at[0]),
            pltpu.make_async_copy(one_u.at[pl.ds(1, 2)], gu_o, out_sem.at[1]),
        ]
        for copy in keep:
            copy.start()
        sum_o.finish(0)
        keep.append(pltpu.make_async_copy(one_o, go_o, out_sem.at[2]))
        keep[-1].start()
        for unit_sum in (sums_d[0], sums_u[0]):
            unit_sum.finish(2)
        keep.append(pltpu.make_async_copy(three_d, d3_o, out_sem.at[3]))
        keep.append(pltpu.make_async_copy(three_u, u3_o, out_sem.at[4]))
        for copy in keep[3:]:
            copy.start()
        for c in range(CHUNKS):
            phases = (0, 1, 2) if c == 0 else (0,)
            sums_d[c].wait_sends(phases)
            sums_u[c].wait_sends(phases)
        sum_o.wait_sends((0,))
    else:
        keep = [
            pltpu.make_async_copy(stage_d, gd_o, out_sem.at[0]),
            pltpu.make_async_copy(stage_u, gu_o, out_sem.at[1]),
            pltpu.make_async_copy(stage_o, go_o, out_sem.at[2]),
        ]
        for copy in keep:
            copy.start()
    for copy in keep:
        copy.wait()


def feed_forward(fast, tokens, att, att_f, cot, w_out, b_out, gain, shift, b_up, b_down, w_up, w_down):
    rows, width = tokens.shape
    ff = w_up.shape[1]
    span = GROUPS * 128
    part_w, part_o = width // GROUPS, width // GROUPS
    any_spec = pl.BlockSpec(memory_space=pl.ANY)
    vmem = pl.BlockSpec(memory_space=pltpu.VMEM)
    sds = jax.ShapeDtypeStruct
    cube = (2, 2, 2)
    outs = [
        sds((rows, width), BF), sds((rows, width), F32), sds((rows, width), BF), sds((width, rows), BF),
        sds((16, rows), F32), sds((8, width), F32), sds((8, span), F32),
    ]
    out_specs = [vmem] * 7
    scratch = [
        pltpu.VMEM((CHUNKS, width, span), BF),
        pltpu.VMEM((CHUNKS, span, width), BF),
        pltpu.VMEM((CHUNKS, *cube, 128, width), BF),
        pltpu.VMEM((CHUNKS, *cube, part_w, span), BF),
        pltpu.VMEM((*cube, part_o, width), BF),
    ]
    if fast:
        outs += [
            sds((2, 2, 2, 128, width), BF), sds((2, 2, 2, part_w, span), BF), sds((2, 2, part_o, width), BF),
            sds((128, width), BF), sds((part_w, span), BF),
        ]
        scratch += [
            pltpu.VMEM((CHUNKS, 2, 2, 128, width), BF),
            pltpu.VMEM((CHUNKS, 2, 2, part_w, span), BF),
            pltpu.VMEM((2, 2, part_o, width), BF),
            pltpu.VMEM((2, 128, width), BF),
            pltpu.VMEM((2, part_w, span), BF),
            pltpu.VMEM((128, width), BF),
            pltpu.VMEM((part_w, span), BF),
            pltpu.SemaphoreType.DMA((7, 3)),
            pltpu.SemaphoreType.DMA((7, 3)),
        ]
    else:
        outs += [
            sds((CHUNKS, *cube, 128, width), BF), sds((CHUNKS, *cube, part_w, span), BF), sds((*cube, part_o, width), BF),
        ]
    out_specs += [any_spec] * (len(outs) - 7)
    scratch += [pltpu.SemaphoreType.DMA((2, CHUNKS, GROUPS)), pltpu.SemaphoreType.DMA((5,))]
    params = dict(vmem_limit_bytes=58 * MIB)
    if fast:
        params.update(collective_id=1, has_side_effects=True)
    return pl.pallas_call(
        partial(feed_forward_kernel, fast),
        out_shape=outs,
        in_specs=[vmem] * 10 + [any_spec] * 2,
        out_specs=out_specs,
        scratch_shapes=scratch,
        compiler_params=pltpu.CompilerParams(**params),
        name="feed_forward",
    )(tokens, att, att_f, cot, w_out, b_out, gain, shift, b_up, b_down, w_up, w_down)


def attend_back_kernel(fast, *refs):
    (
        kn_h, vn_h, kt_h, xt_h, qn, qt_h, d_att, d_att_t_h, delta, lse, wp_h, lens, tok_h, d_mid_h, gain, vec, vec_up,
        *refs,
    ) = refs
    if fast:
        one_d_h, one_u_h, one_o_h, d3_h, u3_h, *refs = refs
    tok_o, *refs = refs
    if fast:
        fin_d_o, fin_u_o, fin_o_o, fin_q_o, fin_v_o, *refs = refs
    else:
        gw_o, stage_v_o, *refs = refs
    (
        kn, vn, kt, xt, qta, dta, dqt, gk, gv, dk, dv, wp, tok, d_mid, dx_own, dxs, rx, stage_q, stage_v, sums,
        in_sem, load_sem, out_sem, dsend, drecv, *refs,
    ) = refs
    rows, width = d_att.shape
    seq = lax.axis_size("seq")
    me = lax.axis_index("seq")
    has_left, has_right = me > 0, me < seq - 1
    at_end = (me == 0) | (me == seq - 1)
    part_w = width // GROUPS

    barrier = pltpu.get_barrier_semaphore()

    @pl.when(has_left)
    def _():
        pl.semaphore_signal(barrier, inc=1, device_id={"seq": me - 1}, device_id_type=MESH)

    @pl.when(has_right)
    def _():
        pl.semaphore_signal(barrier, inc=1, device_id={"seq": me + 1}, device_id_type=MESH)

    if fast:
        for to in dp_place()[1]:
            pl.semaphore_signal(barrier, inc=1, device_id={"dp": to}, device_id_type=MESH)
    greeted = 3 if fast else 0

    def block_at(step):
        b0 = jnp.where(me < 2, seq - 1, 0)
        b1 = jnp.where(me < 2, seq - 2, 1)
        b2 = jnp.where(me == 0, 1, jnp.where(me == 1, 0, jnp.where(me == 2, 3, 2)))
        return jnp.where(step == 0, b0, jnp.where(step == 1, b1, jnp.where(step == 2, b2, me)))

    def loads(step):
        block, slot = block_at(step), step % 2
        return [
            pltpu.make_async_copy(kn_h.at[block], kn.at[slot], in_sem.at[slot, 0]),
            pltpu.make_async_copy(vn_h.at[block], vn.at[slot], in_sem.at[slot, 1]),
            pltpu.make_async_copy(kt_h.at[block], kt.at[slot], in_sem.at[slot, 2]),
            pltpu.make_async_copy(xt_h.at[block], xt.at[slot], in_sem.at[slot, 3]),
        ]

    def halves(j):
        return (slice(0, 64), slice(64, 128)) if j == 0 else (slice(64, 128), slice(0, 64))

    fills = []
    for h in range(HEADS):
        own = pl.ds(64 * (h % 2), 64)
        fills.append(pltpu.make_async_copy(qt_h.at[h // 2, own], qta.at[h, own], load_sem.at[h]))
        fills.append(pltpu.make_async_copy(d_att_t_h.at[pl.ds(64 * h, 64)], dta.at[h, own], load_sem.at[HEADS + h]))
    for copy in fills:
        copy.start()
    for copy in loads(0):
        copy.start()
    late = [
        pltpu.make_async_copy(wp_h, wp, load_sem.at[24]),
        pltpu.make_async_copy(tok_h, tok, load_sem.at[25]),
        pltpu.make_async_copy(d_mid_h, d_mid, load_sem.at[26]),
    ]
    for copy in late:
        copy.start()
    if fast:
        (
            one_d, one_u, one_o, two_d, two_u, two_o, three_d, three_u, three_o,
            one_q, two_q, three_q, one_v, two_v, three_v,
            za_d, zx_d, fin_d, za_u, zx_u, fin_u, za_o, zx_o, fin_o, za_q, zx_q, fin_q, za_v, zx_v, fin_v,
            psend, precv, zsend, zrecv,
        ) = refs
        early = [
            pltpu.make_async_copy(d3_h, three_d.at[0], load_sem.at[27]),
            pltpu.make_async_copy(u3_h, three_u.at[0], load_sem.at[28]),
            pltpu.make_async_copy(one_d_h.at[0], one_d.at[0], load_sem.at[29]),
            pltpu.make_async_copy(one_u_h.at[0], one_u.at[0], load_sem.at[30]),
            pltpu.make_async_copy(one_d_h.at[1], one_d.at[1], load_sem.at[31]),
            pltpu.make_async_copy(one_u_h.at[1], one_u.at[1], load_sem.at[32]),
            pltpu.make_async_copy(one_o_h, one_o, load_sem.at[33]),
        ]
        for copy in early:
            copy.start()
        rs_d = [DpSum("x", None, one_d.at[c], two_d.at[c], three_d.at[c + 1], psend.at[c], precv.at[c]) for c in range(2)]
        rs_u = [
            DpSum("y", None, one_u.at[c], two_u.at[c], three_u.at[c + 1], psend.at[2 + c], precv.at[2 + c])
            for c in range(2)
        ]
        rs_o = DpSum("x", None, one_o, two_o, three_o, psend.at[4], precv.at[4])
        rs_q = [
            DpSum("xy"[c], stage_q.at[c], one_q.at[c], two_q.at[c], three_q.at[c], psend.at[5 + c], precv.at[5 + c])
            for c in range(2)
        ]
        rs_v = DpSum("x", stage_v, one_v, two_v, three_v, psend.at[7], precv.at[7])
        ar_d = [
            SeqSum(three_d.at[c], za_d.at[c], zx_d.at[c], fin_d.at[c], zsend.at[c], zrecv.at[c]) for c in range(3)
        ]
        ar_u = [
            SeqSum(three_u.at[c], za_u.at[c], zx_u.at[c], fin_u.at[c], zsend.at[3 + c], zrecv.at[3 + c]) for c in range(3)
        ]
        ar_o = SeqSum(three_o, za_o, zx_o, fin_o, zsend.at[6], zrecv.at[6])
        ar_q = [
            SeqSum(three_q.at[c], za_q.at[c], zx_q.at[c], fin_q.at[c], zsend.at[7 + c], zrecv.at[7 + c]) for c in range(2)
        ]
        ar_v = SeqSum(three_v, za_v, zx_v, fin_v, zsend.at[9], zrecv.at[9])

    low, high = lane_halves()
    codes = query_codes(lens, me, rows)
    row64 = lax.broadcasted_iota(jnp.int32, (64, rows), 0)
    for h in range(HEADS):
        _, other = halves(h % 2)
        extra = codes
        for r, part in enumerate(three_parts(-lse[h : h + 1])):
            extra = jnp.where(row64 == 8 + r, part, extra)
        qta[h, other] = extra.astype(BF)
        extra = jnp.zeros((64, rows), F32)
        for r, part in enumerate(three_parts(-delta[h : h + 1])):
            extra = jnp.where(row64 == r, part, extra)
        dta[h, other] = extra.astype(BF)
    dqt[...] = jnp.zeros_like(dqt)
    gk[...] = jnp.zeros_like(gk)
    gv[...] = jnp.zeros_like(gv)
    stage_v[...] = jnp.zeros_like(stage_v)
    sums[...] = jnp.zeros_like(sums)
    lane = lax.broadcasted_iota(jnp.int32, (1, 128), 1)
    v_low = jnp.where(lane < 3, 1.0, 0.0).astype(BF)
    v_high = jnp.where((lane >= 64) & (lane < 67), 1.0, 0.0).astype(BF)
    for copy in fills:
        copy.wait()

    @pl.when(at_end)
    def _():
        pl.semaphore_wait(barrier, greeted + 1)

    @pl.when(~at_end)
    def _():
        pl.semaphore_wait(barrier, greeted + 2)

    def dx_copy(way, block):
        return pltpu.make_async_remote_copy(
            src_ref=dxs.at[block], dst_ref=rx.at[block + way],
            send_sem=dsend.at[way, block], recv_sem=drecv.at[way, block],
            device_id={"seq": me - 1 if way == 0 else me + 1}, device_id_type=MESH,
        )

    def relay(way, block):
        dx_copy(way, block).wait_recv()
        dxs[block] = dxs[block] + rx[block + way]
        dx_copy(way, block).start()

    def relay_at(place, way, step):
        @pl.when(me == place)
        def _():
            relay(way, block_at(step))

    def hooks(g):
        if not fast:
            return

        def at(when, action):
            @pl.when(g == when)
            def _():
                action()

        def chunk0_out():
            for copy in early[:4]:
                copy.wait()
            ar_d[0].ends_send()
            ar_u[0].ends_send()
            rs_d[0].start(1)
            rs_u[0].start(1)

        def chunk2_out():
            for copy in early[4:]:
                copy.wait()
            rs_d[1].start(1)
            rs_u[1].start(1)

        def turn(*sums):
            for unit_sum in sums:
                unit_sum.finish(1)
                unit_sum.start(2)

        def close(*sums):
            for unit_sum in sums:
                unit_sum.finish(2)

        at(0, chunk0_out)
        at(2, chunk2_out)
        at(4, lambda: (ar_d[0].middles_swap(), ar_u[0].middles_swap()))
        at(5, lambda: turn(rs_d[0], rs_u[0]))
        at(7, lambda: rs_o.start(1))
        at(8, lambda: (ar_d[0].middles_send(), ar_u[0].middles_send()))
        at(9, lambda: close(rs_d[0], rs_u[0]))
        at(11, lambda: turn(rs_d[1], rs_u[1]))
        at(14, lambda: close(rs_d[1], rs_u[1]))
        at(15, lambda: (relay_at(1, 1, 0), relay_at(2, 0, 0)))
        at(16, lambda: turn(rs_o))
        at(19, lambda: close(rs_o))

    def one_step(step, carry):
        slot = step % 2
        for copy in loads(step):
            copy.wait()

        @pl.when(step < seq - 1)
        def _():
            for copy in loads(step + 1):
                copy.start()

        block = block_at(step)
        hot = key_codes(lens, block, rows)
        hot_low, hot_high = hot * low, hot * high

        def one_pair(i, carry):
            hooks(step * PAIRS + i)
            at = pl.ds(pl.multiple_of(i * 128, 128), 128)
            keys, values = kn[slot, i], vn[slot, i]
            q_pair, d_pair = qn[i], d_att[:, at]
            scores = [
                mm(keys * low + hot_high, qta[2 * i]),
                mm(keys * high + hot_low, qta[2 * i + 1]),
            ]
            slopes = [
                mm(values * low + v_high, dta[2 * i]),
                mm(values * high + v_low, dta[2 * i + 1]),
            ]
            d_keys = jnp.zeros((rows, 128), F32)
            d_values = jnp.zeros((rows, 128), F32)
            for j in range(2):
                h = 2 * i + j
                half = low if j == 0 else high
                probs = jnp.exp(scores[j])
                d_scores = (probs * slopes[j]).astype(BF)
                d_values = d_values + mm(probs.astype(BF), d_pair * half)
                d_keys = d_keys + mm(d_scores, q_pair * half)
                dqt[h] += mm(kt[slot, i, 64 * j : 64 * (j + 1)], d_scores)
            dk[:, at] = d_keys.astype(BF)
            dv[:, at] = d_values.astype(BF)
            return carry

        lax.fori_loop(0, PAIRS, one_pair, 0)

        @pl.when(step == 0)
        def _():
            late[0].wait()

        dx = mm_nt(dk[...], wp[1]) + mm_nt(dv[...], wp[2])

        @pl.when(step < seq - 1)
        def _():
            dxs[block] = dx.astype(BF)

            @pl.when(me == 0)
            def _():
                dx_copy(1, block).start()

            @pl.when(me == seq - 1)
            def _():
                dx_copy(0, block).start()

        @pl.when(step == seq - 1)
        def _():
            dx_own[...] = dx

        gk[...] += mm(xt[slot], dk[...])
        gv[...] += mm(xt[slot], dv[...])
        sums[3:4] += jnp.sum(dv[...].astype(F32), axis=0, keepdims=True)
        return carry

    lax.fori_loop(0, seq, one_step, 0)
    last = (seq - 1) % 2
    dq = ((dqt[...] * (HEAD**-0.5)).reshape(width, rows).T).astype(BF)
    dx_own[...] += mm_nt(dq, wp[0])
    sums[2:3] = jnp.sum(dq.astype(F32), axis=0, keepdims=True)
    gq = mm(xt[last], dq)
    lane_w = lax.broadcasted_iota(jnp.int32, (width, 128), 1)
    lo = lane_w < 64
    for i in range(PAIRS):
        at = slice(128 * i, 128 * (i + 1))
        k_turned = pltpu.roll(gk[:, at], 64, 1)
        tiles = (
            jnp.where(lo, gq[:, at], k_turned), jnp.where(lo, gv[:, at], gq[:, at]), jnp.where(lo, k_turned, gv[:, at])
        )
        for j, tile in enumerate(tiles):
            tile = tile.astype(BF)
            place = 3 * i + j
            if not fast:
                gw_o[:, 128 * place : 128 * (place + 1)] = tile
                continue
            to = slice(128 * (place % 9), 128 * (place % 9 + 1))
            for d in range(GROUPS):
                stage_q[place // 9, d // 4, (d // 2) % 2, d % 2, :, to] = tile[part_w * d : part_w * (d + 1)]
        if fast and i == 2:
            rs_q[0].start(0)
    if fast:
        rs_q[1].start(0)
        for unit in (ar_d[1], ar_u[1], ar_d[2], ar_u[2], ar_o):
            unit.ends_send()
    relay_at(1, 1, 1)
    relay_at(2, 0, 1)
    relay_at(1, 0, 2)
    relay_at(2, 1, 2)
    if fast:
        for unit in rs_q:
            unit.finish(0)
            unit.start(1)

    late[1].wait()
    late[2].wait()
    for way, there in ((0, has_right), (1, has_left)):
        @pl.when(there)
        def _():
            dx_copy(way, me).wait_recv()
            dx_own[...] += rx[me + way].astype(F32)

    values = tok[...].astype(F32)
    centred = values - jnp.mean(values, axis=-1, keepdims=True)
    scale = lax.rsqrt(jnp.mean(centred * centred, axis=-1, keepdims=True) + EPS)
    unit_rows = centred * scale
    d_normed = dx_own[...]
    sums[0:1] = jnp.sum(d_normed * unit_rows, axis=0, keepdims=True)
    sums[1:2] = jnp.sum(d_normed, axis=0, keepdims=True)
    sums[4:8] = vec[0:4]
    scaled = d_normed * gain[...].reshape(1, -1)
    tok_o[...] = (
        d_mid[...]
        + scale
        * (
            scaled
            - jnp.mean(scaled, axis=-1, keepdims=True)
            - unit_rows * jnp.mean(scaled * unit_rows, axis=-1, keepdims=True)
        )
    ).astype(BF)
    rows8 = sums[...]
    for d in range(GROUPS):
        y, x, core = d // 4, (d // 2) % 2, d % 2
        stage_v[y, x, core, 0:8, 0:part_w] = rows8[:, part_w * d : part_w * (d + 1)]
        stage_v[y, x, core, 8 : 8 + CHUNKS] = vec_up[0:CHUNKS, 128 * d : 128 * (d + 1)]
    if fast:
        rs_v.start(0)
        for unit in (ar_d[1], ar_u[1], ar_d[2], ar_u[2], ar_o):
            unit.middles_swap()
        rs_v.finish(0)
        rs_v.start(1)
        for unit in rs_q:
            unit.finish(1)
            unit.start(2)
        rs_v.finish(1)
        rs_v.start(2)
        for unit in (ar_d[1], ar_u[1], ar_d[2], ar_u[2], ar_o):
            unit.middles_send()
        rs_v.finish(2)
        ar_v.ends_send()
        for unit in rs_q:
            unit.finish(2)
        for unit in ar_q:
            unit.ends_send()
        ar_v.middles_swap()
        for unit in ar_q:
            unit.middles_swap()
        ar_v.middles_send()
        for unit in ar_q:
            unit.middles_send()
        for unit in (*ar_d, *ar_u, ar_o, ar_v, *ar_q):
            unit.finish()
        keep = [
            pltpu.make_async_copy(src, dst, out_sem.at[k])
            for k, (src, dst) in enumerate(
                ((fin_d, fin_d_o), (fin_u, fin_u_o), (fin_o, fin_o_o), (fin_q, fin_q_o), (fin_v, fin_v_o))
            )
        ]
        for copy in keep:
            copy.start()
        for unit in (*rs_d, *rs_u, rs_o):
            unit.wait_sends((1, 2))
        for unit in (*rs_q, rs_v):
            unit.wait_sends((0, 1, 2))
        for copy in keep:
            copy.wait()
    else:
        stage_v_o[...] = stage_v[...]

    for place, first, second in ((0, 1, 1), (1, 1, 0), (2, 0, 1), (3, 0, 0)):
        @pl.when(me == place)
        def _():
            for step, way in enumerate((first, first, second)):
                dx_copy(way, block_at(step)).wait_send()


def attend_back(fast, kn, vn, kt, xt, qn, qt, d_att, d_att_t, delta, lse, wp, lens, tokens, d_mid, gain, vec, vec_up, *ready):
    seq, _, rows, _ = kn.shape
    width = wp.shape[1]
    span = GROUPS * 128
    part = width // GROUPS
    half = 3 * width // 2
    any_spec = pl.BlockSpec(memory_space=pl.ANY)
    vmem = pl.BlockSpec(memory_space=pltpu.VMEM)
    sds = jax.ShapeDtypeStruct
    cube = (2, 2, 2)
    outs = [sds((rows, width), BF)]
    out_specs = [vmem]
    if fast:
        outs += [
            sds((CHUNKS, 128, width), BF), sds((CHUNKS, part, span), BF), sds((part, width), BF),
            sds((2, part, half), BF), sds((16, 128), F32),
        ]
        out_specs += [any_spec] * 5
    else:
        outs += [sds((width, 3 * width), BF), sds((*cube, 16, 128), F32)]
        out_specs += [vmem] * 2
    scratch = [
        pltpu.VMEM((2, PAIRS, rows, 128), BF),
        pltpu.VMEM((2, PAIRS, rows, 128), BF),
        pltpu.VMEM((2, PAIRS, 128, rows), BF),
        pltpu.VMEM((2, width, rows), BF),
        pltpu.VMEM((HEADS, 128, rows), BF),
        pltpu.VMEM((HEADS, 128, rows), BF),
        pltpu.VMEM((HEADS, HEAD, rows), F32),
        pltpu.VMEM((width, width), F32),
        pltpu.VMEM((width, width), F32),
        pltpu.VMEM((rows, width), BF),
        pltpu.VMEM((rows, width), BF),
        pltpu.VMEM((3, width, width), BF),
        pltpu.VMEM((rows, width), BF),
        pltpu.VMEM((rows, width), F32),
        pltpu.VMEM((rows, width), F32),
        pltpu.VMEM((seq, rows, width), BF),
        pltpu.VMEM((seq + 1, rows, width), BF),
        pltpu.VMEM((2, *cube, part, half) if fast else (8, 128), BF),
        pltpu.VMEM((*cube, 16, 128), F32),
        pltpu.VMEM((8, width), F32),
        pltpu.SemaphoreType.DMA((2, 4)),
        pltpu.SemaphoreType.DMA((34,)),
        pltpu.SemaphoreType.DMA((5,)),
        pltpu.SemaphoreType.DMA((2, 4)),
        pltpu.SemaphoreType.DMA((2, 4)),
    ]
    if fast:
        d, u, o, q = (128, width), (part, span), (part, width), (part, half)
        scratch += [
            pltpu.VMEM(shape, BF)
            for shape in (
                (2, 2, 2, *d), (2, 2, 2, *u), (2, 2, *o), (2, 2, *d), (2, 2, *u), (2, *o), (3, *d), (3, *u), o,
                (2, 2, 2, *q), (2, 2, *q), (2, *q),
            )
        ]
        scratch += [pltpu.VMEM((2, 2, 16, 128), F32), pltpu.VMEM((2, 16, 128), F32), pltpu.VMEM((16, 128), F32)]
        for shape in ((3, *d), (3, *u), o, (2, *q)):
            scratch += [pltpu.VMEM(shape, BF)] * 3
        scratch += [pltpu.VMEM((16, 128), F32)] * 3
        scratch += [pltpu.SemaphoreType.DMA(shape) for shape in ((8, 3), (8, 3), (10, 3), (10, 3))]
    return pl.pallas_call(
        partial(attend_back_kernel, fast),
        out_shape=outs,
        in_specs=[any_spec] * 4
        + [vmem, any_spec, vmem, any_spec, vmem, vmem, any_spec, pl.BlockSpec(memory_space=pltpu.SMEM)]
        + [any_spec] * 2
        + [vmem] * 3
        + [any_spec] * len(ready),
        out_specs=out_specs,
        scratch_shapes=scratch,
        compiler_params=pltpu.CompilerParams(
            collective_id=2, has_side_effects=True, vmem_limit_bytes=62 * MIB
        ),
        name="attend_back",
    )(kn, vn, kt, xt, qn, qt, d_att, d_att_t, delta, lse, wp, lens, tokens, d_mid, gain, vec, vec_up, *ready)


def unpack_kernel(fin_d, fin_u, fin_o, fin_q, fin_v, down_o, up_o, out_o, qkv_o, *vec_o):
    chunks, _, _ = fin_d.shape
    part, span = fin_u.shape[1:]
    half = fin_q.shape[2]
    for c in range(chunks):
        down_o[128 * c : 128 * (c + 1)] = fin_d[c].astype(F32)
        for d in range(GROUPS):
            at = chunk_columns(up_o.shape[1], c, d)
            up_o[:, at : at + 128] = fin_u[c, :, 128 * d : 128 * (d + 1)].astype(F32)
    out_o[...] = fin_o[...].astype(F32)
    for c in range(2):
        qkv_o[:, half * c : half * (c + 1)] = fin_q[c].astype(F32)
    for r in range(8):
        vec_o[r][...] = fin_v[r : r + 1, :part].reshape(part)
    vec_o[8][...] = jnp.concatenate([fin_v[8 + c : 9 + c] for c in range(chunks)], axis=1).reshape(128 * chunks)


def unpack(fin_d, fin_u, fin_o, fin_q, fin_v):
    vmem = pl.BlockSpec(memory_space=pltpu.VMEM)
    chunks, _, width = fin_d.shape
    part, span = fin_u.shape[1:]
    sds = jax.ShapeDtypeStruct
    outs = [
        sds((128 * chunks, width), F32), sds((part, span * chunks), F32), sds((part, width), F32),
        sds((part, 2 * fin_q.shape[2]), F32),
    ]
    outs += [sds((part,), F32)] * 8 + [sds((128 * chunks,), F32)]
    return pl.pallas_call(
        unpack_kernel, out_shape=outs, in_specs=[vmem] * 5, out_specs=[vmem] * len(outs), name="unpack",
    )(fin_d, fin_u, fin_o, fin_q, fin_v)


def local(
    tokens, cell_lengths, ln1_gain, ln1_shift, w_qkv, b_query, b_value, w_out, b_out,
    ln2_gain, ln2_shift, w_up, b_up, w_down, b_down, cotangent,
):
    bucket_count, local_slots, width = tokens.shape
    ff = w_up.shape[1]
    seq_count = lax.axis_size("seq")
    dp_count = lax.axis_size("dp")
    fast = dp_count == GROUPS
    rows = bucket_count * local_slots
    flat = tokens.reshape(rows, width)
    kn, vn, kt, xt, qn, qt, wp, att_t, attended, lse = gather_attend(
        flat, cell_lengths, ln1_gain, ln1_shift, w_qkv, b_query, b_value, seq_count
    )
    layer_out, d_mid, d_att, d_att_t, delta, vec, vec_up, *sums = feed_forward(
        fast, flat, attended, att_t, cotangent.reshape(rows, width), w_out, b_out, ln2_gain, ln2_shift,
        b_up, b_down, w_up, w_down,
    )
    tokens_grad, *found = attend_back(
        fast, kn, vn, kt, xt, qn, qt, d_att, d_att_t, delta, lse, wp, cell_lengths, flat, d_mid, ln1_gain,
        vec, vec_up, *(sums if fast else ()),
    )
    layer_out = layer_out.reshape(tokens.shape)
    tokens_grad = tokens_grad.reshape(tokens.shape)
    if fast:
        down, up, out, qkv, *vectors = unpack(*found)
    else:

        def summed(g):
            share = lax.psum_scatter(g, "dp", scatter_dimension=0, tiled=True)
            return lax.psum(share, "seq").astype(F32)

        g_down, g_up, g_out = sums
        g_qkv, packed = found
        g_down = jnp.moveaxis(g_down.reshape(CHUNKS, GROUPS, 128, width), 0, 1).reshape(ff, width)
        g_up = jnp.transpose(g_up.reshape(CHUNKS, width, GROUPS, 128), (1, 2, 0, 3)).reshape(width, ff)
        down, up, out, qkv = summed(g_down), summed(g_up), summed(g_out.reshape(width, width)), summed(g_qkv)
        packed = packed.reshape(GROUPS, 16, 128)
        vectors = [packed[:, r, : width // GROUPS].reshape(width) for r in range(8)]
        vectors.append(packed[:, 8 : 8 + CHUNKS].reshape(ff))
        together = jnp.concatenate([v.reshape(dp_count, -1) for v in vectors], axis=1)
        together = lax.psum(together, ("dp", "seq"))
        mine = lax.dynamic_index_in_dim(together, lax.axis_index("dp"), 0, keepdims=False)
        sizes = [v.shape[0] // dp_count for v in vectors]
        vectors = [mine[sum(sizes[:k]) : sum(sizes[: k + 1])] for k in range(len(sizes))]
    g1, s1, bq, bv, bo, g2, s2, bd, bu = vectors
    return layer_out, tokens_grad, g1, s1, qkv, bq, bv, out, bo, g2, s2, up, bu, down, bd


def solution(mesh):
    token_spec = P("dp", "seq", None)
    vector, matrix = P("dp"), P("dp", None)
    placed = (token_spec, P("dp", None)) + (P(),) * 13 + (token_spec,)
    return jax.shard_map(
        local,
        mesh=mesh,
        in_specs=placed,
        out_specs=(
            token_spec, token_spec, vector, vector, matrix, vector, vector, matrix, vector,
            vector, vector, matrix, vector, matrix, vector,
        ),
        check_vma=False,
    )
```

```python
from functools import partial

import jax
import jax.numpy as jnp
from jax import lax
from jax.experimental import pallas as pl
from jax.experimental.pallas import tpu as pltpu
from jax.sharding import PartitionSpec as P

HEADS = 12
HEAD = 64
PAIRS = 6
EPS = 1e-05
ROOT_HALF = 0.7071067811865476
BIG = 1e30
MESH = pl.DeviceIdType.MESH
F32 = jnp.float32
BF = jnp.bfloat16
MIB = 1024 * 1024


def normalize(values, gain, shift):
    average = jnp.mean(values, axis=-1, keepdims=True)
    centred = values - average
    variance = jnp.mean(centred * centred, axis=-1, keepdims=True)
    return centred * lax.rsqrt(variance + EPS) * gain + shift


def gelu_exact(values):
    return 0.5 * values * (1.0 + jax.scipy.special.erf(values * ROOT_HALF))


def mm(a, b):
    return jnp.dot(a, b, preferred_element_type=F32)


def mm_nt(a, b):
    return lax.dot_general(a, b, (((1,), (1,)), ((), ())), preferred_element_type=F32)


def cell_bounds(lens_ref, index):
    start = jnp.zeros(index.shape, jnp.int32)
    end = jnp.zeros(index.shape, jnp.int32)
    at = jnp.int32(0)
    for c in range(lens_ref.shape[1]):
        after = at + lens_ref[0, c]
        start = jnp.where(index == c, at, start)
        end = jnp.where(index == c, after, end)
        at = after
    return start, end


def key_codes(lens_ref, block, rows):
    lane = lax.broadcasted_iota(jnp.int32, (1, 128), 1) % 64
    start, end = cell_bounds(lens_ref, lane)
    ones = ((lane >= 8) & (lane < 11)).astype(F32)
    slot = lax.broadcasted_iota(jnp.int32, (rows, 128), 0) + block * rows
    hot = jnp.where((slot >= start) & (slot < end), 1.0, 0.0)
    return (hot + ones).astype(BF)


def query_codes(lens_ref, block, rows):
    cell = lax.broadcasted_iota(jnp.int32, (64, 1), 0)
    start, end = cell_bounds(lens_ref, cell)
    slot = lax.broadcasted_iota(jnp.int32, (64, rows), 1) + block * rows
    inside = (slot >= start) & (slot < end)
    return jnp.where(inside | (cell >= 8), 0.0, -BIG)


def lane_halves():
    lane = lax.broadcasted_iota(jnp.int32, (1, 128), 1)
    low = jnp.where(lane < 64, 1.0, 0.0).astype(BF)
    high = jnp.where(lane < 64, 0.0, 1.0).astype(BF)
    return low, high


def sort_weights(w_ref, wp):
    depth = w_ref.shape[0]
    lane = lax.broadcasted_iota(jnp.int32, (depth, 128), 1)
    low = lane < 64
    for i in range(PAIRS):
        t0, t1, t2 = (w_ref[:, 384 * i + 128 * j : 384 * i + 128 * (j + 1)].astype(F32) for j in range(3))
        at = slice(128 * i, 128 * (i + 1))
        wp[0, :, at] = jnp.where(low, t0, t1).astype(BF)
        wp[1, :, at] = pltpu.roll(jnp.where(low, t2, t0), 64, 1).astype(BF)
        wp[2, :, at] = jnp.where(low, t1, t2).astype(BF)


def gather_kernel(
    tok, lens, gain, shift, w_h, bq, bv,
    kn_o, vn_o, kt_o, xt_o, qn_o, qt_o, wp_o, att_f, att_o, lse_o,
    xr, w, wp, kn, vn, kt, xt, qn, qt, qta, vta, acc, top, send, recv, in_sem, out_sem,
):
    rows, width = tok.shape
    span = rows // 2
    seq = lax.axis_size("seq")
    me = lax.axis_index("seq")
    has_left, has_right = me > 0, me < seq - 1
    at_end = (me == 0) | (me == seq - 1)

    barrier = pltpu.get_barrier_semaphore()

    @pl.when(has_left)
    def _():
        pl.semaphore_signal(barrier, inc=1, device_id={"seq": me - 1}, device_id_type=MESH)

    @pl.when(has_right)
    def _():
        pl.semaphore_signal(barrier, inc=1, device_id={"seq": me + 1}, device_id_type=MESH)

    own_tokens = pltpu.make_async_copy(tok, xr.at[me], in_sem.at[0])
    own_tokens.start()
    weights = pltpu.make_async_copy(w_h, w, in_sem.at[1])
    weights.start()

    @pl.when(at_end)
    def _():
        pl.semaphore_wait(barrier, 1)

    @pl.when(~at_end)
    def _():
        pl.semaphore_wait(barrier, 2)

    def copy(way, hop, half, block):
        at = pl.ds(half * span, span)
        return pltpu.make_async_remote_copy(
            src_ref=tok.at[at] if hop == 0 else xr.at[block, at],
            dst_ref=xr.at[block, at],
            send_sem=send.at[way, hop, half],
            recv_sem=recv.at[way, hop, half],
            device_id={"seq": me - 1 if way == 0 else me + 1},
            device_id_type=MESH,
        )

    def can_send(way):
        return has_left if way == 0 else has_right

    def holds(way, hop):
        return me + hop < seq if way == 0 else me - hop >= 0

    def block_of(way, hop):
        return me + hop if way == 0 else me - hop

    for half in range(2):
        for way in range(2):
            @pl.when(can_send(way))
            def _():
                copy(way, 0, half, me).start()

    def normed(raw):
        return normalize(raw.astype(F32), gain[...].reshape(1, -1), shift[...].reshape(1, -1)).astype(BF)

    row16 = lax.broadcasted_iota(jnp.int32, (16, span), 0)
    for h in range(HEADS):
        vta[h, 64:] = jnp.where(row16 == 0, 1.0, 0.0).astype(BF)
    acc[...] = jnp.zeros_like(acc)
    top[...] = jnp.full_like(top, -3e38)
    codes = query_codes(lens, me, rows).astype(BF)
    low, high = lane_halves()
    own_tokens.wait()
    weights.wait()
    sort_weights(w, wp)
    keep_w = pltpu.make_async_copy(wp, wp_o, out_sem.at[0])
    keep_w.start()
    q = ((mm(normed(xr[me]), wp[0]) + bq[...].reshape(1, -1)).astype(BF).astype(F32) * (HEAD**-0.5)).astype(BF)
    for i in range(PAIRS):
        pair = q[:, 128 * i : 128 * (i + 1)]
        qn[i] = pair
        turned = pair.T
        qt[i] = turned
        qta[2 * i, :64] = turned[:64]
        qta[2 * i, 64:] = codes
        qta[2 * i + 1, :64] = codes
        qta[2 * i + 1, 64:] = turned[64:]
    keep_q = pltpu.make_async_copy(qn, qn_o, out_sem.at[1])
    keep_q.start()
    keep_qt = pltpu.make_async_copy(qt, qt_o, out_sem.at[2])
    keep_qt.start()

    def keeps(step):
        block = block_at(step)
        return [
            pltpu.make_async_copy(kn.at[block], kn_o.at[block], out_sem.at[3 + 4 * step]),
            pltpu.make_async_copy(vn.at[block], vn_o.at[block], out_sem.at[4 + 4 * step]),
            pltpu.make_async_copy(kt.at[block], kt_o.at[block], out_sem.at[5 + 4 * step]),
            pltpu.make_async_copy(xt.at[block], xt_o.at[block], out_sem.at[6 + 4 * step]),
        ]

    def block_at(step):
        from_end = jnp.where(me == 0, step, seq - 1 - step)
        from_mid = jnp.where(step == 0, me, jnp.where(step == 1, me + 1, jnp.where(step == 2, me - 1, jnp.where(me == 1, seq - 1, 0))))
        return jnp.where(at_end, from_end, from_mid)

    def half_step(turn, carry):
        step, half = turn // 2, turn % 2
        for hop in range(1, 4):
            for part in range(2):
                due = turn == jnp.where(at_end, 2 * hop + part, 4 * hop - 2 + part)
                for way in range(2):
                    @pl.when(due & holds(way, hop))
                    def _():
                        copy(way, hop - 1, part, block_of(way, hop)).wait_recv()

                        @pl.when(can_send(way))
                        def _():
                            copy(way, hop, part, block_of(way, hop)).start()

        block = block_at(step)
        at = pl.ds(pl.multiple_of(half * span, span), span)
        x = normed(xr[block, at])
        keys = mm(x, wp[1]).astype(BF)
        values = (mm(x, wp[2]) + bv[...].reshape(1, -1)).astype(BF)
        hot = key_codes(lens, 2 * block + half, span)
        hot_low, hot_high = hot * low, hot * high
        xt[block, :, at] = x.T
        for i in range(PAIRS):
            cut = slice(128 * i, 128 * (i + 1))
            kn[block, i, at] = keys[:, cut]
            kt[block, i, :, at] = keys[:, cut].T
            vn[block, i, at] = values[:, cut]
            turned = values[:, cut].T
            vta[2 * i, :64] = turned[:64]
            vta[2 * i + 1, :64] = turned[64:]

        def one_pair(i, carry):
            pair = kn[block, i, at]
            scores = [
                mm(pair * low + hot_high, qta[2 * i]),
                mm(pair * high + hot_low, qta[2 * i + 1]),
            ]
            for j in range(2):
                h = 2 * i + j
                before = top[h]
                now = jnp.maximum(before, jnp.max(scores[j], axis=0, keepdims=True))
                raised = jnp.exp(scores[j] - now).astype(BF)
                top[h] = now
                acc[h] = acc[h] * jnp.exp(before - now) + mm(vta[h], raised)
            return carry

        lax.fori_loop(0, PAIRS, one_pair, 0)
        for s in range(4):
            @pl.when(turn == 2 * s + 1)
            def _():
                for c in keeps(s):
                    c.start()

        return carry

    lax.fori_loop(0, 2 * seq, half_step, 0)

    lse_o[...] = jnp.zeros_like(lse_o)
    for h in range(HEADS):
        total = acc[h, 64:65]
        lse_o[h : h + 1] = top[h] + jnp.log(total)
        att_f[64 * h : 64 * (h + 1)] = acc[h, :64] / total
    att_o[...] = att_f[...].T.astype(BF)

    for way in range(2):
        for hop in range(3):
            for half in range(2):
                @pl.when(can_send(way) & holds(way, hop))
                def _():
                    copy(way, hop, half, block_of(way, hop)).wait_send()

    keep_w.wait()
    keep_q.wait()
    keep_qt.wait()
    for step in range(4):
        for c in keeps(step):
            c.wait()


def gather_attend(tokens, lens, gain, shift, w, bq, bv, seq):
    rows, width = tokens.shape
    any_spec = pl.BlockSpec(memory_space=pl.ANY)
    vmem = pl.BlockSpec(memory_space=pltpu.VMEM)
    sds = jax.ShapeDtypeStruct
    outs = [
        sds((seq, PAIRS, rows, 128), BF),
        sds((seq, PAIRS, rows, 128), BF),
        sds((seq, PAIRS, 128, rows), BF),
        sds((seq, width, rows), BF),
        sds((PAIRS, rows, 128), BF),
        sds((PAIRS, 128, rows), BF),
        sds((3, width, width), BF),
        sds((width, rows), F32),
        sds((rows, width), BF),
        sds((16, rows), F32),
    ]
    return pl.pallas_call(
        gather_kernel,
        out_shape=outs,
        in_specs=[any_spec, pl.BlockSpec(memory_space=pltpu.SMEM), vmem, vmem, any_spec, vmem, vmem],
        out_specs=[any_spec] * 7 + [vmem] * 3,
        scratch_shapes=[
            pltpu.VMEM((seq, rows, width), BF),
            pltpu.VMEM((width, 3 * width), BF),
            pltpu.VMEM((3, width, width), BF),
            pltpu.VMEM((seq, PAIRS, rows, 128), BF),
            pltpu.VMEM((seq, PAIRS, rows, 128), BF),
            pltpu.VMEM((seq, PAIRS, 128, rows), BF),
            pltpu.VMEM((seq, width, rows), BF),
            pltpu.VMEM((PAIRS, rows, 128), BF),
            pltpu.VMEM((PAIRS, 128, rows), BF),
            pltpu.VMEM((HEADS, 128, rows), BF),
            pltpu.VMEM((HEADS, 80, rows // 2), BF),
            pltpu.VMEM((HEADS, 80, rows), F32),
            pltpu.VMEM((HEADS, 1, rows), F32),
            pltpu.SemaphoreType.DMA((2, 4, 2)),
            pltpu.SemaphoreType.DMA((2, 4, 2)),
            pltpu.SemaphoreType.DMA((2,)),
            pltpu.SemaphoreType.DMA((20,)),
        ],
        compiler_params=pltpu.CompilerParams(
            collective_id=0, has_side_effects=True, vmem_limit_bytes=58 * MIB
        ),
        name="gather_attend",
    )(tokens, lens, gain, shift, w, bq, bv)


def three_parts(values):
    high = values.astype(BF).astype(F32)
    middle = (values - high).astype(BF).astype(F32)
    return high, middle, values - high - middle


def dp_place():
    dp = lax.axis_index("dp")
    core, x, y = dp % 2, (dp // 2) % 2, dp // 4
    return (core, x, y), (dp + 1 - 2 * core, dp + 2 - 4 * x, dp + 4 - 8 * y)


class DpSum:
    def __init__(self, first, stage, one, two, three, send, recv):
        self.first, self.stage, self.one, self.two, self.three = first, stage, one, two, three
        (self.core, self.x, self.y), (self.to_core, self.to_x, self.to_y) = dp_place()
        self.send, self.recv = send, recv

    def copy(self, phase):
        x_first = self.first == "x"
        if phase == 0:
            src, dst, to = self.stage.at[:, :, 1 - self.core], self.one, self.to_core
        elif phase == 1:
            src = self.one.at[:, 1 - self.x] if x_first else self.one.at[1 - self.y]
            dst, to = self.two, self.to_x if x_first else self.to_y
        else:
            src = self.two.at[1 - self.y] if x_first else self.two.at[1 - self.x]
            dst, to = self.three, self.to_y if x_first else self.to_x
        return pltpu.make_async_remote_copy(
            src_ref=src, dst_ref=dst, send_sem=self.send.at[phase], recv_sem=self.recv.at[phase],
            device_id={"dp": to}, device_id_type=MESH,
        )

    def start(self, phase):
        self.copy(phase).start()

    def finish(self, phase):
        self.copy(phase).wait_recv()
        x_first = self.first == "x"
        if phase == 0:
            for y in range(2):
                for x in range(2):
                    self.one[y, x] = self.one[y, x] + self.stage[y, x, self.core]
        elif phase == 1:
            for other in range(2):
                kept = self.one[other, self.x] if x_first else self.one[self.y, other]
                self.two[other] = self.two[other] + kept
        else:
            kept = self.two[self.y] if x_first else self.two[self.x]
            self.three[...] = self.three[...] + kept

    def wait_sends(self, phases):
        for phase in phases:
            self.copy(phase).wait_send()


class SeqSum:
    def __init__(self, part, from_end, swapped, total, send, recv):
        self.part, self.from_end, self.swapped, self.total = part, from_end, swapped, total
        self.send, self.recv = send, recv
        me = lax.axis_index("seq")
        self.end = (me == 0) | (me == 3)
        self.partner = jnp.where(me < 2, 1 - me, 5 - me)
        self.other = 3 - me

    def copy(self, phase):
        src, dst, to = (
            (self.part, self.from_end, self.partner),
            (self.part, self.swapped, self.other),
            (self.total, self.total, self.partner),
        )[phase]
        return pltpu.make_async_remote_copy(
            src_ref=src, dst_ref=dst, send_sem=self.send.at[phase], recv_sem=self.recv.at[phase],
            device_id={"seq": to}, device_id_type=MESH,
        )

    def ends_send(self):
        @pl.when(self.end)
        def _():
            self.copy(0).start()

    def middles_swap(self):
        @pl.when(~self.end)
        def _():
            self.copy(0).wait_recv()
            self.part[...] = self.part[...] + self.from_end[...]
            self.copy(1).start()

    def middles_send(self):
        @pl.when(~self.end)
        def _():
            self.copy(1).wait_recv()
            self.total[...] = self.part[...] + self.swapped[...]
            self.copy(2).start()

    def finish(self):
        @pl.when(self.end)
        def _():
            self.copy(0).wait_send()
            self.copy(2).wait_recv()

        @pl.when(~self.end)
        def _():
            self.copy(1).wait_send()
            self.copy(2).wait_send()


CHUNKS = 3
GROUPS = 8


def chunk_columns(ff, c, d):
    return (ff // GROUPS) * d + 128 * c


def feed_forward_kernel(fast, *refs):
    (
        tok, att, att_f, cot, w_out, b_out, gain, shift, b_up, b_down, w_up_h, w_down_h,
        layer_o, d_mid_o, d_att_o, d_att_t_o, delta_o, vec_o, vec_up_o, gd_o, gu_o, go_o, *refs,
    ) = refs
    if fast:
        d3_o, u3_o, *refs = refs
    wu, wd, stage_d, stage_u, stage_o, *refs = refs
    if fast:
        one_d, one_u, one_o, two_d, two_u, three_d, three_u, send, recv, *refs = refs
    in_sem, out_sem = refs
    rows, width = tok.shape
    ff = w_up_h.shape[1]
    span = GROUPS * 128

    def loads(c):
        found = []
        for d in range(GROUPS):
            at = pl.ds(chunk_columns(ff, c, d), 128)
            to = pl.ds(128 * d, 128)
            found.append(pltpu.make_async_copy(w_up_h.at[:, at], wu.at[c, :, to], in_sem.at[0, c, d]))
            found.append(pltpu.make_async_copy(w_down_h.at[at], wd.at[c, to], in_sem.at[1, c, d]))
        return found

    for c in range(CHUNKS):
        for copy in loads(c):
            copy.start()
    if fast:
        barrier = pltpu.get_barrier_semaphore()
        for to in dp_place()[1]:
            pl.semaphore_signal(barrier, inc=1, device_id={"dp": to}, device_id_type=MESH)
        pl.semaphore_wait(barrier, 3)
        sums_d = [
            DpSum("x", stage_d.at[c], one_d.at[c], two_d, three_d, send.at[c], recv.at[c]) for c in range(CHUNKS)
        ]
        sums_u = [
            DpSum("y", stage_u.at[c], one_u.at[c], two_u, three_u, send.at[3 + c], recv.at[3 + c]) for c in range(CHUNKS)
        ]
        sum_o = DpSum("x", stage_o, one_o, None, None, send.at[6], recv.at[6])
        kept = [(one_d.at[1], gd_o.at[0]), (one_u.at[1], gu_o.at[0]), (one_d.at[2], gd_o.at[1]), (one_u.at[2], gu_o.at[1])]
        kept += [(one_o, go_o), (three_d, d3_o), (three_u, u3_o)]
        keep = [pltpu.make_async_copy(src, dst, out_sem.at[k]) for k, (src, dst) in enumerate(kept)]

    def per_row(ref):
        return ref[...].reshape(1, -1)

    middle = tok[...].astype(F32) + mm(att[...], w_out[...]) + per_row(b_out)
    average = jnp.mean(middle, axis=-1, keepdims=True)
    centred = middle - average
    scale = lax.rsqrt(jnp.mean(centred * centred, axis=-1, keepdims=True) + EPS)
    unit = centred * scale
    normed = (unit * per_row(gain) + per_row(shift)).astype(BF)
    normed_t = normed.T
    d_out = cot[...]
    up_bias = b_up[...].reshape(1, -1)
    total = middle + per_row(b_down)
    d_normed = jnp.zeros((rows, width), F32)
    vec_up_o[...] = jnp.zeros_like(vec_up_o)
    vec_o[...] = jnp.zeros_like(vec_o)

    for c in range(CHUNKS):
        for copy in loads(c):
            copy.wait()
        bias = jnp.concatenate(
            [up_bias[:, chunk_columns(ff, c, d) : chunk_columns(ff, c, d) + 128] for d in range(GROUPS)], axis=1
        )
        upper = mm(normed, wu[c]) + bias
        cdf = 0.5 * (1.0 + lax.erf(upper * ROOT_HALF))
        hidden = (upper * cdf).astype(BF)
        slope = cdf + upper * (jnp.exp(-0.5 * upper * upper) * 0.3989422804014327)
        d_upper_f = mm_nt(d_out, wd[c]) * slope
        d_upper = d_upper_f.astype(BF)
        vec_up_o[c : c + 1] = jnp.sum(d_upper.astype(F32), axis=0, keepdims=True)
        if fast and c == 1:
            for unit_sum in (sums_d[0], sums_u[0]):
                unit_sum.finish(0)
                unit_sum.start(1)
        if fast and c == 2:
            for unit_sum in (sums_d[1], sums_u[1]):
                unit_sum.finish(0)
            for copy in keep[:2]:
                copy.start()
        total = total + mm(hidden, wd[c])
        d_normed = d_normed + mm_nt(d_upper, wu[c])
        g_down = mm(hidden.T, d_out).astype(BF)
        g_up = mm(normed_t, d_upper).astype(BF)
        for d in range(GROUPS):
            y, x, core = d // 4, (d // 2) % 2, d % 2
            stage_d[c, y, x, core] = g_down[128 * d : 128 * (d + 1)]
            stage_u[c, y, x, core] = g_up[96 * d : 96 * (d + 1)]
        if fast:
            sums_d[c].start(0)
            sums_u[c].start(0)
        if fast and c == 2:
            for unit_sum in (sums_d[0], sums_u[0]):
                unit_sum.finish(1)
                unit_sum.start(2)
    layer_o[...] = total.astype(BF)
    vec_o[3:4] = jnp.sum(d_out.astype(F32), axis=0, keepdims=True)
    vec_o[1:2] = jnp.sum(d_normed * unit, axis=0, keepdims=True)
    vec_o[2:3] = jnp.sum(d_normed, axis=0, keepdims=True)
    scaled = d_normed * per_row(gain)
    d_middle = d_out.astype(F32) + scale * (
        scaled
        - jnp.mean(scaled, axis=-1, keepdims=True)
        - unit * jnp.mean(scaled * unit, axis=-1, keepdims=True)
    )
    d_mid_o[...] = d_middle
    d_branch = d_middle.astype(BF)
    vec_o[0:1] = jnp.sum(d_branch.astype(F32), axis=0, keepdims=True)
    g_out = mm(att_f[...].astype(BF), d_branch).astype(BF)
    for d in range(GROUPS):
        stage_o[d // 4, (d // 2) % 2, d % 2] = g_out[96 * d : 96 * (d + 1)]
    if fast:
        sum_o.start(0)
        for unit_sum in (sums_d[2], sums_u[2]):
            unit_sum.finish(0)
        for copy in keep[2:4]:
            copy.start()
    d_att = mm_nt(d_branch, w_out[...]).astype(BF)
    d_att_o[...] = d_att
    d_att_t = d_att.T
    d_att_t_o[...] = d_att_t
    product = d_att_t.astype(F32) * att_f[...]
    delta_o[...] = jnp.zeros_like(delta_o)
    for h in range(HEADS):
        delta_o[h : h + 1] = jnp.sum(product[64 * h : 64 * (h + 1)], axis=0, keepdims=True)
    if fast:
        sum_o.finish(0)
        keep[4].start()
        for unit_sum in (sums_d[0], sums_u[0]):
            unit_sum.finish(2)
        for copy in keep[5:]:
            copy.start()
        for c in range(CHUNKS):
            phases = (0, 1, 2) if c == 0 else (0,)
            sums_d[c].wait_sends(phases)
            sums_u[c].wait_sends(phases)
        sum_o.wait_sends((0,))
    else:
        keep = [
            pltpu.make_async_copy(stage_d, gd_o, out_sem.at[0]),
            pltpu.make_async_copy(stage_u, gu_o, out_sem.at[1]),
            pltpu.make_async_copy(stage_o, go_o, out_sem.at[2]),
        ]
        for copy in keep:
            copy.start()
    for copy in keep:
        copy.wait()


def feed_forward(fast, tokens, att, att_f, cot, w_out, b_out, gain, shift, b_up, b_down, w_up, w_down):
    rows, width = tokens.shape
    ff = w_up.shape[1]
    span = GROUPS * 128
    part_w, part_o = width // GROUPS, width // GROUPS
    any_spec = pl.BlockSpec(memory_space=pl.ANY)
    vmem = pl.BlockSpec(memory_space=pltpu.VMEM)
    sds = jax.ShapeDtypeStruct
    cube = (2, 2, 2)
    outs = [
        sds((rows, width), BF), sds((rows, width), F32), sds((rows, width), BF), sds((width, rows), BF),
        sds((16, rows), F32), sds((8, width), F32), sds((8, span), F32),
    ]
    out_specs = [vmem] * 7
    scratch = [
        pltpu.VMEM((CHUNKS, width, span), BF),
        pltpu.VMEM((CHUNKS, span, width), BF),
        pltpu.VMEM((CHUNKS, *cube, 128, width), BF),
        pltpu.VMEM((CHUNKS, *cube, part_w, span), BF),
        pltpu.VMEM((*cube, part_o, width), BF),
    ]
    if fast:
        outs += [
            sds((2, 2, 2, 128, width), BF), sds((2, 2, 2, part_w, span), BF), sds((2, 2, part_o, width), BF),
            sds((128, width), BF), sds((part_w, span), BF),
        ]
        scratch += [
            pltpu.VMEM((CHUNKS, 2, 2, 128, width), BF),
            pltpu.VMEM((CHUNKS, 2, 2, part_w, span), BF),
            pltpu.VMEM((2, 2, part_o, width), BF),
            pltpu.VMEM((2, 128, width), BF),
            pltpu.VMEM((2, part_w, span), BF),
            pltpu.VMEM((128, width), BF),
            pltpu.VMEM((part_w, span), BF),
            pltpu.SemaphoreType.DMA((7, 3)),
            pltpu.SemaphoreType.DMA((7, 3)),
        ]
    else:
        outs += [
            sds((CHUNKS, *cube, 128, width), BF), sds((CHUNKS, *cube, part_w, span), BF), sds((*cube, part_o, width), BF),
        ]
    out_specs += [any_spec] * (len(outs) - 7)
    scratch += [pltpu.SemaphoreType.DMA((2, CHUNKS, GROUPS)), pltpu.SemaphoreType.DMA((7,))]
    params = dict(vmem_limit_bytes=58 * MIB)
    if fast:
        params.update(collective_id=1, has_side_effects=True)
    return pl.pallas_call(
        partial(feed_forward_kernel, fast),
        out_shape=outs,
        in_specs=[vmem] * 10 + [any_spec] * 2,
        out_specs=out_specs,
        scratch_shapes=scratch,
        compiler_params=pltpu.CompilerParams(**params),
        name="feed_forward",
    )(tokens, att, att_f, cot, w_out, b_out, gain, shift, b_up, b_down, w_up, w_down)


def attend_back_kernel(fast, *refs):
    (
        kn_h, vn_h, kt_h, xt_h, qn, qt_h, d_att, d_att_t_h, delta, lse, wp_h, lens, tok_h, d_mid_h, gain, vec, vec_up,
        *refs,
    ) = refs
    if fast:
        one_d_h, one_u_h, one_o_h, d3_h, u3_h, *refs = refs
    tok_o, *refs = refs
    if fast:
        fin_d_o, fin_u_o, fin_o_o, fin_q_o, fin_v_o, *refs = refs
    else:
        gw_o, stage_v_o, *refs = refs
    (
        kn, vn, kt, xt, qta, dta, dqt, gk, gv, dk, dv, dq, wp, tok, d_mid, dx_own, dxs, rx, stage_q, stage_v, sums,
        in_sem, load_sem, out_sem, dsend, drecv, *refs,
    ) = refs
    rows, width = d_att.shape
    seq = lax.axis_size("seq")
    me = lax.axis_index("seq")
    has_left, has_right = me > 0, me < seq - 1
    at_end = (me == 0) | (me == seq - 1)
    part_w = width // GROUPS

    barrier = pltpu.get_barrier_semaphore()

    @pl.when(has_left)
    def _():
        pl.semaphore_signal(barrier, inc=1, device_id={"seq": me - 1}, device_id_type=MESH)

    @pl.when(has_right)
    def _():
        pl.semaphore_signal(barrier, inc=1, device_id={"seq": me + 1}, device_id_type=MESH)

    if fast:
        for to in dp_place()[1]:
            pl.semaphore_signal(barrier, inc=1, device_id={"dp": to}, device_id_type=MESH)
    greeted = 3 if fast else 0

    def block_at(step):
        b0 = jnp.where(me < 2, seq - 1, 0)
        b1 = jnp.where(me < 2, seq - 2, 1)
        b2 = jnp.where(me == 0, 1, jnp.where(me == 1, 0, jnp.where(me == 2, 3, 2)))
        return jnp.where(step == 0, b0, jnp.where(step == 1, b1, jnp.where(step == 2, b2, me)))

    def loads(step):
        block, slot = block_at(step), step % 2
        return [
            pltpu.make_async_copy(kn_h.at[block], kn.at[slot], in_sem.at[slot, 0]),
            pltpu.make_async_copy(vn_h.at[block], vn.at[slot], in_sem.at[slot, 1]),
            pltpu.make_async_copy(kt_h.at[block], kt.at[slot], in_sem.at[slot, 2]),
            pltpu.make_async_copy(xt_h.at[block], xt.at[slot], in_sem.at[slot, 3]),
        ]

    fills = []
    for h in range(HEADS):
        own = pl.ds(64 * (h % 2), 64)
        fills.append(pltpu.make_async_copy(qt_h.at[h // 2, own], qta.at[h, own], load_sem.at[h]))
        fills.append(pltpu.make_async_copy(d_att_t_h.at[pl.ds(64 * h, 64)], dta.at[h, own], load_sem.at[HEADS + h]))
    for copy in fills:
        copy.start()
    for copy in loads(0):
        copy.start()
    late = [
        pltpu.make_async_copy(wp_h, wp, load_sem.at[24]),
        pltpu.make_async_copy(tok_h, tok, load_sem.at[25]),
        pltpu.make_async_copy(d_mid_h, d_mid, load_sem.at[26]),
    ]
    if fast:
        (
            one_d, one_u, one_o, two_d, two_u, two_o, three_d, three_u, three_o,
            one_q, two_q, three_q, one_v, two_v, three_v,
            za_d, zx_d, fin_d, za_u, zx_u, fin_u, za_o, zx_o, fin_o, za_q, zx_q, fin_q, za_v, zx_v, fin_v,
            psend, precv, zsend, zrecv,
        ) = refs
        early = [
            pltpu.make_async_copy(d3_h, three_d.at[0], load_sem.at[27]),
            pltpu.make_async_copy(u3_h, three_u.at[0], load_sem.at[28]),
            pltpu.make_async_copy(one_d_h.at[0], one_d.at[0], load_sem.at[29]),
            pltpu.make_async_copy(one_u_h.at[0], one_u.at[0], load_sem.at[30]),
            pltpu.make_async_copy(one_d_h.at[1], one_d.at[1], load_sem.at[31]),
            pltpu.make_async_copy(one_u_h.at[1], one_u.at[1], load_sem.at[32]),
            pltpu.make_async_copy(one_o_h, one_o, load_sem.at[33]),
        ]
        for copy in early[:4]:
            copy.start()
        rs_d = [DpSum("x", None, one_d.at[c], two_d.at[c], three_d.at[c + 1], psend.at[c], precv.at[c]) for c in range(2)]
        rs_u = [
            DpSum("y", None, one_u.at[c], two_u.at[c], three_u.at[c + 1], psend.at[2 + c], precv.at[2 + c])
            for c in range(2)
        ]
        rs_o = DpSum("x", None, one_o, two_o, three_o, psend.at[4], precv.at[4])

        def rs_q(tile, first):
            return DpSum(
                first, stage_q.at[tile], one_q.at[tile], two_q.at[tile], three_q.at[tile],
                psend.at[6 + tile], precv.at[6 + tile],
            )

        def couple(c):
            return rs_q(2 * c, "x"), rs_q(2 * c + 1, "y")

        rs_v = DpSum("x", stage_v, one_v, two_v, three_v, psend.at[5], precv.at[5])
        ar_d = [
            SeqSum(three_d.at[c], za_d.at[c], zx_d.at[c], fin_d.at[c], zsend.at[c], zrecv.at[c]) for c in range(3)
        ]
        ar_u = [
            SeqSum(three_u.at[c], za_u.at[c], zx_u.at[c], fin_u.at[c], zsend.at[3 + c], zrecv.at[3 + c]) for c in range(3)
        ]
        ar_o = SeqSum(three_o, za_o, zx_o, fin_o, zsend.at[6], zrecv.at[6])
        ar_q = [
            SeqSum(three_q.at[c], za_q.at[c], zx_q.at[c], fin_q.at[c], zsend.at[8 + c], zrecv.at[8 + c])
            for c in range(PAIRS)
        ]
        ar_ff = (ar_d[1], ar_u[1], ar_d[2], ar_u[2], ar_o)
        ar_v = SeqSum(three_v, za_v, zx_v, fin_v, zsend.at[7], zrecv.at[7])

    late[0].start()
    if fast:
        for copy in early[4:]:
            copy.start()
    low, high = lane_halves()
    codes = query_codes(lens, me, rows)[:16]
    row16 = lax.broadcasted_iota(jnp.int32, (16, rows), 0)
    blank = jnp.zeros((48, rows), BF)
    for h in range(HEADS):
        first = 64 * (1 - h % 2)
        extra = codes
        for r, part in enumerate(three_parts(-lse[h : h + 1])):
            extra = jnp.where(row16 == 8 + r, part, extra)
        qta[h, first : first + 16] = extra.astype(BF)
        qta[h, first + 16 : first + 64] = blank
        extra = jnp.zeros((16, rows), F32)
        for r, part in enumerate(three_parts(-delta[h : h + 1])):
            extra = jnp.where(row16 == r, part, extra)
        dta[h, first : first + 16] = extra.astype(BF)
        dta[h, first + 16 : first + 64] = blank
    dqt[...] = jnp.zeros_like(dqt)
    stage_v[...] = jnp.zeros_like(stage_v)
    sums[...] = jnp.zeros_like(sums)
    lane = lax.broadcasted_iota(jnp.int32, (1, 128), 1)
    v_low = jnp.where(lane < 3, 1.0, 0.0).astype(BF)
    v_high = jnp.where((lane >= 64) & (lane < 67), 1.0, 0.0).astype(BF)
    for copy in fills:
        copy.wait()

    @pl.when(at_end)
    def _():
        pl.semaphore_wait(barrier, greeted + 1)

    @pl.when(~at_end)
    def _():
        pl.semaphore_wait(barrier, greeted + 2)

    def dx_copy(way, block, half):
        at = pl.ds(half * (rows // 2), rows // 2)
        return pltpu.make_async_remote_copy(
            src_ref=dxs.at[block, at], dst_ref=rx.at[block + way, at],
            send_sem=dsend.at[way, block, half], recv_sem=drecv.at[way, block, half],
            device_id={"seq": me - 1 if way == 0 else me + 1}, device_id_type=MESH,
        )

    def relay_at(place, way, step, half):
        @pl.when(me == place)
        def _():
            block = block_at(step)
            at = pl.ds(half * (rows // 2), rows // 2)
            dx_copy(way, block, half).wait_recv()
            dxs[block, at] = dxs[block, at] + rx[block + way, at]
            dx_copy(way, block, half).start()

    def relay_far(step, half):
        relay_at(1, 1, step, half)
        relay_at(2, 0, step, half)

    def relay_near(half):
        relay_at(1, 0, 2, half)
        relay_at(2, 1, 2, half)

    def send_dx(block, half):
        @pl.when(me == 0)
        def _():
            dx_copy(1, block, half).start()

        @pl.when(me == seq - 1)
        def _():
            dx_copy(0, block, half).start()

    def turn(*sums):
        for unit_sum in sums:
            unit_sum.finish(1)
            unit_sum.start(2)

    def close(*sums):
        for unit_sum in sums:
            unit_sum.finish(2)

    def hooks(g):
        if not fast:
            return

        def at(when, action):
            @pl.when(g == when)
            def _():
                action()

        def chunk0_out():
            for copy in early[:4]:
                copy.wait()
            ar_d[0].ends_send()
            ar_u[0].ends_send()
            rs_d[0].start(1)
            rs_u[0].start(1)

        def chunk2_out():
            for copy in early[4:]:
                copy.wait()
            rs_d[1].start(1)
            rs_u[1].start(1)
            rs_o.start(1)

        at(0, chunk0_out)
        at(12, lambda: (turn(rs_d[0], rs_u[0]), chunk2_out(), ar_d[0].middles_swap(), ar_u[0].middles_swap()))
        at(16, lambda: relay_far(0, 0))
        at(17, lambda: (close(rs_d[0], rs_u[0]), ar_d[1].ends_send(), ar_u[1].ends_send()))
        at(18, lambda: (ar_d[0].middles_send(), ar_u[0].middles_send()))
        at(21, lambda: relay_far(0, 1))
        at(22, lambda: turn(rs_d[1], rs_u[1]))

    def products(slot, i, hot_low, hot_high, part=slice(None)):
        at = pl.ds(pl.multiple_of(i * 128, 128), 128)
        keys, values = kn[slot, i, part], vn[slot, i, part]
        q_pair, d_pair = qn[i], d_att[:, at]
        scores = [
            mm(keys * low + hot_high[part], qta[2 * i]),
            mm(keys * high + hot_low[part], qta[2 * i + 1]),
        ]
        slopes = [
            mm(values * low + v_high, dta[2 * i]),
            mm(values * high + v_low, dta[2 * i + 1]),
        ]
        d_keys = jnp.zeros((keys.shape[0], 128), F32)
        d_values = jnp.zeros((keys.shape[0], 128), F32)
        for j in range(2):
            h = 2 * i + j
            mask = low if j == 0 else high
            probs = jnp.exp(scores[j])
            d_scores = (probs * slopes[j]).astype(BF)
            d_values = d_values + mm(probs.astype(BF), d_pair * mask)
            d_keys = d_keys + mm(d_scores, q_pair * mask)
            dqt[h] += mm(kt[slot, i, 64 * j : 64 * (j + 1), part], d_scores)
        dk[part, at] = d_keys.astype(BF)
        dv[part, at] = d_values.astype(BF)

    def enter(step):
        for copy in loads(step):
            copy.wait()
        hot = key_codes(lens, block_at(step), rows)
        return hot * low, hot * high

    hots = enter(0)
    for copy in loads(1):
        copy.start()
    for half in range(2):
        part = slice(half * (rows // 2), (half + 1) * (rows // 2))

        def one_pair(i, carry):
            hooks(half * PAIRS + i)
            products(0, i, *hots, part)
            return carry

        lax.fori_loop(0, PAIRS, one_pair, 0)
        if half == 0:
            late[0].wait()
        block = block_at(0)
        dxs[block, part] = (mm_nt(dk[part], wp[1]) + mm_nt(dv[part], wp[2])).astype(BF)
        send_dx(block, half)
    gk[...] = mm(xt[0], dk[...])
    gv[...] = mm(xt[0], dv[...])
    sums[3:4] = jnp.sum(dv[...].astype(F32), axis=0, keepdims=True)
    late[1].start()
    late[2].start()

    def one_step(step, carry):
        slot = step % 2
        hots = enter(step)
        for copy in loads(step + 1):
            copy.start()
        block = block_at(step)

        def one_pair(i, carry):
            hooks((step + 1) * PAIRS + i)
            products(slot, i, *hots)
            return carry

        lax.fori_loop(0, PAIRS, one_pair, 0)
        dxs[block] = (mm_nt(dk[...], wp[1]) + mm_nt(dv[...], wp[2])).astype(BF)

        @pl.when((step == 1) | (not fast))
        def _():
            send_dx(block, 0)
            send_dx(block, 1)

        gk[...] += mm(xt[slot], dk[...])
        gv[...] += mm(xt[slot], dv[...])
        sums[3:4] += jnp.sum(dv[...].astype(F32), axis=0, keepdims=True)
        return carry

    lax.fori_loop(1, seq - 1, one_step, 0)

    last = (seq - 1) % 2
    hots = enter(seq - 1)
    lane_w = lax.broadcasted_iota(jnp.int32, (width, 128), 1)
    lo = lane_w < 64

    def one_couple(c, carry):
        if fast:

            @pl.when(c == 0)
            def _():
                turn(rs_o)
                ar_ff[0].middles_swap()
                ar_ff[1].middles_swap()

            @pl.when(c == 1)
            def _():
                close(rs_d[1], rs_u[1], rs_o)
                for unit in ar_ff[2:]:
                    unit.ends_send()
                for half in range(2):
                    send_dx(block_at(2), half)
                    relay_near(half)

            @pl.when(c >= 1)
            def _():
                for unit in couple(c - 1):
                    unit.finish(0)
                    unit.start(1)

            @pl.when(c >= 2)
            def _():
                for unit in couple(c - 2):
                    unit.finish(1)
                    unit.start(2)
                ar_ff[0].middles_send()

        products(last, 2 * c, *hots)
        if fast:

            @pl.when(c == 1)
            def _():
                relay_far(1, 0)

            @pl.when(c == 2)
            def _():
                ar_ff[1].middles_send()
                relay_far(1, 1)

        products(last, 2 * c + 1, *hots)
        at = pl.ds(pl.multiple_of(c * 256, 256), 256)
        turned = dqt[pl.ds(4 * c, 4)].reshape(256, rows) * (HEAD**-0.5)
        dq_part = turned.T.astype(BF)
        dq[:, at] = dq_part
        x_t = xt[last]
        gq_part = mm(x_t, dq_part)
        gk_part = gk[:, at] + mm(x_t, dk[:, at])
        gv_part = gv[:, at] + mm(x_t, dv[:, at])
        for k in range(2):
            cut = slice(128 * k, 128 * (k + 1))
            q_tile, v_tile = gq_part[:, cut], gv_part[:, cut]
            k_tile = pltpu.roll(gk_part[:, cut], 64, 1)
            tiles = jnp.where(lo, q_tile, k_tile), jnp.where(lo, v_tile, q_tile), jnp.where(lo, k_tile, v_tile)
            for j, tile in enumerate(tiles):
                tile = tile.astype(BF)
                for d in range(GROUPS):
                    piece = tile[part_w * d : part_w * (d + 1)]
                    stage_q[2 * c + k, d // 4, (d // 2) % 2, d % 2, :, 128 * j : 128 * (j + 1)] = piece
        if fast:
            for unit in couple(c):
                unit.start(0)
        return carry

    lax.fori_loop(0, PAIRS // 2, one_couple, 0)
    if not fast:
        relay_far(0, 0)
        relay_far(0, 1)
        relay_far(1, 0)
        relay_far(1, 1)
        relay_near(0)
        relay_near(1)
    dx_own[...] = mm_nt(dk[...], wp[1]) + mm_nt(dv[...], wp[2]) + mm_nt(dq[...], wp[0])
    sums[3:4] += jnp.sum(dv[...].astype(F32), axis=0, keepdims=True)
    sums[2:3] = jnp.sum(dq[...].astype(F32), axis=0, keepdims=True)
    if fast:
        for unit in couple(2):
            unit.finish(0)
            unit.start(1)
        for unit in couple(1):
            unit.finish(1)
            unit.start(2)
        for unit in couple(0):
            unit.finish(2)
        for unit in couple(2):
            unit.finish(1)
            unit.start(2)
        for unit in (*couple(1), *couple(2)):
            unit.finish(2)
        for unit in ar_q:
            unit.ends_send()
        for unit in ar_ff[2:]:
            unit.middles_swap()
        ar_ff[2].middles_send()
        ar_ff[3].middles_send()

    late[1].wait()
    late[2].wait()
    for way, there in ((0, has_right), (1, has_left)):
        @pl.when(there)
        def _():
            for half in range(2):
                dx_copy(way, me, half).wait_recv()
            dx_own[...] += rx[me + way].astype(F32)

    values = tok[...].astype(F32)
    centred = values - jnp.mean(values, axis=-1, keepdims=True)
    scale = lax.rsqrt(jnp.mean(centred * centred, axis=-1, keepdims=True) + EPS)
    unit_rows = centred * scale
    d_normed = dx_own[...]
    sums[0:1] = jnp.sum(d_normed * unit_rows, axis=0, keepdims=True)
    sums[1:2] = jnp.sum(d_normed, axis=0, keepdims=True)
    sums[4:8] = vec[0:4]
    rows8 = sums[...]
    for d in range(GROUPS):
        y, x, core = d // 4, (d // 2) % 2, d % 2
        stage_v[y, x, core, 0:8, 0:part_w] = rows8[:, part_w * d : part_w * (d + 1)]
        stage_v[y, x, core, 8 : 8 + CHUNKS] = vec_up[0:CHUNKS, 128 * d : 128 * (d + 1)]
    if fast:
        rs_v.start(0)
    if fast:
        ar_ff[4].middles_send()
        ar_q[0].middles_swap()
        rs_v.finish(0)
        rs_v.start(1)
        ar_q[1].middles_swap()
        ar_q[0].middles_send()
        rs_v.finish(1)
        rs_v.start(2)
        ar_q[2].middles_swap()
        ar_q[1].middles_send()
        rs_v.finish(2)
        ar_v.ends_send()
        ar_q[3].middles_swap()
        ar_q[2].middles_send()
        ar_q[4].middles_swap()
        ar_q[3].middles_send()
    scaled = d_normed * gain[...].reshape(1, -1)
    tok_o[...] = (
        d_mid[...]
        + scale
        * (
            scaled
            - jnp.mean(scaled, axis=-1, keepdims=True)
            - unit_rows * jnp.mean(scaled * unit_rows, axis=-1, keepdims=True)
        )
    ).astype(BF)
    if fast:
        ar_q[5].middles_swap()
        ar_v.middles_swap()
        ar_q[4].middles_send()
        ar_q[5].middles_send()
        ar_v.middles_send()
        for unit in (*ar_d, *ar_u, ar_o, ar_v, *ar_q):
            unit.finish()
        keep = [
            pltpu.make_async_copy(src, dst, out_sem.at[k])
            for k, (src, dst) in enumerate(
                ((fin_d, fin_d_o), (fin_u, fin_u_o), (fin_o, fin_o_o), (fin_q, fin_q_o), (fin_v, fin_v_o))
            )
        ]
        for copy in keep:
            copy.start()
        for unit in (*rs_d, *rs_u, rs_o):
            unit.wait_sends((1, 2))
        for unit in (*couple(0), *couple(1), *couple(2), rs_v):
            unit.wait_sends((0, 1, 2))
        for copy in keep:
            copy.wait()
    else:
        stage_v_o[...] = stage_v[...]
        gw_o[...] = stage_q[...]

    for place, first, second in ((0, 1, 1), (1, 1, 0), (2, 0, 1), (3, 0, 0)):
        @pl.when(me == place)
        def _():
            for step, way in enumerate((first, first, second)):
                for half in range(2):
                    dx_copy(way, block_at(step), half).wait_send()


def attend_back(fast, kn, vn, kt, xt, qn, qt, d_att, d_att_t, delta, lse, wp, lens, tokens, d_mid, gain, vec, vec_up, *ready):
    seq, _, rows, _ = kn.shape
    width = wp.shape[1]
    span = GROUPS * 128
    part = width // GROUPS
    any_spec = pl.BlockSpec(memory_space=pl.ANY)
    vmem = pl.BlockSpec(memory_space=pltpu.VMEM)
    sds = jax.ShapeDtypeStruct
    cube = (2, 2, 2)
    outs = [sds((rows, width), BF)]
    out_specs = [vmem]
    if fast:
        outs += [
            sds((CHUNKS, 128, width), BF), sds((CHUNKS, part, span), BF), sds((part, width), BF),
            sds((PAIRS, part, 384), BF), sds((16, 128), F32),
        ]
        out_specs += [any_spec] * 5
    else:
        outs += [sds((PAIRS, *cube, part, 384), BF), sds((*cube, 16, 128), F32)]
        out_specs += [vmem] * 2
    scratch = [
        pltpu.VMEM((2, PAIRS, rows, 128), BF),
        pltpu.VMEM((2, PAIRS, rows, 128), BF),
        pltpu.VMEM((2, PAIRS, 128, rows), BF),
        pltpu.VMEM((2, width, rows), BF),
        pltpu.VMEM((HEADS, 128, rows), BF),
        pltpu.VMEM((HEADS, 128, rows), BF),
        pltpu.VMEM((HEADS, HEAD, rows), F32),
        pltpu.VMEM((width, width), F32),
        pltpu.VMEM((width, width), F32),
        pltpu.VMEM((rows, width), BF),
        pltpu.VMEM((rows, width), BF),
        pltpu.VMEM((rows, width), BF),
        pltpu.VMEM((3, width, width), BF),
        pltpu.VMEM((rows, width), BF),
        pltpu.VMEM((rows, width), F32),
        pltpu.VMEM((rows, width), F32),
        pltpu.VMEM((seq, rows, width), BF),
        pltpu.VMEM((seq + 1, rows, width), BF),
        pltpu.VMEM((PAIRS, *cube, part, 384), BF),
        pltpu.VMEM((*cube, 16, 128), F32),
        pltpu.VMEM((8, width), F32),
        pltpu.SemaphoreType.DMA((2, 4)),
        pltpu.SemaphoreType.DMA((34,)),
        pltpu.SemaphoreType.DMA((5,)),
        pltpu.SemaphoreType.DMA((2, 4, 2)),
        pltpu.SemaphoreType.DMA((2, 4, 2)),
    ]
    if fast:
        d, u, o, q = (128, width), (part, span), (part, width), (part, 384)
        scratch += [
            pltpu.VMEM(shape, BF)
            for shape in (
                (2, 2, 2, *d), (2, 2, 2, *u), (2, 2, *o), (2, 2, *d), (2, 2, *u), (2, *o), (3, *d), (3, *u), o,
                (PAIRS, 2, 2, *q), (PAIRS, 2, *q), (PAIRS, *q),
            )
        ]
        scratch += [pltpu.VMEM((2, 2, 16, 128), F32), pltpu.VMEM((2, 16, 128), F32), pltpu.VMEM((16, 128), F32)]
        for shape in ((3, *d), (3, *u), o, (PAIRS, *q)):
            scratch += [pltpu.VMEM(shape, BF)] * 3
        scratch += [pltpu.VMEM((16, 128), F32)] * 3
        scratch += [pltpu.SemaphoreType.DMA(shape) for shape in ((12, 3), (12, 3), (14, 3), (14, 3))]
    return pl.pallas_call(
        partial(attend_back_kernel, fast),
        out_shape=outs,
        in_specs=[any_spec] * 4
        + [vmem, any_spec, vmem, any_spec, vmem, vmem, any_spec, pl.BlockSpec(memory_space=pltpu.SMEM)]
        + [any_spec] * 2
        + [vmem] * 3
        + [any_spec] * len(ready),
        out_specs=out_specs,
        scratch_shapes=scratch,
        compiler_params=pltpu.CompilerParams(
            collective_id=2, has_side_effects=True, vmem_limit_bytes=62 * MIB
        ),
        name="attend_back",
    )(kn, vn, kt, xt, qn, qt, d_att, d_att_t, delta, lse, wp, lens, tokens, d_mid, gain, vec, vec_up, *ready)


def unpack_kernel(fin_d, fin_u, fin_o, fin_q, fin_v, down_o, up_o, out_o, qkv_o, *vec_o):
    chunks, _, _ = fin_d.shape
    part, span = fin_u.shape[1:]
    for c in range(chunks):
        down_o[128 * c : 128 * (c + 1)] = fin_d[c].astype(F32)
        for d in range(GROUPS):
            at = chunk_columns(up_o.shape[1], c, d)
            up_o[:, at : at + 128] = fin_u[c, :, 128 * d : 128 * (d + 1)].astype(F32)
    out_o[...] = fin_o[...].astype(F32)
    for i in range(PAIRS):
        qkv_o[:, 384 * i : 384 * (i + 1)] = fin_q[i].astype(F32)
    for r in range(8):
        vec_o[r][...] = fin_v[r : r + 1, :part].reshape(part)
    vec_o[8][...] = jnp.concatenate([fin_v[8 + c : 9 + c] for c in range(chunks)], axis=1).reshape(128 * chunks)


def unpack(fin_d, fin_u, fin_o, fin_q, fin_v):
    vmem = pl.BlockSpec(memory_space=pltpu.VMEM)
    chunks, _, width = fin_d.shape
    part, span = fin_u.shape[1:]
    sds = jax.ShapeDtypeStruct
    outs = [
        sds((128 * chunks, width), F32), sds((part, span * chunks), F32), sds((part, width), F32),
        sds((part, PAIRS * fin_q.shape[2]), F32),
    ]
    outs += [sds((part,), F32)] * 8 + [sds((128 * chunks,), F32)]
    return pl.pallas_call(
        unpack_kernel, out_shape=outs, in_specs=[vmem] * 5, out_specs=[vmem] * len(outs), name="unpack",
    )(fin_d, fin_u, fin_o, fin_q, fin_v)


def local(
    tokens, cell_lengths, ln1_gain, ln1_shift, w_qkv, b_query, b_value, w_out, b_out,
    ln2_gain, ln2_shift, w_up, b_up, w_down, b_down, cotangent,
):
    bucket_count, local_slots, width = tokens.shape
    ff = w_up.shape[1]
    seq_count = lax.axis_size("seq")
    dp_count = lax.axis_size("dp")
    fast = dp_count == GROUPS
    rows = bucket_count * local_slots
    flat = tokens.reshape(rows, width)
    kn, vn, kt, xt, qn, qt, wp, att_t, attended, lse = gather_attend(
        flat, cell_lengths, ln1_gain, ln1_shift, w_qkv, b_query, b_value, seq_count
    )
    layer_out, d_mid, d_att, d_att_t, delta, vec, vec_up, *sums = feed_forward(
        fast, flat, attended, att_t, cotangent.reshape(rows, width), w_out, b_out, ln2_gain, ln2_shift,
        b_up, b_down, w_up, w_down,
    )
    tokens_grad, *found = attend_back(
        fast, kn, vn, kt, xt, qn, qt, d_att, d_att_t, delta, lse, wp, cell_lengths, flat, d_mid, ln1_gain,
        vec, vec_up, *(sums if fast else ()),
    )
    layer_out = layer_out.reshape(tokens.shape)
    tokens_grad = tokens_grad.reshape(tokens.shape)
    if fast:
        down, up, out, qkv, *vectors = unpack(*found)
    else:

        def summed(g):
            share = lax.psum_scatter(g, "dp", scatter_dimension=0, tiled=True)
            return lax.psum(share, "seq").astype(F32)

        g_down, g_up, g_out = sums
        g_qkv, packed = found
        g_qkv = jnp.moveaxis(g_qkv.reshape(PAIRS, width, 384), 0, 1).reshape(width, 3 * width)
        g_down = jnp.moveaxis(g_down.reshape(CHUNKS, GROUPS, 128, width), 0, 1).reshape(ff, width)
        g_up = jnp.transpose(g_up.reshape(CHUNKS, width, GROUPS, 128), (1, 2, 0, 3)).reshape(width, ff)
        down, up, out, qkv = summed(g_down), summed(g_up), summed(g_out.reshape(width, width)), summed(g_qkv)
        packed = packed.reshape(GROUPS, 16, 128)
        vectors = [packed[:, r, : width // GROUPS].reshape(width) for r in range(8)]
        vectors.append(packed[:, 8 : 8 + CHUNKS].reshape(ff))
        together = jnp.concatenate([v.reshape(dp_count, -1) for v in vectors], axis=1)
        together = lax.psum(together, ("dp", "seq"))
        mine = lax.dynamic_index_in_dim(together, lax.axis_index("dp"), 0, keepdims=False)
        sizes = [v.shape[0] // dp_count for v in vectors]
        vectors = [mine[sum(sizes[:k]) : sum(sizes[: k + 1])] for k in range(len(sizes))]
    g1, s1, bq, bv, bo, g2, s2, bd, bu = vectors
    return layer_out, tokens_grad, g1, s1, qkv, bq, bv, out, bo, g2, s2, up, bu, down, bd


def solution(mesh):
    token_spec = P("dp", "seq", None)
    vector, matrix = P("dp"), P("dp", None)
    placed = (token_spec, P("dp", None)) + (P(),) * 13 + (token_spec,)
    return jax.shard_map(
        local,
        mesh=mesh,
        in_specs=placed,
        out_specs=(
            token_spec, token_spec, vector, vector, matrix, vector, vector, matrix, vector,
            vector, vector, matrix, vector, matrix, vector,
        ),
        check_vma=False,
    )
```

```python
from functools import partial

import jax
import jax.numpy as jnp
from jax import lax
from jax.experimental import pallas as pl
from jax.experimental.pallas import tpu as pltpu
from jax.sharding import PartitionSpec as P

HEADS = 12
HEAD = 64
PAIRS = 6
EPS = 1e-05
ROOT_HALF = 0.7071067811865476
BIG = 1e30
MESH = pl.DeviceIdType.MESH
F32 = jnp.float32
BF = jnp.bfloat16
MIB = 1024 * 1024


def normalize(values, gain, shift):
    average = jnp.mean(values, axis=-1, keepdims=True)
    centred = values - average
    variance = jnp.mean(centred * centred, axis=-1, keepdims=True)
    return centred * lax.rsqrt(variance + EPS) * gain + shift


def gelu_exact(values):
    return 0.5 * values * (1.0 + jax.scipy.special.erf(values * ROOT_HALF))


def mm(a, b):
    return jnp.dot(a, b, preferred_element_type=F32)


def mm_nt(a, b):
    return lax.dot_general(a, b, (((1,), (1,)), ((), ())), preferred_element_type=F32)


def cell_bounds(lens_ref, index):
    start = jnp.zeros(index.shape, jnp.int32)
    end = jnp.zeros(index.shape, jnp.int32)
    at = jnp.int32(0)
    for c in range(lens_ref.shape[1]):
        after = at + lens_ref[0, c]
        start = jnp.where(index == c, at, start)
        end = jnp.where(index == c, after, end)
        at = after
    return start, end


def key_codes(lens_ref, block, rows):
    lane = lax.broadcasted_iota(jnp.int32, (1, 128), 1) % 64
    start, end = cell_bounds(lens_ref, lane)
    ones = ((lane >= 8) & (lane < 11)).astype(F32)
    slot = lax.broadcasted_iota(jnp.int32, (rows, 128), 0) + block * rows
    hot = jnp.where((slot >= start) & (slot < end), 1.0, 0.0)
    return (hot + ones).astype(BF)


def query_codes(lens_ref, block, rows):
    cell = lax.broadcasted_iota(jnp.int32, (64, 1), 0)
    start, end = cell_bounds(lens_ref, cell)
    slot = lax.broadcasted_iota(jnp.int32, (64, rows), 1) + block * rows
    inside = (slot >= start) & (slot < end)
    return jnp.where(inside | (cell >= 8), 0.0, -BIG)


def lane_halves():
    lane = lax.broadcasted_iota(jnp.int32, (1, 128), 1)
    low = jnp.where(lane < 64, 1.0, 0.0).astype(BF)
    high = jnp.where(lane < 64, 0.0, 1.0).astype(BF)
    return low, high


def sort_weights(w_ref, wp):
    depth = w_ref.shape[0]
    lane = lax.broadcasted_iota(jnp.int32, (depth, 128), 1)
    low = lane < 64
    for i in range(PAIRS):
        t0, t1, t2 = (w_ref[:, 384 * i + 128 * j : 384 * i + 128 * (j + 1)].astype(F32) for j in range(3))
        at = slice(128 * i, 128 * (i + 1))
        wp[0, :, at] = jnp.where(low, t0, t1).astype(BF)
        wp[1, :, at] = pltpu.roll(jnp.where(low, t2, t0), 64, 1).astype(BF)
        wp[2, :, at] = jnp.where(low, t1, t2).astype(BF)


def gather_kernel(
    tok, lens, gain, shift, w_h, bq, bv,
    kn_o, vn_o, kt_o, xt_o, qn_o, qt_o, wp_o, att_f, att_o, lse_o,
    xr, w, wp, kn, vn, kt, xt, qn, qt, qta, vta, acc, top, send, recv, in_sem, out_sem,
):
    rows, width = tok.shape
    span = rows // 2
    seq = lax.axis_size("seq")
    me = lax.axis_index("seq")
    has_left, has_right = me > 0, me < seq - 1
    at_end = (me == 0) | (me == seq - 1)

    barrier = pltpu.get_barrier_semaphore()

    @pl.when(has_left)
    def _():
        pl.semaphore_signal(barrier, inc=1, device_id={"seq": me - 1}, device_id_type=MESH)

    @pl.when(has_right)
    def _():
        pl.semaphore_signal(barrier, inc=1, device_id={"seq": me + 1}, device_id_type=MESH)

    own_tokens = pltpu.make_async_copy(tok, xr.at[me], in_sem.at[0])
    own_tokens.start()
    weights = pltpu.make_async_copy(w_h, w, in_sem.at[1])
    weights.start()

    @pl.when(at_end)
    def _():
        pl.semaphore_wait(barrier, 1)

    @pl.when(~at_end)
    def _():
        pl.semaphore_wait(barrier, 2)

    def copy(way, hop, half, block):
        at = pl.ds(half * span, span)
        return pltpu.make_async_remote_copy(
            src_ref=tok.at[at] if hop == 0 else xr.at[block, at],
            dst_ref=xr.at[block, at],
            send_sem=send.at[way, hop, half],
            recv_sem=recv.at[way, hop, half],
            device_id={"seq": me - 1 if way == 0 else me + 1},
            device_id_type=MESH,
        )

    def can_send(way):
        return has_left if way == 0 else has_right

    def holds(way, hop):
        return me + hop < seq if way == 0 else me - hop >= 0

    def block_of(way, hop):
        return me + hop if way == 0 else me - hop

    for half in range(2):
        for way in range(2):
            @pl.when(can_send(way))
            def _():
                copy(way, 0, half, me).start()

    def normed(raw):
        return normalize(raw.astype(F32), gain[...].reshape(1, -1), shift[...].reshape(1, -1)).astype(BF)

    row16 = lax.broadcasted_iota(jnp.int32, (16, span), 0)
    for h in range(HEADS):
        vta[h, 64:] = jnp.where(row16 == 0, 1.0, 0.0).astype(BF)
    acc[...] = jnp.zeros_like(acc)
    top[...] = jnp.full_like(top, -3e38)
    codes = query_codes(lens, me, rows).astype(BF)
    low, high = lane_halves()
    own_tokens.wait()
    weights.wait()
    sort_weights(w, wp)
    keep_w = pltpu.make_async_copy(wp, wp_o, out_sem.at[0])
    keep_w.start()
    q = ((mm(normed(xr[me]), wp[0]) + bq[...].reshape(1, -1)).astype(BF).astype(F32) * (HEAD**-0.5)).astype(BF)
    for i in range(PAIRS):
        pair = q[:, 128 * i : 128 * (i + 1)]
        qn[i] = pair
        turned = pair.T
        qt[i] = turned
        qta[2 * i, :64] = turned[:64]
        qta[2 * i, 64:] = codes
        qta[2 * i + 1, :64] = codes
        qta[2 * i + 1, 64:] = turned[64:]
    keep_q = pltpu.make_async_copy(qn, qn_o, out_sem.at[1])
    keep_q.start()
    keep_qt = pltpu.make_async_copy(qt, qt_o, out_sem.at[2])
    keep_qt.start()

    def keeps(step):
        block = block_at(step)
        return [
            pltpu.make_async_copy(kn.at[block], kn_o.at[block], out_sem.at[3 + 4 * step]),
            pltpu.make_async_copy(vn.at[block], vn_o.at[block], out_sem.at[4 + 4 * step]),
            pltpu.make_async_copy(kt.at[block], kt_o.at[block], out_sem.at[5 + 4 * step]),
            pltpu.make_async_copy(xt.at[block], xt_o.at[block], out_sem.at[6 + 4 * step]),
        ]

    def block_at(step):
        from_end = jnp.where(me == 0, step, seq - 1 - step)
        from_mid = jnp.where(step == 0, me, jnp.where(step == 1, me + 1, jnp.where(step == 2, me - 1, jnp.where(me == 1, seq - 1, 0))))
        return jnp.where(at_end, from_end, from_mid)

    def half_step(turn, carry):
        step, half = turn // 2, turn % 2
        for hop in range(1, 4):
            for part in range(2):
                due = turn == jnp.where(at_end, 2 * hop + part, 4 * hop - 2 + part)
                for way in range(2):
                    @pl.when(due & holds(way, hop))
                    def _():
                        copy(way, hop - 1, part, block_of(way, hop)).wait_recv()

                        @pl.when(can_send(way))
                        def _():
                            copy(way, hop, part, block_of(way, hop)).start()

        block = block_at(step)
        at = pl.ds(pl.multiple_of(half * span, span), span)
        x = normed(xr[block, at])
        keys = mm(x, wp[1]).astype(BF)
        values = (mm(x, wp[2]) + bv[...].reshape(1, -1)).astype(BF)
        hot = key_codes(lens, 2 * block + half, span)
        hot_low, hot_high = hot * low, hot * high
        xt[block, :, at] = x.T
        for i in range(PAIRS):
            cut = slice(128 * i, 128 * (i + 1))
            kn[block, i, at] = keys[:, cut]
            kt[block, i, :, at] = keys[:, cut].T
            vn[block, i, at] = values[:, cut]
            turned = values[:, cut].T
            vta[2 * i, :64] = turned[:64]
            vta[2 * i + 1, :64] = turned[64:]

        def one_pair(i, carry):
            pair = kn[block, i, at]
            scores = [
                mm(pair * low + hot_high, qta[2 * i]),
                mm(pair * high + hot_low, qta[2 * i + 1]),
            ]
            for j in range(2):
                h = 2 * i + j
                before = top[h]
                now = jnp.maximum(before, jnp.max(scores[j], axis=0, keepdims=True))
                raised = jnp.exp(scores[j] - now).astype(BF)
                top[h] = now
                acc[h] = acc[h] * jnp.exp(before - now) + mm(vta[h], raised)
            return carry

        lax.fori_loop(0, PAIRS, one_pair, 0)
        for s in range(4):
            @pl.when(turn == 2 * s + 1)
            def _():
                for c in keeps(s):
                    c.start()

        return carry

    lax.fori_loop(0, 2 * seq, half_step, 0)

    lse_o[...] = jnp.zeros_like(lse_o)
    for h in range(HEADS):
        total = acc[h, 64:65]
        lse_o[h : h + 1] = top[h] + jnp.log(total)
        att_f[64 * h : 64 * (h + 1)] = acc[h, :64] / total
    att_o[...] = att_f[...].T.astype(BF)

    for way in range(2):
        for hop in range(3):
            for half in range(2):
                @pl.when(can_send(way) & holds(way, hop))
                def _():
                    copy(way, hop, half, block_of(way, hop)).wait_send()

    keep_w.wait()
    keep_q.wait()
    keep_qt.wait()
    for step in range(4):
        for c in keeps(step):
            c.wait()


def gather_attend(tokens, lens, gain, shift, w, bq, bv, seq):
    rows, width = tokens.shape
    any_spec = pl.BlockSpec(memory_space=pl.ANY)
    vmem = pl.BlockSpec(memory_space=pltpu.VMEM)
    sds = jax.ShapeDtypeStruct
    outs = [
        sds((seq, PAIRS, rows, 128), BF),
        sds((seq, PAIRS, rows, 128), BF),
        sds((seq, PAIRS, 128, rows), BF),
        sds((seq, width, rows), BF),
        sds((PAIRS, rows, 128), BF),
        sds((PAIRS, 128, rows), BF),
        sds((3, width, width), BF),
        sds((width, rows), F32),
        sds((rows, width), BF),
        sds((16, rows), F32),
    ]
    return pl.pallas_call(
        gather_kernel,
        out_shape=outs,
        in_specs=[any_spec, pl.BlockSpec(memory_space=pltpu.SMEM), vmem, vmem, any_spec, vmem, vmem],
        out_specs=[any_spec] * 7 + [vmem] * 3,
        scratch_shapes=[
            pltpu.VMEM((seq, rows, width), BF),
            pltpu.VMEM((width, 3 * width), BF),
            pltpu.VMEM((3, width, width), BF),
            pltpu.VMEM((seq, PAIRS, rows, 128), BF),
            pltpu.VMEM((seq, PAIRS, rows, 128), BF),
            pltpu.VMEM((seq, PAIRS, 128, rows), BF),
            pltpu.VMEM((seq, width, rows), BF),
            pltpu.VMEM((PAIRS, rows, 128), BF),
            pltpu.VMEM((PAIRS, 128, rows), BF),
            pltpu.VMEM((HEADS, 128, rows), BF),
            pltpu.VMEM((HEADS, 80, rows // 2), BF),
            pltpu.VMEM((HEADS, 80, rows), F32),
            pltpu.VMEM((HEADS, 1, rows), F32),
            pltpu.SemaphoreType.DMA((2, 4, 2)),
            pltpu.SemaphoreType.DMA((2, 4, 2)),
            pltpu.SemaphoreType.DMA((2,)),
            pltpu.SemaphoreType.DMA((20,)),
        ],
        compiler_params=pltpu.CompilerParams(
            collective_id=0, has_side_effects=True, vmem_limit_bytes=58 * MIB
        ),
        name="gather_attend",
    )(tokens, lens, gain, shift, w, bq, bv)


def three_parts(values):
    high = values.astype(BF).astype(F32)
    middle = (values - high).astype(BF).astype(F32)
    return high, middle, values - high - middle


def add_parts(total, other, parts=1, step=32):
    depth = total.shape[-2] // step

    def some(k, carry):
        at = (pl.ds(pl.multiple_of(k % depth * step, step), step),)
        if len(total.shape) == 3:
            at = (k // depth, *at)
        total[at] = total[at] + other[at]
        return carry

    lax.fori_loop(0, parts * depth, some, 0)


def dp_place():
    dp = lax.axis_index("dp")
    core, x, y = dp % 2, (dp // 2) % 2, dp // 4
    return (core, x, y), (dp + 1 - 2 * core, dp + 2 - 4 * x, dp + 4 - 8 * y)


class DpSum:
    def __init__(self, first, stage, one, two, three, send, recv):
        self.first, self.stage, self.one, self.two, self.three = first, stage, one, two, three
        (self.core, self.x, self.y), (self.to_core, self.to_x, self.to_y) = dp_place()
        self.send, self.recv = send, recv
        self.step = min(32, three.shape[-2])

    def copy(self, phase):
        x_first = self.first == "x"
        if phase == 0:
            src, dst, to = self.stage.at[:, :, 1 - self.core], self.one, self.to_core
        elif phase == 1:
            src = self.one.at[:, 1 - self.x] if x_first else self.one.at[1 - self.y]
            dst, to = self.two, self.to_x if x_first else self.to_y
        else:
            src = self.two.at[1 - self.y] if x_first else self.two.at[1 - self.x]
            dst, to = self.three, self.to_y if x_first else self.to_x
        return pltpu.make_async_remote_copy(
            src_ref=src, dst_ref=dst, send_sem=self.send.at[phase], recv_sem=self.recv.at[phase],
            device_id={"dp": to}, device_id_type=MESH,
        )

    def start(self, phase):
        self.copy(phase).start()

    def finish(self, phase):
        self.copy(phase).wait_recv()
        x_first = self.first == "x"
        if phase == 0:
            for y in range(2):
                add_parts(self.one.at[y], self.stage.at[y, :, self.core], 2, self.step)
        elif phase == 1:
            add_parts(self.two, self.one.at[:, self.x] if x_first else self.one.at[self.y], 2, self.step)
        else:
            add_parts(self.three, self.two.at[self.y] if x_first else self.two.at[self.x], 1, self.step)

    def wait_sends(self, phases):
        for phase in phases:
            self.copy(phase).wait_send()


class SeqSum:
    def __init__(self, part, total, swapped, send, recv):
        self.part, self.total, self.swapped = part, total, swapped
        self.send, self.recv = send, recv
        me = lax.axis_index("seq")
        self.end = (me == 0) | (me == 3)
        self.partner = jnp.where(me < 2, 1 - me, 5 - me)
        self.other = 3 - me

    def copy(self, phase):
        src, dst, to = (
            (self.part, self.total, self.partner),
            (self.part, self.swapped, self.other),
            (self.total, self.total, self.partner),
        )[phase]
        return pltpu.make_async_remote_copy(
            src_ref=src, dst_ref=dst, send_sem=self.send.at[phase], recv_sem=self.recv.at[phase],
            device_id={"seq": to}, device_id_type=MESH,
        )

    def ends_send(self):
        @pl.when(self.end)
        def _():
            self.copy(0).start()

    def middles_swap(self):
        @pl.when(~self.end)
        def _():
            self.copy(0).wait_recv()
            add_parts(self.part, self.total, 1, min(32, self.part.shape[-2]))
            self.copy(1).start()

    def middles_send(self):
        @pl.when(~self.end)
        def _():
            self.copy(1).wait_recv()
            depth = min(32, self.part.shape[-2])

            def some(k, carry):
                at = pl.ds(pl.multiple_of(k * depth, depth), depth)
                self.total[at] = self.part[at] + self.swapped[at]
                return carry

            lax.fori_loop(0, self.part.shape[-2] // depth, some, 0)
            self.copy(2).start()

    def finish(self):
        @pl.when(self.end)
        def _():
            self.copy(0).wait_send()
            self.copy(2).wait_recv()

        @pl.when(~self.end)
        def _():
            self.copy(1).wait_send()
            self.copy(2).wait_send()


CHUNKS = 3
GROUPS = 8


def chunk_columns(ff, c, d):
    return (ff // GROUPS) * d + 128 * c


def place_of(d):
    return d // 4, (d // 2) % 2, d % 2


def layer_back_kernel(fast, *refs):
    (
        kn_h, vn_h, kt_h, xt_h, qn_h, qt_h, wp_h, att_h, att_f_h, tok_h, cot_h, w_out_h, w_up_h, w_down_h,
        lse, lens, gain_one, b_out, gain, shift, b_up, b_down, *refs,
    ) = refs
    layer_o, tok_o, *refs = refs
    if fast:
        fin_d_o, fin_u_o, fin_o_o, fin_q_o, fin_v_o, *refs = refs
    else:
        gd_o, gu_o, go_o, gq_o, stage_v_o, *refs = refs
    (
        stage_d, stage_u, stage_o, stage_v, sums, vec_up, d_att, dta, d_mid, rx,
        ff_sem, in_sem, load_sem, out_sem, dsend, drecv, *refs,
    ) = refs
    rows, width = tok_h.shape
    ff = w_up_h.shape[1]
    span = GROUPS * 128
    part_w = width // GROUPS
    seq = lax.axis_size("seq")
    me = lax.axis_index("seq")
    has_left, has_right = me > 0, me < seq - 1
    at_end = (me == 0) | (me == seq - 1)
    half_rows = rows // 2

    barrier = pltpu.get_barrier_semaphore()

    @pl.when(has_left)
    def _():
        pl.semaphore_signal(barrier, inc=1, device_id={"seq": me - 1}, device_id_type=MESH)

    @pl.when(has_right)
    def _():
        pl.semaphore_signal(barrier, inc=1, device_id={"seq": me + 1}, device_id_type=MESH)

    if fast:
        for to in dp_place()[1]:
            pl.semaphore_signal(barrier, inc=1, device_id={"dp": to}, device_id_type=MESH)
    greeted = 3 if fast else 0

    def meet():
        @pl.when(at_end)
        def _():
            pl.semaphore_wait(barrier, greeted + 1)

        @pl.when(~at_end)
        def _():
            pl.semaphore_wait(barrier, greeted + 2)

    if fast:
        (
            one_d, one_u, one_o, two_d, two_u, two_o, three_d, three_u, three_o,
            one_q, two_q, three_q, one_v, two_v, three_v,
            zx_d, fin_d, zx_u, fin_u, zx_o, fin_o, zx_q, fin_q, zx_v, fin_v,
            psend, precv, zsend, zrecv,
        ) = refs
        rs_d = [
            DpSum("x", stage_d.at[c], one_d.at[c], two_d.at[c], three_d.at[c], psend.at[c], precv.at[c])
            for c in range(CHUNKS)
        ]
        rs_u = [
            DpSum("y", stage_u.at[c], one_u.at[c], two_u.at[c], three_u.at[c], psend.at[3 + c], precv.at[3 + c])
            for c in range(CHUNKS)
        ]
        rs_o = DpSum("x", stage_o, one_o, two_o, three_o, psend.at[6], precv.at[6])
        rs_v = DpSum("x", stage_v, one_v, two_v, three_v, psend.at[7], precv.at[7])

        def couple(c):
            found = []
            for k in range(2):
                tile = 2 * c + k
                staged = stage_u.at[c, :, :, :, :, pl.ds(384 * k, 384)]
                found.append(
                    DpSum(
                        "xy"[k], staged, one_q.at[tile], two_q.at[tile], three_q.at[tile],
                        psend.at[8 + tile], precv.at[8 + tile],
                    )
                )
            return found

        ar_d = [
            SeqSum(three_d.at[c], fin_d.at[c], zx_d.at[c], zsend.at[c], zrecv.at[c]) for c in range(CHUNKS)
        ]
        ar_u = [
            SeqSum(three_u.at[c], fin_u.at[c], zx_u.at[c], zsend.at[3 + c], zrecv.at[3 + c])
            for c in range(CHUNKS)
        ]
        ar_o = SeqSum(three_o, fin_o, zx_o, zsend.at[6], zrecv.at[6])
        ar_v = SeqSum(three_v, fin_v, zx_v, zsend.at[7], zrecv.at[7])
        ar_q = [
            SeqSum(three_q.at[c], fin_q.at[c], zx_q.at[c], zsend.at[8 + c], zrecv.at[8 + c])
            for c in range(PAIRS)
        ]

    def turn(*found):
        for unit_sum in found:
            unit_sum.finish(1)
            unit_sum.start(2)

    def close(*found):
        for unit_sum in found:
            unit_sum.finish(2)

    def per_row(ref):
        return ref[...].reshape(1, -1)

    stage_v[...] = jnp.zeros_like(stage_v)
    sums[...] = jnp.zeros_like(sums)

    def feed_forward(tok, att, att_f, cot, w_out, wu, wd, d_norm, bias):
        first = [
            pltpu.make_async_copy(src, dst, ff_sem.at[2, k // GROUPS, k % GROUPS])
            for k, (src, dst) in enumerate(((tok_h, tok), (att_h, att), (w_out_h, w_out), (cot_h, cot), (att_f_h, att_f)))
        ]

        def loads(c):
            found = []
            for d in range(GROUPS):
                at = pl.ds(chunk_columns(ff, c, d), 128)
                to = pl.ds(128 * d, 128)
                found.append(pltpu.make_async_copy(w_up_h.at[:, at], wu.at[c % 2, :, to], ff_sem.at[0, c, d]))
                found.append(pltpu.make_async_copy(w_down_h.at[at], wd.at[c % 2, to], ff_sem.at[1, c, d]))
            return found

        for copy in (*first[:3], *loads(0), *first[3:], *loads(1)):
            copy.start()
        meet()
        for copy in first[:3]:
            copy.wait()
        middle = tok[...].astype(F32) + mm(att[...], w_out[...]) + per_row(b_out)
        average = jnp.mean(middle, axis=-1, keepdims=True)
        centred = middle - average
        scale = lax.rsqrt(jnp.mean(centred * centred, axis=-1, keepdims=True) + EPS)
        unit = centred * scale
        normed = (unit * per_row(gain) + per_row(shift)).astype(BF)
        normed_t = normed.T
        for copy in first[3:]:
            copy.wait()
        d_out = cot[...]
        for c in range(CHUNKS):
            for d in range(GROUPS):
                at = chunk_columns(ff, c, d)
                bias[c : c + 1, 128 * d : 128 * (d + 1)] = b_up[at : at + 128].reshape(1, 128)
        d_mid[...] = middle + per_row(b_down)
        d_norm[...] = jnp.zeros_like(d_norm)

        def one_chunk(c, carry):
            for copy in loads(c):
                copy.wait()
            slot = c % 2
            upper = mm(normed, wu[slot]) + bias[pl.ds(c, 1)]
            cdf = 0.5 * (1.0 + lax.erf(upper * ROOT_HALF))
            hidden = (upper * cdf).astype(BF)
            slope = cdf + upper * (jnp.exp(-0.5 * upper * upper) * 0.3989422804014327)
            d_upper = (mm_nt(d_out, wd[slot]) * slope).astype(BF)
            vec_up[pl.ds(c, 1)] = jnp.sum(d_upper.astype(F32), axis=0, keepdims=True)
            if fast:

                @pl.when(c == 1)
                def _():
                    for unit_sum in (rs_d[0], rs_u[0]):
                        unit_sum.finish(0)
                        unit_sum.start(1)

                @pl.when(c == 2)
                def _():
                    for unit_sum in (rs_d[1], rs_u[1]):
                        unit_sum.finish(0)

            g_down = mm(hidden.T, d_out).astype(BF)
            g_up = mm(normed_t, d_upper).astype(BF)
            for d in range(GROUPS):
                stage_d[(c, *place_of(d))] = g_down[128 * d : 128 * (d + 1)]
                stage_u[(c, *place_of(d))] = g_up[96 * d : 96 * (d + 1)]
            if fast:
                for k in range(CHUNKS):

                    @pl.when(c == k)
                    def _():
                        rs_d[k].start(0)
                        rs_u[k].start(0)
                        if k == 2:
                            turn(rs_d[0], rs_u[0])
                            rs_d[1].start(1)
                            rs_u[1].start(1)

            d_mid[...] += mm(hidden, wd[slot])
            d_norm[...] += mm_nt(d_upper, wu[slot])

            @pl.when(c == 0)
            def _():
                for copy in loads(2):
                    copy.start()

            return carry

        lax.fori_loop(0, CHUNKS, one_chunk, 0)
        d_normed = d_norm[...]
        tok[...] = d_mid[...].astype(BF)
        keep_layer = pltpu.make_async_copy(tok, layer_o, out_sem.at[5])
        keep_layer.start()
        sums[7:8] = jnp.sum(d_out.astype(F32), axis=0, keepdims=True)
        sums[5:6] = jnp.sum(d_normed * unit, axis=0, keepdims=True)
        sums[6:7] = jnp.sum(d_normed, axis=0, keepdims=True)
        scaled = d_normed * per_row(gain)
        d_middle = d_out.astype(F32) + scale * (
            scaled
            - jnp.mean(scaled, axis=-1, keepdims=True)
            - unit * jnp.mean(scaled * unit, axis=-1, keepdims=True)
        )
        d_mid[...] = d_middle
        d_branch = d_middle.astype(BF)
        sums[4:5] = jnp.sum(d_branch.astype(F32), axis=0, keepdims=True)
        g_out = mm(att_f[...].astype(BF), d_branch).astype(BF)
        for d in range(GROUPS):
            stage_o[place_of(d)] = g_out[96 * d : 96 * (d + 1)]
        if fast:
            rs_o.start(0)
            for unit_sum in (rs_d[2], rs_u[2]):
                unit_sum.finish(0)
            close(rs_d[0], rs_u[0])
            ar_d[0].ends_send()
            ar_u[0].ends_send()
        d_attended = mm_nt(d_branch, w_out[...]).astype(BF)
        d_att[...] = d_attended
        turned = d_attended.T
        product = turned.astype(F32) * att_f[...]
        row16 = lax.broadcasted_iota(jnp.int32, (16, rows), 0)
        for h in range(HEADS):
            own, other = 64 * (h % 2), 64 * (1 - h % 2)
            dta[h, own : own + 64] = turned[64 * h : 64 * (h + 1)]
            delta = jnp.sum(product[64 * h : 64 * (h + 1)], axis=0, keepdims=True)
            extra = jnp.zeros((16, rows), F32)
            for r, part in enumerate(three_parts(-delta)):
                extra = jnp.where(row16 == r, part, extra)
            dta[h, other : other + 16] = extra.astype(BF)
            dta[h, other + 16 : other + 64] = jnp.zeros((48, rows), BF)
        if fast:
            rs_o.finish(0)
        else:
            keep = [
                pltpu.make_async_copy(stage_d, gd_o, out_sem.at[0]),
                pltpu.make_async_copy(stage_u, gu_o, out_sem.at[1]),
                pltpu.make_async_copy(stage_o, go_o, out_sem.at[2]),
            ]
            for copy in keep:
                copy.start()
            for copy in keep:
                copy.wait()
        keep_layer.wait()

    pl.run_scoped(
        feed_forward,
        pltpu.VMEM((rows, width), BF),
        pltpu.VMEM((rows, width), BF),
        pltpu.VMEM((width, rows), F32),
        pltpu.VMEM((rows, width), BF),
        pltpu.VMEM((width, width), BF),
        pltpu.VMEM((2, width, span), BF),
        pltpu.VMEM((2, span, width), BF),
        pltpu.VMEM((rows, width), F32),
        pltpu.VMEM((8, span), F32),
    )

    def block_at(step):
        b0 = jnp.where(me < 2, seq - 1, 0)
        b1 = jnp.where(me < 2, seq - 2, 1)
        b2 = jnp.where(me == 0, 1, jnp.where(me == 1, 0, jnp.where(me == 2, 3, 2)))
        return jnp.where(step == 0, b0, jnp.where(step == 1, b1, jnp.where(step == 2, b2, me)))

    def dx_stage(step, half):
        return stage_d.at[step // 2, step % 2, half]

    def dx_copy(way, step, block, half):
        return pltpu.make_async_remote_copy(
            src_ref=dx_stage(step, half), dst_ref=rx.at[block + way, half],
            send_sem=dsend.at[way, block, half], recv_sem=drecv.at[way, block, half],
            device_id={"seq": me - 1 if way == 0 else me + 1}, device_id_type=MESH,
        )

    def store_dx(step, half, value):
        for k in range(2):
            stage_d[step // 2, step % 2, half, k] = value[128 * k : 128 * (k + 1)]

    def relay_at(place, way, step, half):
        @pl.when(me == place)
        def _():
            block = block_at(step)
            dx_copy(way, step, block, half).wait_recv()
            add_parts(dx_stage(step, half), rx.at[block + way, half], 2)
            dx_copy(way, step, block, half).start()

    def relay_far(step, half):
        relay_at(1, 1, step, half)
        relay_at(2, 0, step, half)

    def relay_near(half):
        relay_at(1, 0, 2, half)
        relay_at(2, 1, 2, half)

    def send_dx(step, half):
        block = block_at(step)

        @pl.when(me == 0)
        def _():
            dx_copy(1, step, block, half).start()

        @pl.when(me == seq - 1)
        def _():
            dx_copy(0, step, block, half).start()

    def attention(kn, vn, kt, xt, qta, dqt, gk, gv, dk, dv, dq, wp, qn, hot_ref):
        def loads(step):
            block, slot = block_at(step), step % 2
            return [
                pltpu.make_async_copy(kn_h.at[block], kn.at[slot], in_sem.at[slot, 0]),
                pltpu.make_async_copy(vn_h.at[block], vn.at[slot], in_sem.at[slot, 1]),
                pltpu.make_async_copy(kt_h.at[block], kt.at[slot], in_sem.at[slot, 2]),
            ]

        def load_x(step):
            return pltpu.make_async_copy(xt_h.at[block_at(step)], xt, in_sem.at[0, 3])

        fills = [pltpu.make_async_copy(qn_h, qn, load_sem.at[HEADS])]
        for h in range(HEADS):
            own = pl.ds(64 * (h % 2), 64)
            fills.append(pltpu.make_async_copy(qt_h.at[h // 2, own], qta.at[h, own], load_sem.at[h]))
        load_wp = pltpu.make_async_copy(wp_h, wp, load_sem.at[HEADS + 1])
        for copy in (*loads(0), *fills, load_x(0), load_wp):
            copy.start()
        low, high = lane_halves()
        codes = query_codes(lens, me, rows)[:16]
        row16 = lax.broadcasted_iota(jnp.int32, (16, rows), 0)
        for h in range(HEADS):
            other = 64 * (1 - h % 2)
            extra = codes
            for r, part in enumerate(three_parts(-lse[h : h + 1])):
                extra = jnp.where(row16 == 8 + r, part, extra)
            qta[h, other : other + 16] = extra.astype(BF)
            qta[h, other + 16 : other + 64] = jnp.zeros((48, rows), BF)
        dqt[...] = jnp.zeros_like(dqt)
        lane = lax.broadcasted_iota(jnp.int32, (1, 128), 1)
        v_low = jnp.where(lane < 3, 1.0, 0.0).astype(BF)
        v_high = jnp.where((lane >= 64) & (lane < 67), 1.0, 0.0).astype(BF)
        if fast:
            for unit_sum in rs_d:
                unit_sum.wait_sends((0,))
        for copy in fills:
            copy.wait()

        def hooks(g):
            if not fast:
                return

            def at(when, action):
                @pl.when(g == when)
                def _():
                    action()

            def second():
                turn(rs_d[1], rs_u[1])
                for unit_sum in (rs_d[2], rs_u[2], rs_o):
                    unit_sum.start(1)

            at(5, second)
            at(6, lambda: (ar_d[0].middles_swap(), ar_u[0].middles_swap()))
            at(12, lambda: (close(rs_d[1], rs_u[1]), ar_d[1].ends_send(), ar_u[1].ends_send()))
            at(14, lambda: relay_far(0, 0))
            at(16, lambda: (ar_d[0].middles_send(), ar_u[0].middles_send()))
            at(17, lambda: turn(rs_d[2], rs_u[2]))
            at(20, lambda: relay_far(0, 1))
            at(21, lambda: (turn(rs_o), close(rs_d[2], rs_u[2])))
            at(23, lambda: (close(rs_o), [unit.ends_send() for unit in (ar_d[2], ar_u[2], ar_o)]))

        def products(slot, i, part=slice(None)):
            at = pl.ds(pl.multiple_of(i * 128, 128), 128)
            keys, values = kn[slot, i, part], vn[slot, i, part]
            q_pair, d_pair = qn[i], d_att[:, at]
            hot = hot_ref[part]
            scores = [
                mm(keys * low + hot * high, qta[2 * i]),
                mm(keys * high + hot * low, qta[2 * i + 1]),
            ]
            slopes = [
                mm(values * low + v_high, dta[2 * i]),
                mm(values * high + v_low, dta[2 * i + 1]),
            ]
            d_keys = jnp.zeros((keys.shape[0], 128), F32)
            d_values = jnp.zeros((keys.shape[0], 128), F32)
            for j in range(2):
                h = 2 * i + j
                mask = low if j == 0 else high
                probs = jnp.exp(scores[j])
                d_scores = (probs * slopes[j]).astype(BF)
                d_values = d_values + mm(probs.astype(BF), d_pair * mask)
                d_keys = d_keys + mm(d_scores, q_pair * mask)
                dqt[h] += mm(kt[slot, i, 64 * j : 64 * (j + 1), part], d_scores)
            dk[part, at] = d_keys.astype(BF)
            dv[part, at] = d_values.astype(BF)

        def enter(step):
            for copy in loads(step):
                copy.wait()
            hot_ref[...] = key_codes(lens, block_at(step), rows)

        enter(0)
        for copy in loads(1):
            copy.start()

        def one_half(half, carry):
            part = pl.ds(pl.multiple_of(half * half_rows, half_rows), half_rows)

            def one_pair(i, carry):
                hooks(half * PAIRS + i)
                products(0, i, part)
                return carry

            lax.fori_loop(0, PAIRS, one_pair, 0)

            @pl.when(half == 0)
            def _():
                load_wp.wait()

            store_dx(0, half, (mm_nt(dk[part], wp[1]) + mm_nt(dv[part], wp[2])).astype(BF))
            send_dx(0, half)
            return carry

        lax.fori_loop(0, 2, one_half, 0)
        load_x(0).wait()
        gk[...] = mm(xt[...], dk[...])
        gv[...] = mm(xt[...], dv[...])
        load_x(1).start()
        sums[3:4] = jnp.sum(dv[...].astype(F32), axis=0, keepdims=True)

        def one_step(step, carry):
            slot = step % 2
            enter(step)
            for copy in loads(step + 1):
                copy.start()

            def one_pair(i, carry):
                hooks((step + 1) * PAIRS + i)
                products(slot, i)
                return carry

            lax.fori_loop(0, PAIRS, one_pair, 0)
            dx = (mm_nt(dk[...], wp[1]) + mm_nt(dv[...], wp[2])).astype(BF)
            for half in range(2):
                store_dx(step, half, dx[half * half_rows : (half + 1) * half_rows])
                send_dx(step, half)
            load_x(step).wait()
            gk[...] += mm(xt[...], dk[...])
            gv[...] += mm(xt[...], dv[...])
            load_x(step + 1).start()
            sums[3:4] += jnp.sum(dv[...].astype(F32), axis=0, keepdims=True)
            return carry

        lax.fori_loop(1, seq - 1, one_step, 0)

        last = (seq - 1) % 2
        enter(seq - 1)
        load_x(seq - 1).wait()
        lane_w = lax.broadcasted_iota(jnp.int32, (width, 128), 1)
        lo = lane_w < 64
        if fast:
            for unit_sum in rs_u:
                unit_sum.wait_sends((0,))

        def one_couple(c, carry):
            if fast:

                @pl.when(c == 0)
                def _():
                    relay_near(0)
                    ar_d[1].middles_swap()
                    ar_u[1].middles_swap()

                @pl.when(c == 1)
                def _():
                    relay_near(1)
                    relay_far(1, 0)

                @pl.when(c == 2)
                def _():
                    relay_far(1, 1)
                    ar_d[1].middles_send()
                    ar_u[1].middles_send()

                @pl.when(c >= 1)
                def _():
                    for unit in couple(c - 1):
                        unit.finish(0)
                        unit.start(1)

                @pl.when(c >= 2)
                def _():
                    turn(*couple(c - 2))


            def one_pair(k, carry):
                products(last, 2 * c + k)
                return carry

            lax.fori_loop(0, 2, one_pair, 0)
            at = pl.ds(pl.multiple_of(c * 256, 256), 256)
            turned = dqt[pl.ds(4 * c, 4)].reshape(256, rows) * (HEAD**-0.5)
            dq_part = turned.T.astype(BF)
            dq[:, at] = dq_part
            x_t = xt[...]
            gq_part = mm(x_t, dq_part)
            gk_part = gk[:, at] + mm(x_t, dk[:, at])
            gv_part = gv[:, at] + mm(x_t, dv[:, at])
            for k in range(2):
                cut = slice(128 * k, 128 * (k + 1))
                q_tile, v_tile = gq_part[:, cut], gv_part[:, cut]
                k_tile = pltpu.roll(gk_part[:, cut], 64, 1)
                tiles = jnp.where(lo, q_tile, k_tile), jnp.where(lo, v_tile, q_tile), jnp.where(lo, k_tile, v_tile)
                for j, tile in enumerate(tiles):
                    tile = tile.astype(BF)
                    to = slice(384 * k + 128 * j, 384 * k + 128 * (j + 1))
                    for d in range(GROUPS):
                        stage_u[(c, *place_of(d), slice(None), to)] = tile[part_w * d : part_w * (d + 1)]
            if fast:
                for unit in couple(c):
                    unit.start(0)
            return carry

        lax.fori_loop(0, PAIRS // 2, one_couple, 0)
        if not fast:
            for step in range(2):
                for half in range(2):
                    relay_far(step, half)
            relay_near(0)
            relay_near(1)
        dx_own = gk.at[pl.ds(0, rows)]
        dx_own[...] = mm_nt(dk[...], wp[1]) + mm_nt(dv[...], wp[2]) + mm_nt(dq[...], wp[0])
        sums[3:4] += jnp.sum(dv[...].astype(F32), axis=0, keepdims=True)
        sums[2:3] = jnp.sum(dq[...].astype(F32), axis=0, keepdims=True)
        load_tok = pltpu.make_async_copy(tok_h, dv, load_sem.at[HEADS + 2])
        load_tok.start()
        if fast:
            for unit in couple(2):
                unit.finish(0)
                unit.start(1)
            turn(*couple(1))
            close(*couple(0))
            ar_d[2].middles_swap()
            turn(*couple(2))
            ar_u[2].middles_swap()
            close(*couple(1), *couple(2))
            ar_o.middles_swap()
            for unit in ar_q:
                unit.ends_send()
            ar_d[2].middles_send()
            ar_u[2].middles_send()

        load_tok.wait()
        for way, there in ((0, has_right), (1, has_left)):
            @pl.when(there)
            def _():
                for half in range(2):
                    dx_copy(way, 0, me, half).wait_recv()

                def some(k, carry):
                    at = pl.ds(pl.multiple_of(k * 32, 32), 32)
                    piece = rx[me + way, k // 8, k // 4 % 2, pl.ds(pl.multiple_of(k % 4 * 32, 32), 32)]
                    dx_own[at] += piece.astype(F32)
                    return carry

                lax.fori_loop(0, rows // 32, some, 0)

        values = dv[...].astype(F32)
        centred = values - jnp.mean(values, axis=-1, keepdims=True)
        scale = lax.rsqrt(jnp.mean(centred * centred, axis=-1, keepdims=True) + EPS)
        unit_rows = centred * scale
        d_normed = dx_own[...]
        sums[0:1] = jnp.sum(d_normed * unit_rows, axis=0, keepdims=True)
        sums[1:2] = jnp.sum(d_normed, axis=0, keepdims=True)
        rows8 = sums[...]
        for d in range(GROUPS):
            y, x, core = place_of(d)
            stage_v[y, x, core, 0:8, 0:part_w] = rows8[:, part_w * d : part_w * (d + 1)]
            stage_v[y, x, core, 8 : 8 + CHUNKS] = vec_up[0:CHUNKS, 128 * d : 128 * (d + 1)]
        if fast:
            rs_v.start(0)
        if fast:
            ar_o.middles_send()
            ar_q[0].middles_swap()
            rs_v.finish(0)
            rs_v.start(1)
            ar_q[1].middles_swap()
            ar_q[0].middles_send()
            rs_v.finish(1)
            rs_v.start(2)
            ar_q[2].middles_swap()
            ar_q[1].middles_send()
            rs_v.finish(2)
            ar_v.ends_send()
            ar_q[3].middles_swap()
            ar_q[2].middles_send()
            ar_q[4].middles_swap()
            ar_q[3].middles_send()
        scaled = d_normed * per_row(gain_one)
        dk[...] = (
            d_mid[...]
            + scale
            * (
                scaled
                - jnp.mean(scaled, axis=-1, keepdims=True)
                - unit_rows * jnp.mean(scaled * unit_rows, axis=-1, keepdims=True)
            )
        ).astype(BF)
        keep = [pltpu.make_async_copy(dk, tok_o, out_sem.at[6])]
        keep[0].start()
        if fast:
            ar_q[5].middles_swap()
            ar_v.middles_swap()
            ar_q[4].middles_send()
            ar_q[5].middles_send()
            ar_v.middles_send()
            for unit in (*ar_d, *ar_u, ar_o, ar_v, *ar_q):
                unit.finish()
            done = ((fin_d, fin_d_o), (fin_u, fin_u_o), (fin_o, fin_o_o), (fin_q, fin_q_o), (fin_v, fin_v_o))
            for unit in (*rs_d, *rs_u):
                unit.wait_sends((1, 2))
            for unit in (rs_o, rs_v, *couple(0), *couple(1), *couple(2)):
                unit.wait_sends((0, 1, 2))
        else:
            done = ((stage_u, gq_o), (stage_v, stage_v_o))
        keep += [pltpu.make_async_copy(src, dst, out_sem.at[k]) for k, (src, dst) in enumerate(done)]
        for copy in keep[1:]:
            copy.start()
        for copy in keep:
            copy.wait()

        for place, first, second in ((0, 1, 1), (1, 1, 0), (2, 0, 1), (3, 0, 0)):
            @pl.when(me == place)
            def _():
                for step, way in enumerate((first, first, second)):
                    for half in range(2):
                        dx_copy(way, step, block_at(step), half).wait_send()

    pl.run_scoped(
        attention,
        pltpu.VMEM((2, PAIRS, rows, 128), BF),
        pltpu.VMEM((2, PAIRS, rows, 128), BF),
        pltpu.VMEM((2, PAIRS, 128, rows), BF),
        pltpu.VMEM((width, rows), BF),
        pltpu.VMEM((HEADS, 128, rows), BF),
        pltpu.VMEM((HEADS, HEAD, rows), F32),
        pltpu.VMEM((width, width), F32),
        pltpu.VMEM((width, width), F32),
        pltpu.VMEM((rows, width), BF),
        pltpu.VMEM((rows, width), BF),
        pltpu.VMEM((rows, width), BF),
        pltpu.VMEM((3, width, width), BF),
        pltpu.VMEM((PAIRS, rows, 128), BF),
        pltpu.VMEM((rows, 128), BF),
    )


def layer_back(fast, *args):
    kn, wp = args[0], args[6]
    seq, _, rows, _ = kn.shape
    width = wp.shape[1]
    span = GROUPS * 128
    part = width // GROUPS
    any_spec = pl.BlockSpec(memory_space=pl.ANY)
    vmem = pl.BlockSpec(memory_space=pltpu.VMEM)
    sds = jax.ShapeDtypeStruct
    cube = (2, 2, 2)
    outs = [sds((rows, width), BF), sds((rows, width), BF)]
    if fast:
        outs += [
            sds((CHUNKS, 128, width), BF), sds((CHUNKS, part, span), BF), sds((part, width), BF),
            sds((PAIRS, part, 384), BF), sds((16, 128), F32),
        ]
    else:
        outs += [
            sds((CHUNKS, *cube, 128, width), BF), sds((CHUNKS, *cube, part, span), BF), sds((*cube, part, width), BF),
            sds((CHUNKS, *cube, part, span), BF), sds((*cube, 16, 128), F32),
        ]
    scratch = [
        pltpu.VMEM((CHUNKS, *cube, 128, width), BF),
        pltpu.VMEM((CHUNKS, *cube, part, span), BF),
        pltpu.VMEM((*cube, part, width), BF),
        pltpu.VMEM((*cube, 16, 128), F32),
        pltpu.VMEM((8, width), F32),
        pltpu.VMEM((8, span), F32),
        pltpu.VMEM((rows, width), BF),
        pltpu.VMEM((HEADS, 128, rows), BF),
        pltpu.VMEM((rows, width), F32),
        pltpu.VMEM((seq + 1, 2, 2, 128, width), BF),
        pltpu.SemaphoreType.DMA((3, CHUNKS, GROUPS)),
        pltpu.SemaphoreType.DMA((2, 4)),
        pltpu.SemaphoreType.DMA((HEADS + 3,)),
        pltpu.SemaphoreType.DMA((7,)),
        pltpu.SemaphoreType.DMA((2, 4, 2)),
        pltpu.SemaphoreType.DMA((2, 4, 2)),
    ]
    if fast:
        d, u, o, q = (128, width), (part, span), (part, width), (part, 384)
        scratch += [
            pltpu.VMEM(shape, BF)
            for shape in (
                (CHUNKS, 2, 2, *d), (CHUNKS, 2, 2, *u), (2, 2, *o), (CHUNKS, 2, *d), (CHUNKS, 2, *u), (2, *o),
                (CHUNKS, *d), (CHUNKS, *u), o, (PAIRS, 2, 2, *q), (PAIRS, 2, *q), (PAIRS, *q),
            )
        ]
        scratch += [pltpu.VMEM((2, 2, 16, 128), F32), pltpu.VMEM((2, 16, 128), F32), pltpu.VMEM((16, 128), F32)]
        for shape in ((CHUNKS, *d), (CHUNKS, *u), o, (PAIRS, *q)):
            scratch += [pltpu.VMEM(shape, BF)] * 2
        scratch += [pltpu.VMEM((16, 128), F32)] * 2
        scratch += [pltpu.SemaphoreType.DMA((14, 3))] * 4
    return pl.pallas_call(
        partial(layer_back_kernel, fast),
        out_shape=outs,
        in_specs=[any_spec] * 14 + [vmem, pl.BlockSpec(memory_space=pltpu.SMEM)] + [vmem] * 6,
        out_specs=[any_spec] * len(outs),
        scratch_shapes=scratch,
        compiler_params=pltpu.CompilerParams(
            collective_id=1, has_side_effects=True, vmem_limit_bytes=62 * MIB
        ),
        name="layer_back",
    )(*args)


def unpack_kernel(fin_d, fin_u, fin_o, fin_q, fin_v, down_o, up_o, out_o, qkv_o, *vec_o):
    chunks, _, _ = fin_d.shape
    part, span = fin_u.shape[1:]
    for c in range(chunks):
        down_o[128 * c : 128 * (c + 1)] = fin_d[c].astype(F32)
        for d in range(GROUPS):
            at = chunk_columns(up_o.shape[1], c, d)
            up_o[:, at : at + 128] = fin_u[c, :, 128 * d : 128 * (d + 1)].astype(F32)
    out_o[...] = fin_o[...].astype(F32)
    for i in range(PAIRS):
        qkv_o[:, 384 * i : 384 * (i + 1)] = fin_q[i].astype(F32)
    for r in range(8):
        vec_o[r][...] = fin_v[r : r + 1, :part].reshape(part)
    vec_o[8][...] = jnp.concatenate([fin_v[8 + c : 9 + c] for c in range(chunks)], axis=1).reshape(128 * chunks)


def unpack(fin_d, fin_u, fin_o, fin_q, fin_v):
    vmem = pl.BlockSpec(memory_space=pltpu.VMEM)
    chunks, _, width = fin_d.shape
    part, span = fin_u.shape[1:]
    sds = jax.ShapeDtypeStruct
    outs = [
        sds((128 * chunks, width), F32), sds((part, span * chunks), F32), sds((part, width), F32),
        sds((part, PAIRS * fin_q.shape[2]), F32),
    ]
    outs += [sds((part,), F32)] * 8 + [sds((128 * chunks,), F32)]
    return pl.pallas_call(
        unpack_kernel, out_shape=outs, in_specs=[vmem] * 5, out_specs=[vmem] * len(outs), name="unpack",
    )(fin_d, fin_u, fin_o, fin_q, fin_v)


def local(
    tokens, cell_lengths, ln1_gain, ln1_shift, w_qkv, b_query, b_value, w_out, b_out,
    ln2_gain, ln2_shift, w_up, b_up, w_down, b_down, cotangent,
):
    bucket_count, local_slots, width = tokens.shape
    ff = w_up.shape[1]
    seq_count = lax.axis_size("seq")
    dp_count = lax.axis_size("dp")
    fast = dp_count == GROUPS
    rows = bucket_count * local_slots
    flat = tokens.reshape(rows, width)
    kn, vn, kt, xt, qn, qt, wp, att_t, attended, lse = gather_attend(
        flat, cell_lengths, ln1_gain, ln1_shift, w_qkv, b_query, b_value, seq_count
    )
    layer_out, tokens_grad, *found = layer_back(
        fast, kn, vn, kt, xt, qn, qt, wp, attended, att_t, flat, cotangent.reshape(rows, width), w_out, w_up, w_down,
        lse, cell_lengths, ln1_gain, b_out, ln2_gain, ln2_shift, b_up, b_down,
    )
    layer_out = layer_out.reshape(tokens.shape)
    tokens_grad = tokens_grad.reshape(tokens.shape)
    if fast:
        down, up, out, qkv, *vectors = unpack(*found)
    else:

        def summed(g):
            share = lax.psum_scatter(g, "dp", scatter_dimension=0, tiled=True)
            return lax.psum(share, "seq").astype(F32)

        g_down, g_up, g_out, g_qkv, packed = found
        g_qkv = g_qkv.reshape(CHUNKS, width, GROUPS * 128)[:, :, :768]
        g_qkv = jnp.moveaxis(g_qkv, 0, 1).reshape(width, 3 * width)
        g_down = jnp.moveaxis(g_down.reshape(CHUNKS, GROUPS, 128, width), 0, 1).reshape(ff, width)
        g_up = jnp.transpose(g_up.reshape(CHUNKS, width, GROUPS, 128), (1, 2, 0, 3)).reshape(width, ff)
        down, up, out, qkv = summed(g_down), summed(g_up), summed(g_out.reshape(width, width)), summed(g_qkv)
        packed = packed.reshape(GROUPS, 16, 128)
        vectors = [packed[:, r, : width // GROUPS].reshape(width) for r in range(8)]
        vectors.append(packed[:, 8 : 8 + CHUNKS].reshape(ff))
        together = jnp.concatenate([v.reshape(dp_count, -1) for v in vectors], axis=1)
        together = lax.psum(together, ("dp", "seq"))
        mine = lax.dynamic_index_in_dim(together, lax.axis_index("dp"), 0, keepdims=False)
        sizes = [v.shape[0] // dp_count for v in vectors]
        vectors = [mine[sum(sizes[:k]) : sum(sizes[: k + 1])] for k in range(len(sizes))]
    g1, s1, bq, bv, bo, g2, s2, bd, bu = vectors
    return layer_out, tokens_grad, g1, s1, qkv, bq, bv, out, bo, g2, s2, up, bu, down, bd


def solution(mesh):
    token_spec = P("dp", "seq", None)
    vector, matrix = P("dp"), P("dp", None)
    placed = (token_spec, P("dp", None)) + (P(),) * 13 + (token_spec,)
    return jax.shard_map(
        local,
        mesh=mesh,
        in_specs=placed,
        out_specs=(
            token_spec, token_spec, vector, vector, matrix, vector, vector, matrix, vector,
            vector, vector, matrix, vector, matrix, vector,
        ),
        check_vma=False,
    )
```

```python
from functools import partial

import jax
import jax.numpy as jnp
from jax import lax
from jax.experimental import pallas as pl
from jax.experimental.pallas import tpu as pltpu
from jax.sharding import PartitionSpec as P

HEADS = 12
HEAD = 64
PAIRS = 6
EPS = 1e-05
ROOT_HALF = 0.7071067811865476
BIG = 1e30
MESH = pl.DeviceIdType.MESH
F32 = jnp.float32
BF = jnp.bfloat16
MIB = 1024 * 1024


def normalize(values, gain, shift):
    average = jnp.mean(values, axis=-1, keepdims=True)
    centred = values - average
    variance = jnp.mean(centred * centred, axis=-1, keepdims=True)
    return centred * lax.rsqrt(variance + EPS) * gain + shift


def gelu_exact(values):
    return 0.5 * values * (1.0 + jax.scipy.special.erf(values * ROOT_HALF))


def mm(a, b):
    return jnp.dot(a, b, preferred_element_type=F32)


def mm_nt(a, b):
    return lax.dot_general(a, b, (((1,), (1,)), ((), ())), preferred_element_type=F32)


def cell_bounds(lens_ref, index):
    start = jnp.zeros(index.shape, jnp.int32)
    end = jnp.zeros(index.shape, jnp.int32)
    at = jnp.int32(0)
    for c in range(lens_ref.shape[1]):
        after = at + lens_ref[0, c]
        start = jnp.where(index == c, at, start)
        end = jnp.where(index == c, after, end)
        at = after
    return start, end


def key_codes(lens_ref, block, rows):
    lane = lax.broadcasted_iota(jnp.int32, (1, 128), 1) % 64
    start, end = cell_bounds(lens_ref, lane)
    ones = ((lane >= 8) & (lane < 11)).astype(F32)
    slot = lax.broadcasted_iota(jnp.int32, (rows, 128), 0) + block * rows
    hot = jnp.where((slot >= start) & (slot < end), 1.0, 0.0)
    return (hot + ones).astype(BF)


def query_codes(lens_ref, block, rows):
    cell = lax.broadcasted_iota(jnp.int32, (64, 1), 0)
    start, end = cell_bounds(lens_ref, cell)
    slot = lax.broadcasted_iota(jnp.int32, (64, rows), 1) + block * rows
    inside = (slot >= start) & (slot < end)
    return jnp.where(inside | (cell >= 8), 0.0, -BIG)


def lane_halves():
    lane = lax.broadcasted_iota(jnp.int32, (1, 128), 1)
    low = jnp.where(lane < 64, 1.0, 0.0).astype(BF)
    high = jnp.where(lane < 64, 0.0, 1.0).astype(BF)
    return low, high


def sort_weights(w_ref, wp):
    depth = w_ref.shape[0]
    lane = lax.broadcasted_iota(jnp.int32, (depth, 128), 1)
    low = lane < 64
    for i in range(PAIRS):
        t0, t1, t2 = (w_ref[:, 384 * i + 128 * j : 384 * i + 128 * (j + 1)].astype(F32) for j in range(3))
        at = slice(128 * i, 128 * (i + 1))
        wp[0, :, at] = jnp.where(low, t0, t1).astype(BF)
        wp[1, :, at] = pltpu.roll(jnp.where(low, t2, t0), 64, 1).astype(BF)
        wp[2, :, at] = jnp.where(low, t1, t2).astype(BF)


def gather_kernel(
    tok, lens, gain, shift, w_h, bq, bv,
    kn_o, vn_o, kt_o, xt_o, qn_o, qt_o, wp_o, att_o, lse_o,
    xr, w, wp, kn, vn, kt, xt, qn, qt, qta, vta, acc, top, att_t, send, recv, in_sem, out_sem,
):
    rows, width = tok.shape
    span = rows // 2
    seq = lax.axis_size("seq")
    me = lax.axis_index("seq")
    has_left, has_right = me > 0, me < seq - 1
    at_end = (me == 0) | (me == seq - 1)

    barrier = pltpu.get_barrier_semaphore()

    @pl.when(has_left)
    def _():
        pl.semaphore_signal(barrier, inc=1, device_id={"seq": me - 1}, device_id_type=MESH)

    @pl.when(has_right)
    def _():
        pl.semaphore_signal(barrier, inc=1, device_id={"seq": me + 1}, device_id_type=MESH)

    own_tokens = pltpu.make_async_copy(tok, xr.at[me], in_sem.at[0])
    own_tokens.start()
    weights = pltpu.make_async_copy(w_h, w, in_sem.at[1])
    weights.start()

    @pl.when(at_end)
    def _():
        pl.semaphore_wait(barrier, 1)

    @pl.when(~at_end)
    def _():
        pl.semaphore_wait(barrier, 2)

    def copy(way, hop, quarter, block):
        at = pl.ds(quarter * (rows // 4), rows // 4)
        return pltpu.make_async_remote_copy(
            src_ref=tok.at[at] if hop == 0 else xr.at[block, at],
            dst_ref=xr.at[block, at],
            send_sem=send.at[way, hop, quarter],
            recv_sem=recv.at[way, hop, quarter],
            device_id={"seq": me - 1 if way == 0 else me + 1},
            device_id_type=MESH,
        )

    def can_send(way):
        return has_left if way == 0 else has_right

    def holds(way, hop):
        return me + hop < seq if way == 0 else me - hop >= 0

    def block_of(way, hop):
        return me + hop if way == 0 else me - hop

    for quarter in range(4):
        for way in range(2):
            @pl.when(can_send(way))
            def _():
                copy(way, 0, quarter, me).start()

    def normed(raw):
        return normalize(raw.astype(F32), gain[...].reshape(1, -1), shift[...].reshape(1, -1)).astype(BF)

    row16 = lax.broadcasted_iota(jnp.int32, (16, span), 0)
    for h in range(HEADS):
        vta[h, 64:] = jnp.where(row16 == 0, 1.0, 0.0).astype(BF)
    acc[...] = jnp.zeros_like(acc)
    top[...] = jnp.full_like(top, -3e38)
    codes = query_codes(lens, me, rows).astype(BF)
    low, high = lane_halves()
    own_tokens.wait()
    weights.wait()
    sort_weights(w, wp)
    keep_w = pltpu.make_async_copy(wp, wp_o, out_sem.at[4, 0])
    keep_w.start()
    q = ((mm(normed(xr[me]), wp[0]) + bq[...].reshape(1, -1)).astype(BF).astype(F32) * (HEAD**-0.5)).astype(BF)
    for i in range(PAIRS):
        pair = q[:, 128 * i : 128 * (i + 1)]
        qn[i] = pair
        turned = pair.T
        qt[i] = turned
        qta[2 * i, :64] = turned[:64]
        qta[2 * i, 64:] = codes
        qta[2 * i + 1, :64] = codes
        qta[2 * i + 1, 64:] = turned[64:]
    keep_q = pltpu.make_async_copy(qn, qn_o, out_sem.at[4, 1])
    keep_q.start()
    keep_qt = pltpu.make_async_copy(qt, qt_o, out_sem.at[4, 2])
    keep_qt.start()

    def keep_att(i):
        at = pl.ds(128 * i, 128)
        return pltpu.make_async_copy(att_t.at[at], att_o.at[at], out_sem.at[5, i])

    def keeps(step):
        block = block_at(step)
        return [
            pltpu.make_async_copy(src.at[block], dst.at[block], out_sem.at[step, k])
            for k, (src, dst) in enumerate(((kn, kn_o), (vn, vn_o), (kt, kt_o), (xt, xt_o)))
        ]

    def block_at(step):
        from_end = jnp.where(me == 0, step, seq - 1 - step)
        from_mid = jnp.where(step == 0, me, jnp.where(step == 1, me + 1, jnp.where(step == 2, me - 1, jnp.where(me == 1, seq - 1, 0))))
        return jnp.where(at_end, from_end, from_mid)

    def arrive(due, way, hop, quarter):
        @pl.when(due & holds(way, hop))
        def _():
            block = block_of(way, hop)
            copy(way, hop - 1, quarter, block).wait_recv()

            @pl.when(can_send(way))
            def _():
                copy(way, hop, quarter, block).start()

    def attend(step, part, span):
        block = block_at(step)
        at = pl.ds(pl.multiple_of(part * span, span), span)
        x = normed(xr[block, at])
        keys = mm(x, wp[1]).astype(BF)
        values = (mm(x, wp[2]) + bv[...].reshape(1, -1)).astype(BF)
        hot = key_codes(lens, block * (rows // span) + part, span)
        hot_low, hot_high = hot * low, hot * high
        xt[block, :, at] = x.T
        for i in range(PAIRS):
            cut = slice(128 * i, 128 * (i + 1))
            kn[block, i, at] = keys[:, cut]
            kt[block, i, :, at] = keys[:, cut].T
            vn[block, i, at] = values[:, cut]
            turned = values[:, cut].T
            vta[2 * i, :64, :span] = turned[:64]
            vta[2 * i + 1, :64, :span] = turned[64:]

        @pl.when(part == rows // span - 1)
        def _():
            for c in keeps(step):
                c.start()

        def one_pair(i, carry):
            pair = kn[block, i, at]
            scores = [
                mm(pair * low + hot_high, qta[2 * i]),
                mm(pair * high + hot_low, qta[2 * i + 1]),
            ]
            for j in range(2):
                h = 2 * i + j
                before = top[h]
                now = jnp.maximum(before, jnp.max(scores[j], axis=0, keepdims=True))
                raised = jnp.exp(scores[j] - now).astype(BF)
                top[h] = now
                acc[h] = acc[h] * jnp.exp(before - now) + mm(vta[h, :, :span], raised)
            return carry

        lax.fori_loop(0, PAIRS, one_pair, 0)

    def half_step(turn, carry):
        for hop in range(1, 3):
            for quarter in range(4):
                first = jnp.where(at_end, 2 * hop, 2 * hop if hop == 1 else -2)
                for way in range(2):
                    arrive(turn == first + quarter // 2, way, hop, quarter)
        attend(turn // 2, turn % 2, rows // 2)
        return carry

    def last_step(turn, carry):
        for hop in range(2, 4):
            for quarter in range(4):
                due = (turn == quarter) & (at_end if hop == 3 else ~at_end)
                for way in range(2):
                    arrive(due, way, hop, quarter)
        attend(seq - 1, turn, rows // 4)
        return carry

    lax.fori_loop(0, 2 * (seq - 1), half_step, 0)
    lax.fori_loop(0, 4, last_step, 0)

    for i in range(PAIRS):
        for j in range(2):
            h = 2 * i + j
            total = acc[h, 64:65]
            lse_o[h : h + 1] = top[h] + jnp.log(total)
            att_t[64 * h : 64 * (h + 1)] = (acc[h, :64] * (1.0 / total)).astype(BF)
        keep_att(i).start()
    lse_o[HEADS:] = jnp.zeros((16 - HEADS, rows), F32)

    for way in range(2):
        for hop in range(3):
            for quarter in range(4):
                @pl.when(can_send(way) & holds(way, hop))
                def _():
                    copy(way, hop, quarter, block_of(way, hop)).wait_send()

    keep_w.wait()
    keep_q.wait()
    keep_qt.wait()
    for i in range(PAIRS):
        keep_att(i).wait()
    for step in range(4):
        for c in keeps(step):
            c.wait()


def gather_attend(tokens, lens, gain, shift, w, bq, bv, seq):
    rows, width = tokens.shape
    any_spec = pl.BlockSpec(memory_space=pl.ANY)
    vmem = pl.BlockSpec(memory_space=pltpu.VMEM)
    sds = jax.ShapeDtypeStruct
    outs = [
        sds((seq, PAIRS, rows, 128), BF),
        sds((seq, PAIRS, rows, 128), BF),
        sds((seq, PAIRS, 128, rows), BF),
        sds((seq, width, rows), BF),
        sds((PAIRS, rows, 128), BF),
        sds((PAIRS, 128, rows), BF),
        sds((3, width, width), BF),
        sds((width, rows), BF),
        sds((16, rows), F32),
    ]
    return pl.pallas_call(
        gather_kernel,
        out_shape=outs,
        in_specs=[any_spec, pl.BlockSpec(memory_space=pltpu.SMEM), vmem, vmem, any_spec, vmem, vmem],
        out_specs=[any_spec] * 8 + [vmem],
        scratch_shapes=[
            pltpu.VMEM((seq, rows, width), BF),
            pltpu.VMEM((width, 3 * width), BF),
            pltpu.VMEM((3, width, width), BF),
            pltpu.VMEM((seq, PAIRS, rows, 128), BF),
            pltpu.VMEM((seq, PAIRS, rows, 128), BF),
            pltpu.VMEM((seq, PAIRS, 128, rows), BF),
            pltpu.VMEM((seq, width, rows), BF),
            pltpu.VMEM((PAIRS, rows, 128), BF),
            pltpu.VMEM((PAIRS, 128, rows), BF),
            pltpu.VMEM((HEADS, 128, rows), BF),
            pltpu.VMEM((HEADS, 80, rows // 2), BF),
            pltpu.VMEM((HEADS, 80, rows), F32),
            pltpu.VMEM((HEADS, 1, rows), F32),
            pltpu.VMEM((width, rows), BF),
            pltpu.SemaphoreType.DMA((2, 4, 4)),
            pltpu.SemaphoreType.DMA((2, 4, 4)),
            pltpu.SemaphoreType.DMA((2,)),
            pltpu.SemaphoreType.DMA((6, 6)),
        ],
        compiler_params=pltpu.CompilerParams(
            collective_id=0, has_side_effects=True, vmem_limit_bytes=58 * MIB
        ),
        name="gather_attend",
    )(tokens, lens, gain, shift, w, bq, bv)


def three_parts(values):
    high = values.astype(BF).astype(F32)
    middle = (values - high).astype(BF).astype(F32)
    return high, middle, values - high - middle


def add_parts(total, other, parts=1, step=32):
    depth = total.shape[-2] // step

    def some(k, carry):
        at = (pl.ds(pl.multiple_of(k % depth * step, step), step),)
        if len(total.shape) == 3:
            at = (k // depth, *at)
        total[at] = total[at] + other[at]
        return carry

    lax.fori_loop(0, parts * depth, some, 0)


def dp_place():
    dp = lax.axis_index("dp")
    core, x, y = dp % 2, (dp // 2) % 2, dp // 4
    return (core, x, y), (dp + 1 - 2 * core, dp + 2 - 4 * x, dp + 4 - 8 * y)


class DpSum:
    def __init__(self, first, stage, one, two, three, send, recv):
        self.first, self.stage, self.one, self.two, self.three = first, stage, one, two, three
        (self.core, self.x, self.y), (self.to_core, self.to_x, self.to_y) = dp_place()
        self.send, self.recv = send, recv
        self.step = min(32, three.shape[-2])

    def copy(self, phase):
        x_first = self.first == "x"
        if phase == 0:
            src, dst, to = self.stage.at[:, :, 1 - self.core], self.one, self.to_core
        elif phase == 1:
            src = self.one.at[:, 1 - self.x] if x_first else self.one.at[1 - self.y]
            dst, to = self.two, self.to_x if x_first else self.to_y
        else:
            src = self.two.at[1 - self.y] if x_first else self.two.at[1 - self.x]
            dst, to = self.three, self.to_y if x_first else self.to_x
        return pltpu.make_async_remote_copy(
            src_ref=src, dst_ref=dst, send_sem=self.send.at[phase], recv_sem=self.recv.at[phase],
            device_id={"dp": to}, device_id_type=MESH,
        )

    def start(self, phase):
        self.copy(phase).start()

    def finish(self, phase):
        self.copy(phase).wait_recv()
        x_first = self.first == "x"
        if phase == 0:
            for y in range(2):
                add_parts(self.one.at[y], self.stage.at[y, :, self.core], 2, self.step)
        elif phase == 1:
            add_parts(self.two, self.one.at[:, self.x] if x_first else self.one.at[self.y], 2, self.step)
        else:
            add_parts(self.three, self.two.at[self.y] if x_first else self.two.at[self.x], 1, self.step)

    def wait_sends(self, phases):
        for phase in phases:
            self.copy(phase).wait_send()


class SeqSum:
    def __init__(self, part, total, swapped, send, recv):
        self.part, self.total, self.swapped = part, total, swapped
        self.send, self.recv = send, recv
        me = lax.axis_index("seq")
        self.end = (me == 0) | (me == 3)
        self.partner = jnp.where(me < 2, 1 - me, 5 - me)
        self.other = 3 - me

    def copy(self, phase):
        src, dst, to = (
            (self.part, self.total, self.partner),
            (self.part, self.swapped, self.other),
            (self.total, self.total, self.partner),
        )[phase]
        return pltpu.make_async_remote_copy(
            src_ref=src, dst_ref=dst, send_sem=self.send.at[phase], recv_sem=self.recv.at[phase],
            device_id={"seq": to}, device_id_type=MESH,
        )

    def ends_send(self):
        @pl.when(self.end)
        def _():
            self.copy(0).start()

    def middles_swap(self):
        @pl.when(~self.end)
        def _():
            self.copy(0).wait_recv()
            add_parts(self.part, self.total, 1, min(32, self.part.shape[-2]))
            self.copy(1).start()

    def middles_send(self):
        @pl.when(~self.end)
        def _():
            self.copy(1).wait_recv()
            depth = min(32, self.part.shape[-2])

            def some(k, carry):
                at = pl.ds(pl.multiple_of(k * depth, depth), depth)
                self.total[at] = self.part[at] + self.swapped[at]
                return carry

            lax.fori_loop(0, self.part.shape[-2] // depth, some, 0)
            self.copy(2).start()

    def finish(self):
        @pl.when(self.end)
        def _():
            self.copy(0).wait_send()
            self.copy(2).wait_recv()

        @pl.when(~self.end)
        def _():
            self.copy(1).wait_send()
            self.copy(2).wait_send()


CHUNKS = 3
GROUPS = 8


def chunk_columns(ff, c, d):
    return (ff // GROUPS) * d + 128 * c


def place_of(d):
    return d // 4, (d // 2) % 2, d % 2


def layer_back_kernel(fast, *refs):
    (
        kn_h, vn_h, kt_h, xt_h, qn_h, qt_h, wp_h, att_h, tok_h, cot_h, w_out_h, w_up_h, w_down_h,
        lse, lens, gain_one, b_out, gain, shift, b_up, b_down, *refs,
    ) = refs
    layer_o, tok_o, *refs = refs
    if fast:
        fin_d_o, fin_u_o, fin_o_o, fin_q_o, fin_v_o, *refs = refs
    else:
        gd_o, gu_o, go_o, gq_o, stage_v_o, *refs = refs
    (
        stage_d, stage_u, stage_o, stage_v, sums, vec_up, d_att, dta, d_mid, rx, kn, vn, kt, qta, qn,
        ff_sem, in_sem, load_sem, out_sem, dsend, drecv, *refs,
    ) = refs
    rows, width = tok_h.shape
    ff = w_up_h.shape[1]
    span = GROUPS * 128
    part_w = width // GROUPS
    seq = lax.axis_size("seq")
    me = lax.axis_index("seq")
    has_left, has_right = me > 0, me < seq - 1
    at_end = (me == 0) | (me == seq - 1)
    half_rows = rows // 2

    barrier = pltpu.get_barrier_semaphore()

    @pl.when(has_left)
    def _():
        pl.semaphore_signal(barrier, inc=1, device_id={"seq": me - 1}, device_id_type=MESH)

    @pl.when(has_right)
    def _():
        pl.semaphore_signal(barrier, inc=1, device_id={"seq": me + 1}, device_id_type=MESH)

    if fast:
        for to in dp_place()[1]:
            pl.semaphore_signal(barrier, inc=1, device_id={"dp": to}, device_id_type=MESH)
    greeted = 3 if fast else 0

    def meet():
        @pl.when(at_end)
        def _():
            pl.semaphore_wait(barrier, greeted + 1)

        @pl.when(~at_end)
        def _():
            pl.semaphore_wait(barrier, greeted + 2)

    if fast:
        (
            one_d, one_u, one_o, two_d, two_u, two_o, three_d, three_u, three_o,
            one_q, two_q, three_q, one_v, two_v, three_v,
            zx_d, fin_d, zx_u, fin_u, zx_o, fin_o, zx_q, fin_q, zx_v, fin_v,
            psend, precv, zsend, zrecv,
        ) = refs
        rs_d = [
            DpSum("x", stage_d.at[c], one_d.at[c], two_d.at[c], three_d.at[c], psend.at[c], precv.at[c])
            for c in range(CHUNKS)
        ]
        rs_u = [
            DpSum("y", stage_u.at[c], one_u.at[c], two_u.at[c], three_u.at[c], psend.at[3 + c], precv.at[3 + c])
            for c in range(CHUNKS)
        ]
        rs_o = DpSum("x", stage_o, one_o, two_o, three_o, psend.at[6], precv.at[6])
        rs_v = DpSum("x", stage_v, one_v, two_v, three_v, psend.at[7], precv.at[7])

        def couple(c):
            found = []
            for k in range(2):
                tile = 2 * c + k
                staged = stage_u.at[c, :, :, :, :, pl.ds(384 * k, 384)]
                found.append(
                    DpSum(
                        "xy"[k], staged, one_q.at[tile], two_q.at[tile], three_q.at[tile],
                        psend.at[8 + tile], precv.at[8 + tile],
                    )
                )
            return found

        ar_d = [
            SeqSum(three_d.at[c], fin_d.at[c], zx_d.at[c], zsend.at[c], zrecv.at[c]) for c in range(CHUNKS)
        ]
        ar_u = [
            SeqSum(three_u.at[c], fin_u.at[c], zx_u.at[c], zsend.at[3 + c], zrecv.at[3 + c])
            for c in range(CHUNKS)
        ]
        ar_o = SeqSum(three_o, fin_o, zx_o, zsend.at[6], zrecv.at[6])
        ar_v = SeqSum(three_v, fin_v, zx_v, zsend.at[7], zrecv.at[7])
        ar_q = [
            SeqSum(three_q.at[c], fin_q.at[c], zx_q.at[c], zsend.at[8 + c], zrecv.at[8 + c])
            for c in range(PAIRS)
        ]

    def turn(*found):
        for unit_sum in found:
            unit_sum.finish(1)
            unit_sum.start(2)

    def close(*found):
        for unit_sum in found:
            unit_sum.finish(2)

    def per_row(ref):
        return ref[...].reshape(1, -1)

    stage_v[...] = jnp.zeros_like(stage_v)
    sums[...] = jnp.zeros_like(sums)

    def block_at(step):
        b0 = jnp.where(me < 2, seq - 1, 0)
        b1 = jnp.where(me < 2, seq - 2, 1)
        b2 = jnp.where(me == 0, 1, jnp.where(me == 1, 0, jnp.where(me == 2, 3, 2)))
        return jnp.where(step == 0, b0, jnp.where(step == 1, b1, jnp.where(step == 2, b2, me)))

    def loads(step):
        block, slot = block_at(step), step % 2
        return [
            pltpu.make_async_copy(kn_h.at[block], kn.at[slot], in_sem.at[slot, 0]),
            pltpu.make_async_copy(vn_h.at[block], vn.at[slot], in_sem.at[slot, 1]),
            pltpu.make_async_copy(kt_h.at[block], kt.at[slot], in_sem.at[slot, 2]),
        ]

    fills = [pltpu.make_async_copy(qn_h, qn, load_sem.at[HEADS])]
    for h in range(HEADS):
        own = pl.ds(64 * (h % 2), 64)
        fills.append(pltpu.make_async_copy(qt_h.at[h // 2, own], qta.at[h, own], load_sem.at[h]))

    def feed_forward(tok, att_t, cot, w_out, wu, wd, d_norm, bias):
        first = [
            pltpu.make_async_copy(src, dst, ff_sem.at[2, k // GROUPS, k % GROUPS])
            for k, (src, dst) in enumerate(((att_h, att_t), (w_out_h, w_out), (tok_h, tok), (cot_h, cot)))
        ]

        def weights(c):
            found = []
            for d in range(GROUPS):
                at = pl.ds(chunk_columns(ff, c, d), 128)
                to = pl.ds(128 * d, 128)
                found.append(pltpu.make_async_copy(w_up_h.at[:, at], wu.at[c % 2, :, to], ff_sem.at[0, c, d]))
                found.append(pltpu.make_async_copy(w_down_h.at[at], wd.at[c % 2, to], ff_sem.at[1, c, d]))
            return found

        for copy in (*first[:3], *weights(0), *first[3:], *weights(1), *loads(0), *fills):
            copy.start()
        codes = query_codes(lens, me, rows)[:16]
        row16 = lax.broadcasted_iota(jnp.int32, (16, rows), 0)
        for h in range(HEADS):
            other = 64 * (1 - h % 2)
            extra = codes
            for r, part in enumerate(three_parts(-lse[h : h + 1])):
                extra = jnp.where(row16 == 8 + r, part, extra)
            qta[h, other : other + 16] = extra.astype(BF)
            qta[h, other + 16 : other + 64] = jnp.zeros((48, rows), BF)
        meet()
        for copy in first[:3]:
            copy.wait()
        middle = tok[...].astype(F32) + mm(att_t[...].T, w_out[...]) + per_row(b_out)
        average = jnp.mean(middle, axis=-1, keepdims=True)
        centred = middle - average
        scale = lax.rsqrt(jnp.mean(centred * centred, axis=-1, keepdims=True) + EPS)
        unit = centred * scale
        normed = (unit * per_row(gain) + per_row(shift)).astype(BF)
        normed_t = normed.T
        for copy in first[3:]:
            copy.wait()
        d_out = cot[...]
        for c in range(CHUNKS):
            for d in range(GROUPS):
                at = chunk_columns(ff, c, d)
                bias[c : c + 1, 128 * d : 128 * (d + 1)] = b_up[at : at + 128].reshape(1, 128)
        d_mid[...] = middle + per_row(b_down)
        d_norm[...] = jnp.zeros_like(d_norm)

        def one_chunk(c, carry):
            for copy in weights(c):
                copy.wait()
            slot = c % 2
            upper = mm(normed, wu[slot]) + bias[pl.ds(c, 1)]
            cdf = 0.5 * (1.0 + lax.erf(upper * ROOT_HALF))
            hidden = (upper * cdf).astype(BF)
            slope = cdf + upper * (jnp.exp(-0.5 * upper * upper) * 0.3989422804014327)
            d_upper = (mm_nt(d_out, wd[slot]) * slope).astype(BF)
            vec_up[pl.ds(c, 1)] = jnp.sum(d_upper.astype(F32), axis=0, keepdims=True)
            if fast:

                @pl.when(c == 1)
                def _():
                    for unit_sum in (rs_d[0], rs_u[0]):
                        unit_sum.finish(0)
                        unit_sum.start(1)

                @pl.when(c == 2)
                def _():
                    for unit_sum in (rs_d[1], rs_u[1]):
                        unit_sum.finish(0)

            g_down = mm(hidden.T, d_out).astype(BF)
            g_up = mm(normed_t, d_upper).astype(BF)
            for d in range(GROUPS):
                stage_d[(c, *place_of(d))] = g_down[128 * d : 128 * (d + 1)]
                stage_u[(c, *place_of(d))] = g_up[96 * d : 96 * (d + 1)]
            if fast:
                for k in range(CHUNKS):

                    @pl.when(c == k)
                    def _():
                        rs_d[k].start(0)
                        rs_u[k].start(0)
                        if k == 2:
                            turn(rs_d[0], rs_u[0])
                            rs_d[1].start(1)
                            rs_u[1].start(1)

            d_mid[...] += mm(hidden, wd[slot])
            d_norm[...] += mm_nt(d_upper, wu[slot])

            @pl.when(c == 0)
            def _():
                for copy in weights(2):
                    copy.start()

            return carry

        lax.fori_loop(0, CHUNKS, one_chunk, 0)
        d_normed = d_norm[...]
        tok[...] = d_mid[...].astype(BF)
        keep_layer = pltpu.make_async_copy(tok, layer_o, out_sem.at[5])
        keep_layer.start()
        sums[7:8] = jnp.sum(d_out.astype(F32), axis=0, keepdims=True)
        sums[5:6] = jnp.sum(d_normed * unit, axis=0, keepdims=True)
        sums[6:7] = jnp.sum(d_normed, axis=0, keepdims=True)
        scaled = d_normed * per_row(gain)
        d_middle = d_out.astype(F32) + scale * (
            scaled
            - jnp.mean(scaled, axis=-1, keepdims=True)
            - unit * jnp.mean(scaled * unit, axis=-1, keepdims=True)
        )
        d_mid[...] = d_middle
        d_branch = d_middle.astype(BF)
        sums[4:5] = jnp.sum(d_branch.astype(F32), axis=0, keepdims=True)
        g_out = mm(att_t[...], d_branch).astype(BF)
        for d in range(GROUPS):
            stage_o[place_of(d)] = g_out[96 * d : 96 * (d + 1)]
        if fast:
            rs_o.start(0)
            close(rs_d[0], rs_u[0])
            ar_d[0].ends_send()
            ar_u[0].ends_send()
        d_attended = mm_nt(d_branch, w_out[...]).astype(BF)
        d_att[...] = d_attended
        turned = d_attended.T
        product = turned.astype(F32) * att_t[...].astype(F32)
        row16 = lax.broadcasted_iota(jnp.int32, (16, rows), 0)
        for h in range(HEADS):
            own, other = 64 * (h % 2), 64 * (1 - h % 2)
            dta[h, own : own + 64] = turned[64 * h : 64 * (h + 1)]
            delta = jnp.sum(product[64 * h : 64 * (h + 1)], axis=0, keepdims=True)
            extra = jnp.zeros((16, rows), F32)
            for r, part in enumerate(three_parts(-delta)):
                extra = jnp.where(row16 == r, part, extra)
            dta[h, other : other + 16] = extra.astype(BF)
            dta[h, other + 16 : other + 64] = jnp.zeros((48, rows), BF)
        if not fast:
            keep = [
                pltpu.make_async_copy(stage_d, gd_o, out_sem.at[0]),
                pltpu.make_async_copy(stage_u, gu_o, out_sem.at[1]),
                pltpu.make_async_copy(stage_o, go_o, out_sem.at[2]),
            ]
            for copy in keep:
                copy.start()
            for copy in keep:
                copy.wait()
        keep_layer.wait()

    pl.run_scoped(
        feed_forward,
        pltpu.VMEM((rows, width), BF),
        pltpu.VMEM((width, rows), BF),
        pltpu.VMEM((rows, width), BF),
        pltpu.VMEM((width, width), BF),
        pltpu.VMEM((2, width, span), BF),
        pltpu.VMEM((2, span, width), BF),
        pltpu.VMEM((rows, width), F32),
        pltpu.VMEM((8, span), F32),
    )

    def dx_stage(step, half):
        return stage_d.at[step // 2, step % 2, half]

    def dx_copy(way, step, block, half):
        return pltpu.make_async_remote_copy(
            src_ref=dx_stage(step, half), dst_ref=rx.at[block + way, half],
            send_sem=dsend.at[way, block, half], recv_sem=drecv.at[way, block, half],
            device_id={"seq": me - 1 if way == 0 else me + 1}, device_id_type=MESH,
        )

    def store_dx(step, half, value):
        for k in range(2):
            stage_d[step // 2, step % 2, half, k] = value[128 * k : 128 * (k + 1)]

    def relay_at(place, way, step, half):
        @pl.when(me == place)
        def _():
            block = block_at(step)
            dx_copy(way, step, block, half).wait_recv()
            add_parts(dx_stage(step, half), rx.at[block + way, half], 2)
            dx_copy(way, step, block, half).start()

    def relay_far(step, half):
        relay_at(1, 1, step, half)
        relay_at(2, 0, step, half)

    def relay_near(half):
        relay_at(1, 0, 2, half)
        relay_at(2, 1, 2, half)

    def send_dx(step, half):
        block = block_at(step)

        @pl.when(me == 0)
        def _():
            dx_copy(1, step, block, half).start()

        @pl.when(me == seq - 1)
        def _():
            dx_copy(0, step, block, half).start()

    def attention(xt, dqt, gk, gv, dk, dv, dq, wp, hot_ref):
        def load_x(step):
            return pltpu.make_async_copy(xt_h.at[block_at(step)], xt, in_sem.at[0, 3])

        load_wp = pltpu.make_async_copy(wp_h, wp, load_sem.at[HEADS + 1])
        for copy in (load_x(0), load_wp):
            copy.start()
        low, high = lane_halves()
        dqt[...] = jnp.zeros_like(dqt)
        lane = lax.broadcasted_iota(jnp.int32, (1, 128), 1)
        v_low = jnp.where(lane < 3, 1.0, 0.0).astype(BF)
        v_high = jnp.where((lane >= 64) & (lane < 67), 1.0, 0.0).astype(BF)
        if fast:
            for unit_sum in rs_d:
                unit_sum.wait_sends((0,))
        for copy in fills:
            copy.wait()

        def hooks(g):
            if not fast:
                return

            def at(when, action):
                @pl.when(g == when)
                def _():
                    action()

            def second():
                turn(rs_d[1], rs_u[1])
                for unit_sum in (rs_d[2], rs_u[2], rs_o):
                    unit_sum.finish(0)
                    unit_sum.start(1)

            at(6, lambda: (second(), ar_d[0].middles_swap(), ar_u[0].middles_swap()))
            at(12, lambda: (close(rs_d[1], rs_u[1]), ar_d[1].ends_send(), ar_u[1].ends_send()))
            at(14, lambda: relay_far(0, 0))
            at(16, lambda: (ar_d[0].middles_send(), ar_u[0].middles_send()))
            at(17, lambda: turn(rs_d[2], rs_u[2]))
            at(20, lambda: relay_far(0, 1))
            at(21, lambda: (turn(rs_o), close(rs_d[2], rs_u[2])))
            at(23, lambda: (close(rs_o), [unit.ends_send() for unit in (ar_d[2], ar_u[2], ar_o)]))

        def products(slot, i, part=slice(None)):
            at = pl.ds(pl.multiple_of(i * 128, 128), 128)
            keys, values = kn[slot, i, part], vn[slot, i, part]
            q_pair, d_pair = qn[i], d_att[:, at]
            hot = hot_ref[part]
            scores = [
                mm(keys * low + hot * high, qta[2 * i]),
                mm(keys * high + hot * low, qta[2 * i + 1]),
            ]
            slopes = [
                mm(values * low + v_high, dta[2 * i]),
                mm(values * high + v_low, dta[2 * i + 1]),
            ]
            d_keys = jnp.zeros((keys.shape[0], 128), F32)
            d_values = jnp.zeros((keys.shape[0], 128), F32)
            for j in range(2):
                h = 2 * i + j
                mask = low if j == 0 else high
                probs = jnp.exp(scores[j])
                d_scores = (probs * slopes[j]).astype(BF)
                d_values = d_values + mm(probs.astype(BF), d_pair * mask)
                d_keys = d_keys + mm(d_scores, q_pair * mask)
                dqt[h] += mm(kt[slot, i, 64 * j : 64 * (j + 1), part], d_scores)
            dk[part, at] = d_keys.astype(BF)
            dv[part, at] = d_values.astype(BF)

        def enter(step):
            for copy in loads(step):
                copy.wait()
            hot_ref[...] = key_codes(lens, block_at(step), rows)

        enter(0)
        for copy in loads(1):
            copy.start()

        def one_half(half, carry):
            part = pl.ds(pl.multiple_of(half * half_rows, half_rows), half_rows)

            def one_pair(i, carry):
                hooks(half * PAIRS + i)
                products(0, i, part)
                return carry

            lax.fori_loop(0, PAIRS, one_pair, 0)

            @pl.when(half == 0)
            def _():
                load_wp.wait()

            store_dx(0, half, (mm_nt(dk[part], wp[1]) + mm_nt(dv[part], wp[2])).astype(BF))
            send_dx(0, half)
            return carry

        lax.fori_loop(0, 2, one_half, 0)
        load_x(0).wait()
        gk[...] = mm(xt[...], dk[...])
        gv[...] = mm(xt[...], dv[...])
        load_x(1).start()
        sums[3:4] = jnp.sum(dv[...].astype(F32), axis=0, keepdims=True)

        def one_step(step, carry):
            slot = step % 2
            enter(step)
            for copy in loads(step + 1):
                copy.start()

            def one_pair(i, carry):
                hooks((step + 1) * PAIRS + i)
                products(slot, i)
                return carry

            lax.fori_loop(0, PAIRS, one_pair, 0)
            dx = (mm_nt(dk[...], wp[1]) + mm_nt(dv[...], wp[2])).astype(BF)
            for half in range(2):
                store_dx(step, half, dx[half * half_rows : (half + 1) * half_rows])
                send_dx(step, half)
            load_x(step).wait()
            gk[...] += mm(xt[...], dk[...])
            gv[...] += mm(xt[...], dv[...])
            load_x(step + 1).start()
            sums[3:4] += jnp.sum(dv[...].astype(F32), axis=0, keepdims=True)
            return carry

        lax.fori_loop(1, seq - 1, one_step, 0)

        last = (seq - 1) % 2
        enter(seq - 1)
        load_x(seq - 1).wait()
        lane_w = lax.broadcasted_iota(jnp.int32, (width, 128), 1)
        lo = lane_w < 64
        if fast:
            for unit_sum in rs_u:
                unit_sum.wait_sends((0,))

        def one_couple(c, carry):
            if fast:

                @pl.when(c == 0)
                def _():
                    relay_near(0)
                    ar_d[1].middles_swap()
                    ar_u[1].middles_swap()

                @pl.when(c == 1)
                def _():
                    relay_near(1)
                    relay_far(1, 0)

                @pl.when(c == 2)
                def _():
                    relay_far(1, 1)
                    ar_d[1].middles_send()
                    ar_u[1].middles_send()

                @pl.when(c >= 1)
                def _():
                    for unit in couple(c - 1):
                        unit.finish(0)
                        unit.start(1)

                @pl.when(c >= 2)
                def _():
                    turn(*couple(c - 2))


            def one_pair(k, carry):
                products(last, 2 * c + k)
                return carry

            lax.fori_loop(0, 2, one_pair, 0)
            at = pl.ds(pl.multiple_of(c * 256, 256), 256)
            turned = dqt[pl.ds(4 * c, 4)].reshape(256, rows) * (HEAD**-0.5)
            dq_part = turned.T.astype(BF)
            dq[:, at] = dq_part
            x_t = xt[...]
            gq_part = mm(x_t, dq_part)
            gk_part = gk[:, at] + mm(x_t, dk[:, at])
            gv_part = gv[:, at] + mm(x_t, dv[:, at])
            for k in range(2):
                cut = slice(128 * k, 128 * (k + 1))
                q_tile, v_tile = gq_part[:, cut], gv_part[:, cut]
                k_tile = pltpu.roll(gk_part[:, cut], 64, 1)
                tiles = jnp.where(lo, q_tile, k_tile), jnp.where(lo, v_tile, q_tile), jnp.where(lo, k_tile, v_tile)
                for j, tile in enumerate(tiles):
                    tile = tile.astype(BF)
                    to = slice(384 * k + 128 * j, 384 * k + 128 * (j + 1))
                    for d in range(GROUPS):
                        stage_u[(c, *place_of(d), slice(None), to)] = tile[part_w * d : part_w * (d + 1)]
            if fast:
                for unit in couple(c):
                    unit.start(0)
            return carry

        lax.fori_loop(0, PAIRS // 2, one_couple, 0)
        if not fast:
            for step in range(2):
                for half in range(2):
                    relay_far(step, half)
            relay_near(0)
            relay_near(1)
        dx_own = gk.at[pl.ds(0, rows)]
        dx_own[...] = mm_nt(dk[...], wp[1]) + mm_nt(dv[...], wp[2]) + mm_nt(dq[...], wp[0])
        sums[3:4] += jnp.sum(dv[...].astype(F32), axis=0, keepdims=True)
        sums[2:3] = jnp.sum(dq[...].astype(F32), axis=0, keepdims=True)
        load_tok = pltpu.make_async_copy(tok_h, dv, load_sem.at[HEADS + 2])
        load_tok.start()
        if fast:
            for unit in couple(2):
                unit.finish(0)
                unit.start(1)
            turn(*couple(1))
            close(*couple(0))
            ar_d[2].middles_swap()
            turn(*couple(2))
            ar_u[2].middles_swap()
            close(*couple(1), *couple(2))
            ar_o.middles_swap()
            for unit in ar_q:
                unit.ends_send()
            ar_d[2].middles_send()
            ar_u[2].middles_send()

        load_tok.wait()
        for way, there in ((0, has_right), (1, has_left)):
            @pl.when(there)
            def _():
                for half in range(2):
                    dx_copy(way, 0, me, half).wait_recv()

                def some(k, carry):
                    at = pl.ds(pl.multiple_of(k * 32, 32), 32)
                    piece = rx[me + way, k // 8, k // 4 % 2, pl.ds(pl.multiple_of(k % 4 * 32, 32), 32)]
                    dx_own[at] += piece.astype(F32)
                    return carry

                lax.fori_loop(0, rows // 32, some, 0)

        values = dv[...].astype(F32)
        centred = values - jnp.mean(values, axis=-1, keepdims=True)
        scale = lax.rsqrt(jnp.mean(centred * centred, axis=-1, keepdims=True) + EPS)
        unit_rows = centred * scale
        d_normed = dx_own[...]
        sums[0:1] = jnp.sum(d_normed * unit_rows, axis=0, keepdims=True)
        sums[1:2] = jnp.sum(d_normed, axis=0, keepdims=True)
        rows8 = sums[...]
        for d in range(GROUPS):
            y, x, core = place_of(d)
            stage_v[y, x, core, 0:8, 0:part_w] = rows8[:, part_w * d : part_w * (d + 1)]
            stage_v[y, x, core, 8 : 8 + CHUNKS] = vec_up[0:CHUNKS, 128 * d : 128 * (d + 1)]
        if fast:
            rs_v.start(0)
        if fast:
            ar_o.middles_send()
            ar_q[0].middles_swap()
        scaled = d_normed * per_row(gain_one)
        dk[...] = (
            d_mid[...]
            + scale
            * (
                scaled
                - jnp.mean(scaled, axis=-1, keepdims=True)
                - unit_rows * jnp.mean(scaled * unit_rows, axis=-1, keepdims=True)
            )
        ).astype(BF)
        keep = [pltpu.make_async_copy(dk, tok_o, out_sem.at[6])]
        keep[0].start()
        if fast:
            ar_q[1].middles_swap()
            rs_v.finish(0)
            rs_v.start(1)
            ar_q[2].middles_swap()
            ar_q[0].middles_send()
            rs_v.finish(1)
            rs_v.start(2)
            ar_q[3].middles_swap()
            ar_q[1].middles_send()
            rs_v.finish(2)
            ar_v.ends_send()
            ar_q[4].middles_swap()
            ar_q[2].middles_send()
            ar_q[5].middles_swap()
            ar_q[3].middles_send()
            ar_v.middles_swap()
            ar_q[4].middles_send()
            ar_q[5].middles_send()
            ar_v.middles_send()
            for unit in (*ar_d, *ar_u, ar_o, ar_v, *ar_q):
                unit.finish()
            done = ((fin_d, fin_d_o), (fin_u, fin_u_o), (fin_o, fin_o_o), (fin_q, fin_q_o), (fin_v, fin_v_o))
            for unit in (*rs_d, *rs_u):
                unit.wait_sends((1, 2))
            for unit in (rs_o, rs_v, *couple(0), *couple(1), *couple(2)):
                unit.wait_sends((0, 1, 2))
        else:
            done = ((stage_u, gq_o), (stage_v, stage_v_o))
        keep += [pltpu.make_async_copy(src, dst, out_sem.at[k]) for k, (src, dst) in enumerate(done)]
        for copy in keep[1:]:
            copy.start()
        for copy in keep:
            copy.wait()

        for place, first, second in ((0, 1, 1), (1, 1, 0), (2, 0, 1), (3, 0, 0)):
            @pl.when(me == place)
            def _():
                for step, way in enumerate((first, first, second)):
                    for half in range(2):
                        dx_copy(way, step, block_at(step), half).wait_send()

    pl.run_scoped(
        attention,
        pltpu.VMEM((width, rows), BF),
        pltpu.VMEM((HEADS, HEAD, rows), F32),
        pltpu.VMEM((width, width), F32),
        pltpu.VMEM((width, width), F32),
        pltpu.VMEM((rows, width), BF),
        pltpu.VMEM((rows, width), BF),
        pltpu.VMEM((rows, width), BF),
        pltpu.VMEM((3, width, width), BF),
        pltpu.VMEM((rows, 128), BF),
    )


def layer_back(fast, *args):
    kn, wp = args[0], args[6]
    seq, _, rows, _ = kn.shape
    width = wp.shape[1]
    span = GROUPS * 128
    part = width // GROUPS
    any_spec = pl.BlockSpec(memory_space=pl.ANY)
    vmem = pl.BlockSpec(memory_space=pltpu.VMEM)
    sds = jax.ShapeDtypeStruct
    cube = (2, 2, 2)
    outs = [sds((rows, width), BF), sds((rows, width), BF)]
    if fast:
        outs += [
            sds((CHUNKS, 128, width), BF), sds((CHUNKS, part, span), BF), sds((part, width), BF),
            sds((PAIRS, part, 384), BF), sds((16, 128), F32),
        ]
    else:
        outs += [
            sds((CHUNKS, *cube, 128, width), BF), sds((CHUNKS, *cube, part, span), BF), sds((*cube, part, width), BF),
            sds((CHUNKS, *cube, part, span), BF), sds((*cube, 16, 128), F32),
        ]
    scratch = [
        pltpu.VMEM((CHUNKS, *cube, 128, width), BF),
        pltpu.VMEM((CHUNKS, *cube, part, span), BF),
        pltpu.VMEM((*cube, part, width), BF),
        pltpu.VMEM((*cube, 16, 128), F32),
        pltpu.VMEM((8, width), F32),
        pltpu.VMEM((8, span), F32),
        pltpu.VMEM((rows, width), BF),
        pltpu.VMEM((HEADS, 128, rows), BF),
        pltpu.VMEM((rows, width), F32),
        pltpu.VMEM((seq + 1, 2, 2, 128, width), BF),
        pltpu.VMEM((2, PAIRS, rows, 128), BF),
        pltpu.VMEM((2, PAIRS, rows, 128), BF),
        pltpu.VMEM((2, PAIRS, 128, rows), BF),
        pltpu.VMEM((HEADS, 128, rows), BF),
        pltpu.VMEM((PAIRS, rows, 128), BF),
        pltpu.SemaphoreType.DMA((3, CHUNKS, GROUPS)),
        pltpu.SemaphoreType.DMA((2, 4)),
        pltpu.SemaphoreType.DMA((HEADS + 3,)),
        pltpu.SemaphoreType.DMA((7,)),
        pltpu.SemaphoreType.DMA((2, 4, 2)),
        pltpu.SemaphoreType.DMA((2, 4, 2)),
    ]
    if fast:
        d, u, o, q = (128, width), (part, span), (part, width), (part, 384)
        scratch += [
            pltpu.VMEM(shape, BF)
            for shape in (
                (CHUNKS, 2, 2, *d), (CHUNKS, 2, 2, *u), (2, 2, *o), (CHUNKS, 2, *d), (CHUNKS, 2, *u), (2, *o),
                (CHUNKS, *d), (CHUNKS, *u), o, (PAIRS, 2, 2, *q), (PAIRS, 2, *q), (PAIRS, *q),
            )
        ]
        scratch += [pltpu.VMEM((2, 2, 16, 128), F32), pltpu.VMEM((2, 16, 128), F32), pltpu.VMEM((16, 128), F32)]
        for shape in ((CHUNKS, *d), (CHUNKS, *u), o, (PAIRS, *q)):
            scratch += [pltpu.VMEM(shape, BF)] * 2
        scratch += [pltpu.VMEM((16, 128), F32)] * 2
        scratch += [pltpu.SemaphoreType.DMA((14, 3))] * 4
    return pl.pallas_call(
        partial(layer_back_kernel, fast),
        out_shape=outs,
        in_specs=[any_spec] * 13 + [vmem, pl.BlockSpec(memory_space=pltpu.SMEM)] + [vmem] * 6,
        out_specs=[any_spec] * len(outs),
        scratch_shapes=scratch,
        compiler_params=pltpu.CompilerParams(
            collective_id=1, has_side_effects=True, vmem_limit_bytes=62 * MIB
        ),
        name="layer_back",
    )(*args)


def unpack_kernel(fin_d, fin_u, fin_o, fin_q, fin_v, layer, grad, layer_o, grad_o, down_o, up_o, out_o, qkv_o, *refs):
    *vec_o, held, sem = refs
    inward = [pltpu.make_async_copy(src, held.at[k], sem.at[0, k]) for k, src in enumerate((layer, grad))]
    outward = [pltpu.make_async_copy(held.at[k], dst, sem.at[1, k]) for k, dst in enumerate((layer_o, grad_o))]
    for copy in inward:
        copy.start()
    chunks, _, _ = fin_d.shape
    part, span = fin_u.shape[1:]
    for c in range(chunks):
        down_o[128 * c : 128 * (c + 1)] = fin_d[c].astype(F32)
        for d in range(GROUPS):
            at = chunk_columns(up_o.shape[1], c, d)
            up_o[:, at : at + 128] = fin_u[c, :, 128 * d : 128 * (d + 1)].astype(F32)
    for k in range(2):
        inward[k].wait()
        outward[k].start()
    out_o[...] = fin_o[...].astype(F32)
    for i in range(PAIRS):
        qkv_o[:, 384 * i : 384 * (i + 1)] = fin_q[i].astype(F32)
    for r in range(8):
        vec_o[r][...] = fin_v[r : r + 1, :part].reshape(part)
    vec_o[8][...] = jnp.concatenate([fin_v[8 + c : 9 + c] for c in range(chunks)], axis=1).reshape(128 * chunks)
    for copy in outward:
        copy.wait()


def unpack(fin_d, fin_u, fin_o, fin_q, fin_v, layer, grad):
    vmem = pl.BlockSpec(memory_space=pltpu.VMEM)
    any_spec = pl.BlockSpec(memory_space=pl.ANY)
    chunks, _, width = fin_d.shape
    part, span = fin_u.shape[1:]
    sds = jax.ShapeDtypeStruct
    outs = [
        sds(layer.shape, BF), sds(grad.shape, BF),
        sds((128 * chunks, width), F32), sds((part, span * chunks), F32), sds((part, width), F32),
        sds((part, PAIRS * fin_q.shape[2]), F32),
    ]
    outs += [sds((part,), F32)] * 8 + [sds((128 * chunks,), F32)]
    return pl.pallas_call(
        unpack_kernel, out_shape=outs, in_specs=[vmem] * 5 + [any_spec] * 2,
        out_specs=[any_spec] * 2 + [vmem] * (len(outs) - 2),
        scratch_shapes=[pltpu.VMEM((2, *layer.shape), BF), pltpu.SemaphoreType.DMA((2, 2))], name="unpack",
    )(fin_d, fin_u, fin_o, fin_q, fin_v, layer, grad)


def local(
    tokens, cell_lengths, ln1_gain, ln1_shift, w_qkv, b_query, b_value, w_out, b_out,
    ln2_gain, ln2_shift, w_up, b_up, w_down, b_down, cotangent,
):
    bucket_count, local_slots, width = tokens.shape
    ff = w_up.shape[1]
    seq_count = lax.axis_size("seq")
    dp_count = lax.axis_size("dp")
    fast = dp_count == GROUPS
    rows = bucket_count * local_slots
    flat = tokens.reshape(rows, width)
    kn, vn, kt, xt, qn, qt, wp, att_t, lse = gather_attend(
        flat, cell_lengths, ln1_gain, ln1_shift, w_qkv, b_query, b_value, seq_count
    )
    layer_out, tokens_grad, *found = layer_back(
        fast, kn, vn, kt, xt, qn, qt, wp, att_t, flat, cotangent.reshape(rows, width), w_out, w_up, w_down,
        lse, cell_lengths, ln1_gain, b_out, ln2_gain, ln2_shift, b_up, b_down,
    )
    if fast:
        layer_out, tokens_grad, down, up, out, qkv, *vectors = unpack(*found, layer_out, tokens_grad)
    else:

        def summed(g):
            share = lax.psum_scatter(g, "dp", scatter_dimension=0, tiled=True)
            return lax.psum(share, "seq").astype(F32)

        g_down, g_up, g_out, g_qkv, packed = found
        g_qkv = g_qkv.reshape(CHUNKS, width, GROUPS * 128)[:, :, :768]
        g_qkv = jnp.moveaxis(g_qkv, 0, 1).reshape(width, 3 * width)
        g_down = jnp.moveaxis(g_down.reshape(CHUNKS, GROUPS, 128, width), 0, 1).reshape(ff, width)
        g_up = jnp.transpose(g_up.reshape(CHUNKS, width, GROUPS, 128), (1, 2, 0, 3)).reshape(width, ff)
        down, up, out, qkv = summed(g_down), summed(g_up), summed(g_out.reshape(width, width)), summed(g_qkv)
        packed = packed.reshape(GROUPS, 16, 128)
        vectors = [packed[:, r, : width // GROUPS].reshape(width) for r in range(8)]
        vectors.append(packed[:, 8 : 8 + CHUNKS].reshape(ff))
        together = jnp.concatenate([v.reshape(dp_count, -1) for v in vectors], axis=1)
        together = lax.psum(together, ("dp", "seq"))
        mine = lax.dynamic_index_in_dim(together, lax.axis_index("dp"), 0, keepdims=False)
        sizes = [v.shape[0] // dp_count for v in vectors]
        vectors = [mine[sum(sizes[:k]) : sum(sizes[: k + 1])] for k in range(len(sizes))]
    layer_out = layer_out.reshape(tokens.shape)
    tokens_grad = tokens_grad.reshape(tokens.shape)
    g1, s1, bq, bv, bo, g2, s2, bd, bu = vectors
    return layer_out, tokens_grad, g1, s1, qkv, bq, bv, out, bo, g2, s2, up, bu, down, bd


def solution(mesh):
    token_spec = P("dp", "seq", None)
    vector, matrix = P("dp"), P("dp", None)
    placed = (token_spec, P("dp", None)) + (P(),) * 13 + (token_spec,)
    return jax.shard_map(
        local,
        mesh=mesh,
        in_specs=placed,
        out_specs=(
            token_spec, token_spec, vector, vector, matrix, vector, vector, matrix, vector,
            vector, vector, matrix, vector, matrix, vector,
        ),
        check_vma=False,
    )
```

```python
from functools import partial

import jax
import jax.numpy as jnp
from jax import lax
from jax.experimental import pallas as pl
from jax.experimental.pallas import tpu as pltpu
from jax.sharding import PartitionSpec as P

HEADS = 12
HEAD = 64
PAIRS = 6
EPS = 1e-05
ROOT_HALF = 0.7071067811865476
BIG = 1e30
MESH = pl.DeviceIdType.MESH
F32 = jnp.float32
BF = jnp.bfloat16
MIB = 1024 * 1024


def normalize(values, gain, shift):
    average = jnp.mean(values, axis=-1, keepdims=True)
    centred = values - average
    variance = jnp.mean(centred * centred, axis=-1, keepdims=True)
    return centred * lax.rsqrt(variance + EPS) * gain + shift


def gelu_exact(values):
    return 0.5 * values * (1.0 + jax.scipy.special.erf(values * ROOT_HALF))


def mm(a, b):
    return jnp.dot(a, b, preferred_element_type=F32)


def mm_nt(a, b):
    return lax.dot_general(a, b, (((1,), (1,)), ((), ())), preferred_element_type=F32)


def cell_bounds(lens_ref, index):
    start = jnp.zeros(index.shape, jnp.int32)
    end = jnp.zeros(index.shape, jnp.int32)
    at = jnp.int32(0)
    for c in range(lens_ref.shape[1]):
        after = at + lens_ref[0, c]
        start = jnp.where(index == c, at, start)
        end = jnp.where(index == c, after, end)
        at = after
    return start, end


def key_codes(lens_ref, block, rows):
    lane = lax.broadcasted_iota(jnp.int32, (1, 128), 1) % 64
    start, end = cell_bounds(lens_ref, lane)
    ones = ((lane >= 8) & (lane < 11)).astype(F32)
    slot = lax.broadcasted_iota(jnp.int32, (rows, 128), 0) + block * rows
    hot = jnp.where((slot >= start) & (slot < end), 1.0, 0.0)
    return (hot + ones).astype(BF)


def query_codes(lens_ref, block, rows):
    cell = lax.broadcasted_iota(jnp.int32, (64, 1), 0)
    start, end = cell_bounds(lens_ref, cell)
    slot = lax.broadcasted_iota(jnp.int32, (64, rows), 1) + block * rows
    inside = (slot >= start) & (slot < end)
    return jnp.where(inside | (cell >= 8), 0.0, -BIG)


def lane_halves():
    lane = lax.broadcasted_iota(jnp.int32, (1, 128), 1)
    low = jnp.where(lane < 64, 1.0, 0.0).astype(BF)
    high = jnp.where(lane < 64, 0.0, 1.0).astype(BF)
    return low, high


def sort_weights(w_ref, wp):
    depth = w_ref.shape[0]
    lane = lax.broadcasted_iota(jnp.int32, (depth, 128), 1)
    low = lane < 64
    for i in range(PAIRS):
        t0, t1, t2 = (w_ref[:, 384 * i + 128 * j : 384 * i + 128 * (j + 1)].astype(F32) for j in range(3))
        at = slice(128 * i, 128 * (i + 1))
        wp[0, :, at] = jnp.where(low, t0, t1).astype(BF)
        wp[1, :, at] = pltpu.roll(jnp.where(low, t2, t0), 64, 1).astype(BF)
        wp[2, :, at] = jnp.where(low, t1, t2).astype(BF)


def gather_kernel(
    tok, lens, gain, shift, w_h, bq, bv,
    kn_o, vn_o, kt_o, xt_o, qn_o, qt_o, wp_o, att_o, lse_h,
    xr, w, wp, kn, vn, kt, xt, qn, qt, qta, vta, acc, top, att_t, lse_o, send, recv, in_sem, out_sem,
):
    rows, width = tok.shape
    span = rows // 2
    seq = lax.axis_size("seq")
    me = lax.axis_index("seq")
    has_left, has_right = me > 0, me < seq - 1
    at_end = (me == 0) | (me == seq - 1)

    barrier = pltpu.get_barrier_semaphore()

    @pl.when(has_left)
    def _():
        pl.semaphore_signal(barrier, inc=1, device_id={"seq": me - 1}, device_id_type=MESH)

    @pl.when(has_right)
    def _():
        pl.semaphore_signal(barrier, inc=1, device_id={"seq": me + 1}, device_id_type=MESH)

    own_tokens = pltpu.make_async_copy(tok, xr.at[me], in_sem.at[0])
    own_tokens.start()
    weights = pltpu.make_async_copy(w_h, w, in_sem.at[1])
    weights.start()

    @pl.when(at_end)
    def _():
        pl.semaphore_wait(barrier, 1)

    @pl.when(~at_end)
    def _():
        pl.semaphore_wait(barrier, 2)

    def copy(way, hop, quarter, block):
        at = pl.ds(quarter * (rows // 4), rows // 4)
        return pltpu.make_async_remote_copy(
            src_ref=tok.at[at] if hop == 0 else xr.at[block, at],
            dst_ref=xr.at[block, at],
            send_sem=send.at[way, hop, quarter],
            recv_sem=recv.at[way, hop, quarter],
            device_id={"seq": me - 1 if way == 0 else me + 1},
            device_id_type=MESH,
        )

    def can_send(way):
        return has_left if way == 0 else has_right

    def holds(way, hop):
        return me + hop < seq if way == 0 else me - hop >= 0

    def block_of(way, hop):
        return me + hop if way == 0 else me - hop

    for quarter in range(4):
        for way in range(2):
            @pl.when(can_send(way))
            def _():
                copy(way, 0, quarter, me).start()

    def normed(raw):
        return normalize(raw.astype(F32), gain[...].reshape(1, -1), shift[...].reshape(1, -1)).astype(BF)

    row16 = lax.broadcasted_iota(jnp.int32, (16, span), 0)
    for h in range(HEADS):
        vta[h, 64:] = jnp.where(row16 == 0, 1.0, 0.0).astype(BF)
    acc[...] = jnp.zeros_like(acc)
    top[...] = jnp.full_like(top, -3e38)
    codes = query_codes(lens, me, rows).astype(BF)
    low, high = lane_halves()
    own_tokens.wait()
    weights.wait()
    sort_weights(w, wp)
    keep_w = pltpu.make_async_copy(wp, wp_o, out_sem.at[4, 0])
    keep_w.start()
    q = ((mm(normed(xr[me]), wp[0]) + bq[...].reshape(1, -1)).astype(BF).astype(F32) * (HEAD**-0.5)).astype(BF)
    for i in range(PAIRS):
        pair = q[:, 128 * i : 128 * (i + 1)]
        qn[i] = pair
        turned = pair.T
        qt[i] = turned
        qta[2 * i, :64] = turned[:64]
        qta[2 * i, 64:] = codes
        qta[2 * i + 1, :64] = codes
        qta[2 * i + 1, 64:] = turned[64:]
    keep_q = pltpu.make_async_copy(qn, qn_o, out_sem.at[4, 1])
    keep_q.start()
    keep_qt = pltpu.make_async_copy(qt, qt_o, out_sem.at[4, 2])
    keep_qt.start()

    def keep_att(i):
        at = pl.ds(128 * i, 128)
        return pltpu.make_async_copy(att_t.at[at], att_o.at[at], out_sem.at[5, i])

    def keeps(step):
        block = block_at(step)
        return [
            pltpu.make_async_copy(src.at[block], dst.at[block], out_sem.at[step, k])
            for k, (src, dst) in enumerate(((kn, kn_o), (vn, vn_o), (kt, kt_o), (xt, xt_o)))
        ]

    def block_at(step):
        from_end = jnp.where(me == 0, step, seq - 1 - step)
        from_mid = jnp.where(step == 0, me, jnp.where(step == 1, me + 1, jnp.where(step == 2, me - 1, jnp.where(me == 1, seq - 1, 0))))
        return jnp.where(at_end, from_end, from_mid)

    def arrive(due, way, hop, quarter):
        @pl.when(due & holds(way, hop))
        def _():
            block = block_of(way, hop)
            copy(way, hop - 1, quarter, block).wait_recv()

            @pl.when(can_send(way))
            def _():
                copy(way, hop, quarter, block).start()

    def attend(step, part, span):
        block = block_at(step)
        at = pl.ds(pl.multiple_of(part * span, span), span)
        x = normed(xr[block, at])
        keys = mm(x, wp[1]).astype(BF)
        values = (mm(x, wp[2]) + bv[...].reshape(1, -1)).astype(BF)
        hot = key_codes(lens, block * (rows // span) + part, span)
        hot_low, hot_high = hot * low, hot * high
        xt[block, :, at] = x.T
        for i in range(PAIRS):
            cut = slice(128 * i, 128 * (i + 1))
            kn[block, i, at] = keys[:, cut]
            kt[block, i, :, at] = keys[:, cut].T
            vn[block, i, at] = values[:, cut]
            turned = values[:, cut].T
            vta[2 * i, :64, :span] = turned[:64]
            vta[2 * i + 1, :64, :span] = turned[64:]

        @pl.when(part == rows // span - 1)
        def _():
            for c in keeps(step):
                c.start()

        def one_pair(i, carry):
            pair = kn[block, i, at]
            scores = [
                mm(pair * low + hot_high, qta[2 * i]),
                mm(pair * high + hot_low, qta[2 * i + 1]),
            ]
            for j in range(2):
                h = 2 * i + j
                before = top[h]
                now = jnp.maximum(before, jnp.max(scores[j], axis=0, keepdims=True))
                raised = jnp.exp(scores[j] - now).astype(BF)
                top[h] = now
                acc[h] = acc[h] * jnp.exp(before - now) + mm(vta[h, :, :span], raised)
            return carry

        lax.fori_loop(0, PAIRS, one_pair, 0)

    def half_step(turn, carry):
        for hop in range(1, 3):
            for quarter in range(4):
                first = jnp.where(at_end, 2 * hop, 2 * hop if hop == 1 else -2)
                for way in range(2):
                    arrive(turn == first + quarter // 2, way, hop, quarter)
        attend(turn // 2, turn % 2, rows // 2)
        return carry

    def last_step(turn, carry):
        for hop in range(2, 4):
            for quarter in range(4):
                due = (turn == quarter) & (at_end if hop == 3 else ~at_end)
                for way in range(2):
                    arrive(due, way, hop, quarter)
        attend(seq - 1, turn, rows // 4)
        return carry

    lax.fori_loop(0, 2 * (seq - 1), half_step, 0)
    lax.fori_loop(0, 4, last_step, 0)

    for i in range(PAIRS):
        for j in range(2):
            h = 2 * i + j
            total = acc[h, 64:65]
            lse_o[h : h + 1] = top[h] + jnp.log(total)
            att_t[64 * h : 64 * (h + 1)] = (acc[h, :64] * (1.0 / total)).astype(BF)
        keep_att(i).start()
    lse_o[HEADS:] = jnp.zeros((16 - HEADS, rows), F32)
    keep_lse = pltpu.make_async_copy(lse_o, lse_h, out_sem.at[4, 4])
    keep_lse.start()

    for way in range(2):
        for hop in range(3):
            for quarter in range(4):
                @pl.when(can_send(way) & holds(way, hop))
                def _():
                    copy(way, hop, quarter, block_of(way, hop)).wait_send()

    keep_w.wait()
    keep_q.wait()
    keep_qt.wait()
    for i in range(PAIRS):
        keep_att(i).wait()
    keep_lse.wait()
    for step in range(4):
        for c in keeps(step):
            c.wait()


def gather_attend(tokens, lens, gain, shift, w, bq, bv, seq):
    rows, width = tokens.shape
    any_spec = pl.BlockSpec(memory_space=pl.ANY)
    vmem = pl.BlockSpec(memory_space=pltpu.VMEM)
    sds = jax.ShapeDtypeStruct
    outs = [
        sds((seq, PAIRS, rows, 128), BF),
        sds((seq, PAIRS, rows, 128), BF),
        sds((seq, PAIRS, 128, rows), BF),
        sds((seq, width, rows), BF),
        sds((PAIRS, rows, 128), BF),
        sds((PAIRS, 128, rows), BF),
        sds((3, width, width), BF),
        sds((width, rows), BF),
        sds((16, rows), F32),
    ]
    return pl.pallas_call(
        gather_kernel,
        out_shape=outs,
        in_specs=[any_spec, pl.BlockSpec(memory_space=pltpu.SMEM), vmem, vmem, any_spec, vmem, vmem],
        out_specs=[any_spec] * 9,
        scratch_shapes=[
            pltpu.VMEM((seq, rows, width), BF),
            pltpu.VMEM((width, 3 * width), BF),
            pltpu.VMEM((3, width, width), BF),
            pltpu.VMEM((seq, PAIRS, rows, 128), BF),
            pltpu.VMEM((seq, PAIRS, rows, 128), BF),
            pltpu.VMEM((seq, PAIRS, 128, rows), BF),
            pltpu.VMEM((seq, width, rows), BF),
            pltpu.VMEM((PAIRS, rows, 128), BF),
            pltpu.VMEM((PAIRS, 128, rows), BF),
            pltpu.VMEM((HEADS, 128, rows), BF),
            pltpu.VMEM((HEADS, 80, rows // 2), BF),
            pltpu.VMEM((HEADS, 80, rows), F32),
            pltpu.VMEM((HEADS, 1, rows), F32),
            pltpu.VMEM((width, rows), BF),
            pltpu.VMEM((16, rows), F32),
            pltpu.SemaphoreType.DMA((2, 4, 4)),
            pltpu.SemaphoreType.DMA((2, 4, 4)),
            pltpu.SemaphoreType.DMA((2,)),
            pltpu.SemaphoreType.DMA((6, 6)),
        ],
        compiler_params=pltpu.CompilerParams(
            collective_id=0, has_side_effects=True, vmem_limit_bytes=58 * MIB
        ),
        name="gather_attend",
    )(tokens, lens, gain, shift, w, bq, bv)


def three_parts(values):
    high = values.astype(BF).astype(F32)
    middle = (values - high).astype(BF).astype(F32)
    return high, middle, values - high - middle


def add_parts(total, other, parts=1, step=32):
    depth = total.shape[-2] // step

    def some(k, carry):
        at = (pl.ds(pl.multiple_of(k % depth * step, step), step),)
        if len(total.shape) == 3:
            at = (k // depth, *at)
        total[at] = total[at] + other[at]
        return carry

    lax.fori_loop(0, parts * depth, some, 0)


def dp_place():
    dp = lax.axis_index("dp")
    core, x, y = dp % 2, (dp // 2) % 2, dp // 4
    return (core, x, y), (dp + 1 - 2 * core, dp + 2 - 4 * x, dp + 4 - 8 * y)


class DpSum:
    def __init__(self, first, stage, one, two, three, send, recv):
        self.first, self.stage, self.one, self.two, self.three = first, stage, one, two, three
        (self.core, self.x, self.y), (self.to_core, self.to_x, self.to_y) = dp_place()
        self.send, self.recv = send, recv
        self.step = min(32, three.shape[-2])

    def copy(self, phase):
        x_first = self.first == "x"
        if phase == 0:
            src, dst, to = self.stage.at[:, :, 1 - self.core], self.one, self.to_core
        elif phase == 1:
            src = self.one.at[:, 1 - self.x] if x_first else self.one.at[1 - self.y]
            dst, to = self.two, self.to_x if x_first else self.to_y
        else:
            src = self.two.at[1 - self.y] if x_first else self.two.at[1 - self.x]
            dst, to = self.three, self.to_y if x_first else self.to_x
        return pltpu.make_async_remote_copy(
            src_ref=src, dst_ref=dst, send_sem=self.send.at[phase], recv_sem=self.recv.at[phase],
            device_id={"dp": to}, device_id_type=MESH,
        )

    def start(self, phase):
        self.copy(phase).start()

    def finish(self, phase):
        self.copy(phase).wait_recv()
        x_first = self.first == "x"
        if phase == 0:
            for y in range(2):
                add_parts(self.one.at[y], self.stage.at[y, :, self.core], 2, self.step)
        elif phase == 1:
            add_parts(self.two, self.one.at[:, self.x] if x_first else self.one.at[self.y], 2, self.step)
        else:
            add_parts(self.three, self.two.at[self.y] if x_first else self.two.at[self.x], 1, self.step)

    def wait_sends(self, phases):
        for phase in phases:
            self.copy(phase).wait_send()


class SeqSum:
    def __init__(self, part, total, swapped, send, recv):
        self.part, self.total, self.swapped = part, total, swapped
        self.send, self.recv = send, recv
        me = lax.axis_index("seq")
        self.end = (me == 0) | (me == 3)
        self.partner = jnp.where(me < 2, 1 - me, 5 - me)
        self.other = 3 - me

    def copy(self, phase):
        src, dst, to = (
            (self.part, self.total, self.partner),
            (self.part, self.swapped, self.other),
            (self.total, self.total, self.partner),
        )[phase]
        return pltpu.make_async_remote_copy(
            src_ref=src, dst_ref=dst, send_sem=self.send.at[phase], recv_sem=self.recv.at[phase],
            device_id={"seq": to}, device_id_type=MESH,
        )

    def ends_send(self):
        @pl.when(self.end)
        def _():
            self.copy(0).start()

    def middles_swap(self):
        @pl.when(~self.end)
        def _():
            self.copy(0).wait_recv()
            add_parts(self.part, self.total, 1, min(32, self.part.shape[-2]))
            self.copy(1).start()

    def middles_send(self):
        @pl.when(~self.end)
        def _():
            self.copy(1).wait_recv()
            depth = min(32, self.part.shape[-2])

            def some(k, carry):
                at = pl.ds(pl.multiple_of(k * depth, depth), depth)
                self.total[at] = self.part[at] + self.swapped[at]
                return carry

            lax.fori_loop(0, self.part.shape[-2] // depth, some, 0)
            self.copy(2).start()

    def finish(self):
        @pl.when(self.end)
        def _():
            self.copy(0).wait_send()
            self.copy(2).wait_recv()

        @pl.when(~self.end)
        def _():
            self.copy(1).wait_send()
            self.copy(2).wait_send()


CHUNKS = 3
GROUPS = 8


def chunk_columns(ff, c, d):
    return (ff // GROUPS) * d + 128 * c


def place_of(d):
    return d // 4, (d // 2) % 2, d % 2


def layer_back_kernel(fast, *refs):
    (
        kn_h, vn_h, kt_h, xt_h, qn_h, qt_h, wp_h, att_h, tok_h, cot_h, w_out_h, w_up_h, w_down_h,
        lse, lens, gain_one, b_out, gain, shift, b_up, b_down, *refs,
    ) = refs
    layer_o, tok_o, *refs = refs
    if fast:
        fin_d_o, fin_u_o, fin_o_o, fin_q_o, fin_v_o, *refs = refs
    else:
        gd_o, gu_o, go_o, gq_o, stage_v_o, *refs = refs
    (
        stage_d, stage_u, stage_o, stage_v, sums, vec_up, d_att, dta, d_mid, rx, kn, vn, kt, qta, qn,
        ff_sem, in_sem, load_sem, out_sem, dsend, drecv, *refs,
    ) = refs
    rows, width = tok_h.shape
    ff = w_up_h.shape[1]
    span = GROUPS * 128
    part_w = width // GROUPS
    seq = lax.axis_size("seq")
    me = lax.axis_index("seq")
    has_left, has_right = me > 0, me < seq - 1
    at_end = (me == 0) | (me == seq - 1)
    half_rows = rows // 2

    barrier = pltpu.get_barrier_semaphore()

    @pl.when(has_left)
    def _():
        pl.semaphore_signal(barrier, inc=1, device_id={"seq": me - 1}, device_id_type=MESH)

    @pl.when(has_right)
    def _():
        pl.semaphore_signal(barrier, inc=1, device_id={"seq": me + 1}, device_id_type=MESH)

    if fast:
        for to in dp_place()[1]:
            pl.semaphore_signal(barrier, inc=1, device_id={"dp": to}, device_id_type=MESH)
    greeted = 3 if fast else 0

    def meet():
        @pl.when(at_end)
        def _():
            pl.semaphore_wait(barrier, greeted + 1)

        @pl.when(~at_end)
        def _():
            pl.semaphore_wait(barrier, greeted + 2)

    if fast:
        (
            one_d, one_u, one_o, two_d, two_u, two_o, three_d, three_u, three_o,
            one_q, two_q, three_q, one_v, two_v, three_v,
            zx_d, fin_d, zx_u, fin_u, zx_o, fin_o, zx_q, fin_q, zx_v, fin_v,
            psend, precv, zsend, zrecv,
        ) = refs
        rs_d = [
            DpSum("x", stage_d.at[c], one_d.at[c], two_d.at[c], three_d.at[c], psend.at[c], precv.at[c])
            for c in range(CHUNKS)
        ]
        rs_u = [
            DpSum("y", stage_u.at[c], one_u.at[c], two_u.at[c], three_u.at[c], psend.at[3 + c], precv.at[3 + c])
            for c in range(CHUNKS)
        ]
        rs_o = DpSum("x", stage_o, one_o, two_o, three_o, psend.at[6], precv.at[6])
        rs_v = DpSum("x", stage_v, one_v, two_v, three_v, psend.at[7], precv.at[7])

        def couple(c):
            found = []
            for k in range(2):
                tile = 2 * c + k
                staged = stage_u.at[c, :, :, :, :, pl.ds(384 * k, 384)]
                found.append(
                    DpSum(
                        "xy"[k], staged, one_q.at[tile], two_q.at[tile], three_q.at[tile],
                        psend.at[8 + tile], precv.at[8 + tile],
                    )
                )
            return found

        ar_d = [
            SeqSum(three_d.at[c], fin_d.at[c], zx_d.at[c], zsend.at[c], zrecv.at[c]) for c in range(CHUNKS)
        ]
        ar_u = [
            SeqSum(three_u.at[c], fin_u.at[c], zx_u.at[c], zsend.at[3 + c], zrecv.at[3 + c])
            for c in range(CHUNKS)
        ]
        ar_o = SeqSum(three_o, fin_o, zx_o, zsend.at[6], zrecv.at[6])
        ar_v = SeqSum(three_v, fin_v, zx_v, zsend.at[7], zrecv.at[7])
        ar_q = [
            SeqSum(three_q.at[c], fin_q.at[c], zx_q.at[c], zsend.at[8 + c], zrecv.at[8 + c])
            for c in range(PAIRS)
        ]

    def turn(*found):
        for unit_sum in found:
            unit_sum.finish(1)
            unit_sum.start(2)

    def close(*found):
        for unit_sum in found:
            unit_sum.finish(2)

    def per_row(ref):
        return ref[...].reshape(1, -1)

    stage_v[...] = jnp.zeros_like(stage_v)
    sums[...] = jnp.zeros_like(sums)

    def block_at(step):
        b0 = jnp.where(me < 2, seq - 1, 0)
        b1 = jnp.where(me < 2, seq - 2, 1)
        b2 = jnp.where(me == 0, 1, jnp.where(me == 1, 0, jnp.where(me == 2, 3, 2)))
        return jnp.where(step == 0, b0, jnp.where(step == 1, b1, jnp.where(step == 2, b2, me)))

    def loads(step):
        block, slot = block_at(step), step % 2
        return [
            pltpu.make_async_copy(kn_h.at[block], kn.at[slot], in_sem.at[slot, 0]),
            pltpu.make_async_copy(vn_h.at[block], vn.at[slot], in_sem.at[slot, 1]),
            pltpu.make_async_copy(kt_h.at[block], kt.at[slot], in_sem.at[slot, 2]),
        ]

    fills = [pltpu.make_async_copy(qn_h, qn, load_sem.at[HEADS])]
    for h in range(HEADS):
        own = pl.ds(64 * (h % 2), 64)
        fills.append(pltpu.make_async_copy(qt_h.at[h // 2, own], qta.at[h, own], load_sem.at[h]))

    def feed_forward(tok, att_t, cot, w_out, wu, wd, d_norm, bias):
        first = [
            pltpu.make_async_copy(src, dst, ff_sem.at[2, k // GROUPS, k % GROUPS])
            for k, (src, dst) in enumerate(((att_h, att_t), (w_out_h, w_out), (tok_h, tok), (cot_h, cot)))
        ]

        def weights(c):
            found = []
            for d in range(GROUPS):
                at = pl.ds(chunk_columns(ff, c, d), 128)
                to = pl.ds(128 * d, 128)
                found.append(pltpu.make_async_copy(w_up_h.at[:, at], wu.at[c % 2, :, to], ff_sem.at[0, c, d]))
                found.append(pltpu.make_async_copy(w_down_h.at[at], wd.at[c % 2, to], ff_sem.at[1, c, d]))
            return found

        for copy in (*first[:3], *weights(0), *first[3:], *weights(1), *loads(0), *fills):
            copy.start()
        codes = query_codes(lens, me, rows)[:16]
        row16 = lax.broadcasted_iota(jnp.int32, (16, rows), 0)
        for h in range(HEADS):
            other = 64 * (1 - h % 2)
            extra = codes
            for r, part in enumerate(three_parts(-lse[h : h + 1])):
                extra = jnp.where(row16 == 8 + r, part, extra)
            qta[h, other : other + 16] = extra.astype(BF)
            qta[h, other + 16 : other + 64] = jnp.zeros((48, rows), BF)
        meet()
        for copy in first[:3]:
            copy.wait()
        middle = tok[...].astype(F32) + mm(att_t[...].T, w_out[...]) + per_row(b_out)
        average = jnp.mean(middle, axis=-1, keepdims=True)
        centred = middle - average
        scale = lax.rsqrt(jnp.mean(centred * centred, axis=-1, keepdims=True) + EPS)
        unit = centred * scale
        normed = (unit * per_row(gain) + per_row(shift)).astype(BF)
        normed_t = normed.T
        for copy in first[3:]:
            copy.wait()
        d_out = cot[...]
        for c in range(CHUNKS):
            for d in range(GROUPS):
                at = chunk_columns(ff, c, d)
                bias[c : c + 1, 128 * d : 128 * (d + 1)] = b_up[at : at + 128].reshape(1, 128)
        d_mid[...] = middle + per_row(b_down)
        d_norm[...] = jnp.zeros_like(d_norm)

        def one_chunk(c, carry):
            for copy in weights(c):
                copy.wait()
            slot = c % 2
            upper = mm(normed, wu[slot]) + bias[pl.ds(c, 1)]
            cdf = 0.5 * (1.0 + lax.erf(upper * ROOT_HALF))
            hidden = (upper * cdf).astype(BF)
            slope = cdf + upper * (jnp.exp(-0.5 * upper * upper) * 0.3989422804014327)
            d_upper = (mm_nt(d_out, wd[slot]) * slope).astype(BF)
            vec_up[pl.ds(c, 1)] = jnp.sum(d_upper.astype(F32), axis=0, keepdims=True)
            if fast:

                @pl.when(c == 1)
                def _():
                    for unit_sum in (rs_d[0], rs_u[0]):
                        unit_sum.finish(0)
                        unit_sum.start(1)

                @pl.when(c == 2)
                def _():
                    for unit_sum in (rs_d[1], rs_u[1]):
                        unit_sum.finish(0)

            g_down = mm(hidden.T, d_out).astype(BF)
            g_up = mm(normed_t, d_upper).astype(BF)
            for d in range(GROUPS):
                stage_d[(c, *place_of(d))] = g_down[128 * d : 128 * (d + 1)]
                stage_u[(c, *place_of(d))] = g_up[96 * d : 96 * (d + 1)]
            if fast:
                for k in range(CHUNKS):

                    @pl.when(c == k)
                    def _():
                        rs_d[k].start(0)
                        rs_u[k].start(0)
                        if k == 2:
                            turn(rs_d[0], rs_u[0])
                            rs_d[1].start(1)
                            rs_u[1].start(1)

            d_mid[...] += mm(hidden, wd[slot])
            d_norm[...] += mm_nt(d_upper, wu[slot])

            @pl.when(c == 0)
            def _():
                for copy in weights(2):
                    copy.start()

            return carry

        lax.fori_loop(0, CHUNKS, one_chunk, 0)
        d_normed = d_norm[...]
        tok[...] = d_mid[...].astype(BF)
        keep_layer = pltpu.make_async_copy(tok, layer_o, out_sem.at[5])
        keep_layer.start()
        sums[7:8] = jnp.sum(d_out.astype(F32), axis=0, keepdims=True)
        sums[5:6] = jnp.sum(d_normed * unit, axis=0, keepdims=True)
        sums[6:7] = jnp.sum(d_normed, axis=0, keepdims=True)
        scaled = d_normed * per_row(gain)
        d_middle = d_out.astype(F32) + scale * (
            scaled
            - jnp.mean(scaled, axis=-1, keepdims=True)
            - unit * jnp.mean(scaled * unit, axis=-1, keepdims=True)
        )
        d_mid[...] = d_middle
        d_branch = d_middle.astype(BF)
        sums[4:5] = jnp.sum(d_branch.astype(F32), axis=0, keepdims=True)
        g_out = mm(att_t[...], d_branch).astype(BF)
        for d in range(GROUPS):
            stage_o[place_of(d)] = g_out[96 * d : 96 * (d + 1)]
        if fast:
            rs_o.start(0)
            close(rs_d[0], rs_u[0])
            ar_d[0].ends_send()
            ar_u[0].ends_send()
        d_attended = mm_nt(d_branch, w_out[...]).astype(BF)
        d_att[...] = d_attended
        turned = d_attended.T
        product = turned.astype(F32) * att_t[...].astype(F32)
        row16 = lax.broadcasted_iota(jnp.int32, (16, rows), 0)
        for h in range(HEADS):
            own, other = 64 * (h % 2), 64 * (1 - h % 2)
            dta[h, own : own + 64] = turned[64 * h : 64 * (h + 1)]
            delta = jnp.sum(product[64 * h : 64 * (h + 1)], axis=0, keepdims=True)
            extra = jnp.zeros((16, rows), F32)
            for r, part in enumerate(three_parts(-delta)):
                extra = jnp.where(row16 == r, part, extra)
            dta[h, other : other + 16] = extra.astype(BF)
            dta[h, other + 16 : other + 64] = jnp.zeros((48, rows), BF)
        if not fast:
            keep = [
                pltpu.make_async_copy(stage_d, gd_o, out_sem.at[0]),
                pltpu.make_async_copy(stage_u, gu_o, out_sem.at[1]),
                pltpu.make_async_copy(stage_o, go_o, out_sem.at[2]),
            ]
            for copy in keep:
                copy.start()
            for copy in keep:
                copy.wait()
        keep_layer.wait()

    pl.run_scoped(
        feed_forward,
        pltpu.VMEM((rows, width), BF),
        pltpu.VMEM((width, rows), BF),
        pltpu.VMEM((rows, width), BF),
        pltpu.VMEM((width, width), BF),
        pltpu.VMEM((2, width, span), BF),
        pltpu.VMEM((2, span, width), BF),
        pltpu.VMEM((rows, width), F32),
        pltpu.VMEM((8, span), F32),
    )

    def dx_stage(step, half):
        return stage_d.at[step // 2, step % 2, half]

    def dx_copy(way, step, block, half):
        return pltpu.make_async_remote_copy(
            src_ref=dx_stage(step, half), dst_ref=rx.at[block + way, half],
            send_sem=dsend.at[way, block, half], recv_sem=drecv.at[way, block, half],
            device_id={"seq": me - 1 if way == 0 else me + 1}, device_id_type=MESH,
        )

    def store_dx(step, half, value):
        for k in range(2):
            stage_d[step // 2, step % 2, half, k] = value[128 * k : 128 * (k + 1)]

    def relay_at(place, way, step, half):
        @pl.when(me == place)
        def _():
            block = block_at(step)
            dx_copy(way, step, block, half).wait_recv()
            add_parts(dx_stage(step, half), rx.at[block + way, half], 2)
            dx_copy(way, step, block, half).start()

    def relay_far(step, half):
        relay_at(1, 1, step, half)
        relay_at(2, 0, step, half)

    def relay_near(half):
        relay_at(1, 0, 2, half)
        relay_at(2, 1, 2, half)

    def send_dx(step, half):
        block = block_at(step)

        @pl.when(me == 0)
        def _():
            dx_copy(1, step, block, half).start()

        @pl.when(me == seq - 1)
        def _():
            dx_copy(0, step, block, half).start()

    def attention(xt, dqt, gk, gv, dk, dv, dq, wp, hot_ref):
        def load_x(step):
            return pltpu.make_async_copy(xt_h.at[block_at(step)], xt, in_sem.at[0, 3])

        load_wp = pltpu.make_async_copy(wp_h, wp, load_sem.at[HEADS + 1])
        for copy in (load_x(0), load_wp):
            copy.start()
        low, high = lane_halves()
        dqt[...] = jnp.zeros_like(dqt)
        lane = lax.broadcasted_iota(jnp.int32, (1, 128), 1)
        v_low = jnp.where(lane < 3, 1.0, 0.0).astype(BF)
        v_high = jnp.where((lane >= 64) & (lane < 67), 1.0, 0.0).astype(BF)
        if fast:
            for unit_sum in rs_d:
                unit_sum.wait_sends((0,))
        for copy in fills:
            copy.wait()

        def hooks(g):
            if not fast:
                return

            def at(when, action):
                @pl.when(g == when)
                def _():
                    action()

            def second():
                turn(rs_d[1], rs_u[1])
                for unit_sum in (rs_d[2], rs_u[2], rs_o):
                    unit_sum.finish(0)
                    unit_sum.start(1)

            at(6, lambda: (second(), ar_d[0].middles_swap(), ar_u[0].middles_swap()))
            at(12, lambda: (close(rs_d[1], rs_u[1]), ar_d[1].ends_send(), ar_u[1].ends_send()))
            at(14, lambda: relay_far(0, 0))
            at(16, lambda: (ar_d[0].middles_send(), ar_u[0].middles_send()))
            at(17, lambda: turn(rs_d[2], rs_u[2]))
            at(20, lambda: relay_far(0, 1))
            at(21, lambda: (turn(rs_o), close(rs_d[2], rs_u[2])))
            at(23, lambda: (close(rs_o), [unit.ends_send() for unit in (ar_d[2], ar_u[2], ar_o)]))

        def products(slot, i, part=slice(None)):
            at = pl.ds(pl.multiple_of(i * 128, 128), 128)
            keys, values = kn[slot, i, part], vn[slot, i, part]
            q_pair, d_pair = qn[i], d_att[:, at]
            hot = hot_ref[part]
            scores = [
                mm(keys * low + hot * high, qta[2 * i]),
                mm(keys * high + hot * low, qta[2 * i + 1]),
            ]
            slopes = [
                mm(values * low + v_high, dta[2 * i]),
                mm(values * high + v_low, dta[2 * i + 1]),
            ]
            d_keys = jnp.zeros((keys.shape[0], 128), F32)
            d_values = jnp.zeros((keys.shape[0], 128), F32)
            for j in range(2):
                h = 2 * i + j
                mask = low if j == 0 else high
                probs = jnp.exp(scores[j])
                d_scores = (probs * slopes[j]).astype(BF)
                d_values = d_values + mm(probs.astype(BF), d_pair * mask)
                d_keys = d_keys + mm(d_scores, q_pair * mask)
                dqt[h] += mm(kt[slot, i, 64 * j : 64 * (j + 1), part], d_scores)
            dk[part, at] = d_keys.astype(BF)
            dv[part, at] = d_values.astype(BF)

        def enter(step):
            for copy in loads(step):
                copy.wait()
            hot_ref[...] = key_codes(lens, block_at(step), rows)

        enter(0)
        for copy in loads(1):
            copy.start()

        def one_half(half, carry):
            part = pl.ds(pl.multiple_of(half * half_rows, half_rows), half_rows)

            def one_pair(i, carry):
                hooks(half * PAIRS + i)
                products(0, i, part)
                return carry

            lax.fori_loop(0, PAIRS, one_pair, 0)

            @pl.when(half == 0)
            def _():
                load_wp.wait()

            store_dx(0, half, (mm_nt(dk[part], wp[1]) + mm_nt(dv[part], wp[2])).astype(BF))
            send_dx(0, half)
            return carry

        lax.fori_loop(0, 2, one_half, 0)
        load_x(0).wait()
        gk[...] = mm(xt[...], dk[...])
        gv[...] = mm(xt[...], dv[...])
        load_x(1).start()
        sums[3:4] = jnp.sum(dv[...].astype(F32), axis=0, keepdims=True)

        def one_step(step, carry):
            slot = step % 2
            enter(step)
            for copy in loads(step + 1):
                copy.start()

            def one_pair(i, carry):
                hooks((step + 1) * PAIRS + i)
                products(slot, i)
                return carry

            lax.fori_loop(0, PAIRS, one_pair, 0)
            dx = (mm_nt(dk[...], wp[1]) + mm_nt(dv[...], wp[2])).astype(BF)
            for half in range(2):
                store_dx(step, half, dx[half * half_rows : (half + 1) * half_rows])
                send_dx(step, half)
            load_x(step).wait()
            gk[...] += mm(xt[...], dk[...])
            gv[...] += mm(xt[...], dv[...])
            load_x(step + 1).start()
            sums[3:4] += jnp.sum(dv[...].astype(F32), axis=0, keepdims=True)
            return carry

        lax.fori_loop(1, seq - 1, one_step, 0)

        last = (seq - 1) % 2
        enter(seq - 1)
        load_x(seq - 1).wait()
        lane_w = lax.broadcasted_iota(jnp.int32, (width, 128), 1)
        lo = lane_w < 64
        if fast:
            for unit_sum in rs_u:
                unit_sum.wait_sends((0,))

        def one_couple(c, carry):
            if fast:

                @pl.when(c == 0)
                def _():
                    relay_near(0)
                    ar_d[1].middles_swap()
                    ar_u[1].middles_swap()

                @pl.when(c == 1)
                def _():
                    relay_near(1)
                    relay_far(1, 0)

                @pl.when(c == 2)
                def _():
                    relay_far(1, 1)
                    ar_d[1].middles_send()
                    ar_u[1].middles_send()

                @pl.when(c >= 1)
                def _():
                    for unit in couple(c - 1):
                        unit.finish(0)
                        unit.start(1)

                @pl.when(c >= 2)
                def _():
                    turn(*couple(c - 2))


            def one_pair(k, carry):
                products(last, 2 * c + k)
                return carry

            lax.fori_loop(0, 2, one_pair, 0)
            at = pl.ds(pl.multiple_of(c * 256, 256), 256)
            turned = dqt[pl.ds(4 * c, 4)].reshape(256, rows) * (HEAD**-0.5)
            dq_part = turned.T.astype(BF)
            dq[:, at] = dq_part
            x_t = xt[...]
            gq_part = mm(x_t, dq_part)
            gk_part = gk[:, at] + mm(x_t, dk[:, at])
            gv_part = gv[:, at] + mm(x_t, dv[:, at])
            for k in range(2):
                cut = slice(128 * k, 128 * (k + 1))
                q_tile, v_tile = gq_part[:, cut], gv_part[:, cut]
                k_tile = pltpu.roll(gk_part[:, cut], 64, 1)
                tiles = jnp.where(lo, q_tile, k_tile), jnp.where(lo, v_tile, q_tile), jnp.where(lo, k_tile, v_tile)
                for j, tile in enumerate(tiles):
                    tile = tile.astype(BF)
                    to = slice(384 * k + 128 * j, 384 * k + 128 * (j + 1))
                    for d in range(GROUPS):
                        stage_u[(c, *place_of(d), slice(None), to)] = tile[part_w * d : part_w * (d + 1)]
            if fast:
                for unit in couple(c):
                    unit.start(0)
            return carry

        lax.fori_loop(0, PAIRS // 2, one_couple, 0)
        if not fast:
            for step in range(2):
                for half in range(2):
                    relay_far(step, half)
            relay_near(0)
            relay_near(1)
        dx_own = gk.at[pl.ds(0, rows)]
        dx_own[...] = mm_nt(dk[...], wp[1]) + mm_nt(dv[...], wp[2]) + mm_nt(dq[...], wp[0])
        sums[3:4] += jnp.sum(dv[...].astype(F32), axis=0, keepdims=True)
        sums[2:3] = jnp.sum(dq[...].astype(F32), axis=0, keepdims=True)
        load_tok = pltpu.make_async_copy(tok_h, dv, load_sem.at[HEADS + 2])
        load_tok.start()
        if fast:
            for unit in couple(2):
                unit.finish(0)
                unit.start(1)
            turn(*couple(1))
            close(*couple(0))
            ar_d[2].middles_swap()
            turn(*couple(2))
            ar_u[2].middles_swap()
            close(*couple(1), *couple(2))
            ar_o.middles_swap()
            for unit in ar_q:
                unit.ends_send()
            ar_d[2].middles_send()
            ar_u[2].middles_send()

        load_tok.wait()
        for way, there in ((0, has_right), (1, has_left)):
            @pl.when(there)
            def _():
                for half in range(2):
                    dx_copy(way, 0, me, half).wait_recv()

                def some(k, carry):
                    at = pl.ds(pl.multiple_of(k * 32, 32), 32)
                    piece = rx[me + way, k // 8, k // 4 % 2, pl.ds(pl.multiple_of(k % 4 * 32, 32), 32)]
                    dx_own[at] += piece.astype(F32)
                    return carry

                lax.fori_loop(0, rows // 32, some, 0)

        values = dv[...].astype(F32)
        centred = values - jnp.mean(values, axis=-1, keepdims=True)
        scale = lax.rsqrt(jnp.mean(centred * centred, axis=-1, keepdims=True) + EPS)
        unit_rows = centred * scale
        d_normed = dx_own[...]
        sums[0:1] = jnp.sum(d_normed * unit_rows, axis=0, keepdims=True)
        sums[1:2] = jnp.sum(d_normed, axis=0, keepdims=True)
        rows8 = sums[...]
        for d in range(GROUPS):
            y, x, core = place_of(d)
            stage_v[y, x, core, 0:8, 0:part_w] = rows8[:, part_w * d : part_w * (d + 1)]
            stage_v[y, x, core, 8 : 8 + CHUNKS] = vec_up[0:CHUNKS, 128 * d : 128 * (d + 1)]
        if fast:
            rs_v.start(0)
        if fast:
            ar_o.middles_send()
            ar_q[0].middles_swap()
        scaled = d_normed * per_row(gain_one)
        dk[...] = (
            d_mid[...]
            + scale
            * (
                scaled
                - jnp.mean(scaled, axis=-1, keepdims=True)
                - unit_rows * jnp.mean(scaled * unit_rows, axis=-1, keepdims=True)
            )
        ).astype(BF)
        keep = [pltpu.make_async_copy(dk, tok_o, out_sem.at[6])]
        keep[0].start()
        if fast:
            ar_q[1].middles_swap()
            rs_v.finish(0)
            rs_v.start(1)
            ar_q[2].middles_swap()
            ar_q[0].middles_send()
            rs_v.finish(1)
            rs_v.start(2)
            ar_q[3].middles_swap()
            ar_q[1].middles_send()
            rs_v.finish(2)
            ar_v.ends_send()
            ar_q[4].middles_swap()
            ar_q[2].middles_send()
            ar_q[5].middles_swap()
            ar_q[3].middles_send()
            ar_v.middles_swap()
            ar_q[4].middles_send()
            ar_q[5].middles_send()
            ar_v.middles_send()
            done = ((ar_d, fin_d, fin_d_o), (ar_u, fin_u, fin_u_o), ((ar_o,), fin_o, fin_o_o), (ar_q, fin_q, fin_q_o), ((ar_v,), fin_v, fin_v_o))
            for k, (units, src, dst) in enumerate(done):
                for unit in units:
                    unit.finish()
                keep.append(pltpu.make_async_copy(src, dst, out_sem.at[k]))
                keep[-1].start()
            for unit in (*rs_d, *rs_u):
                unit.wait_sends((1, 2))
            for unit in (rs_o, rs_v, *couple(0), *couple(1), *couple(2)):
                unit.wait_sends((0, 1, 2))
        else:
            for k, (src, dst) in enumerate(((stage_u, gq_o), (stage_v, stage_v_o))):
                keep.append(pltpu.make_async_copy(src, dst, out_sem.at[k]))
                keep[-1].start()
        for copy in keep:
            copy.wait()

        for place, first, second in ((0, 1, 1), (1, 1, 0), (2, 0, 1), (3, 0, 0)):
            @pl.when(me == place)
            def _():
                for step, way in enumerate((first, first, second)):
                    for half in range(2):
                        dx_copy(way, step, block_at(step), half).wait_send()

    pl.run_scoped(
        attention,
        pltpu.VMEM((width, rows), BF),
        pltpu.VMEM((HEADS, HEAD, rows), F32),
        pltpu.VMEM((width, width), F32),
        pltpu.VMEM((width, width), F32),
        pltpu.VMEM((rows, width), BF),
        pltpu.VMEM((rows, width), BF),
        pltpu.VMEM((rows, width), BF),
        pltpu.VMEM((3, width, width), BF),
        pltpu.VMEM((rows, 128), BF),
    )


def layer_back(fast, *args):
    kn, wp = args[0], args[6]
    seq, _, rows, _ = kn.shape
    width = wp.shape[1]
    span = GROUPS * 128
    part = width // GROUPS
    any_spec = pl.BlockSpec(memory_space=pl.ANY)
    vmem = pl.BlockSpec(memory_space=pltpu.VMEM)
    sds = jax.ShapeDtypeStruct
    cube = (2, 2, 2)
    outs = [sds((rows, width), BF), sds((rows, width), BF)]
    if fast:
        outs += [
            sds((CHUNKS, 128, width), BF), sds((CHUNKS, part, span), BF), sds((part, width), BF),
            sds((PAIRS, part, 384), BF), sds((16, 128), F32),
        ]
    else:
        outs += [
            sds((CHUNKS, *cube, 128, width), BF), sds((CHUNKS, *cube, part, span), BF), sds((*cube, part, width), BF),
            sds((CHUNKS, *cube, part, span), BF), sds((*cube, 16, 128), F32),
        ]
    scratch = [
        pltpu.VMEM((CHUNKS, *cube, 128, width), BF),
        pltpu.VMEM((CHUNKS, *cube, part, span), BF),
        pltpu.VMEM((*cube, part, width), BF),
        pltpu.VMEM((*cube, 16, 128), F32),
        pltpu.VMEM((8, width), F32),
        pltpu.VMEM((8, span), F32),
        pltpu.VMEM((rows, width), BF),
        pltpu.VMEM((HEADS, 128, rows), BF),
        pltpu.VMEM((rows, width), F32),
        pltpu.VMEM((seq + 1, 2, 2, 128, width), BF),
        pltpu.VMEM((2, PAIRS, rows, 128), BF),
        pltpu.VMEM((2, PAIRS, rows, 128), BF),
        pltpu.VMEM((2, PAIRS, 128, rows), BF),
        pltpu.VMEM((HEADS, 128, rows), BF),
        pltpu.VMEM((PAIRS, rows, 128), BF),
        pltpu.SemaphoreType.DMA((3, CHUNKS, GROUPS)),
        pltpu.SemaphoreType.DMA((2, 4)),
        pltpu.SemaphoreType.DMA((HEADS + 3,)),
        pltpu.SemaphoreType.DMA((7,)),
        pltpu.SemaphoreType.DMA((2, 4, 2)),
        pltpu.SemaphoreType.DMA((2, 4, 2)),
    ]
    if fast:
        d, u, o, q = (128, width), (part, span), (part, width), (part, 384)
        scratch += [
            pltpu.VMEM(shape, BF)
            for shape in (
                (CHUNKS, 2, 2, *d), (CHUNKS, 2, 2, *u), (2, 2, *o), (CHUNKS, 2, *d), (CHUNKS, 2, *u), (2, *o),
                (CHUNKS, *d), (CHUNKS, *u), o, (PAIRS, 2, 2, *q), (PAIRS, 2, *q), (PAIRS, *q),
            )
        ]
        scratch += [pltpu.VMEM((2, 2, 16, 128), F32), pltpu.VMEM((2, 16, 128), F32), pltpu.VMEM((16, 128), F32)]
        for shape in ((CHUNKS, *d), (CHUNKS, *u), o, (PAIRS, *q)):
            scratch += [pltpu.VMEM(shape, BF)] * 2
        scratch += [pltpu.VMEM((16, 128), F32)] * 2
        scratch += [pltpu.SemaphoreType.DMA((14, 3))] * 4
    return pl.pallas_call(
        partial(layer_back_kernel, fast),
        out_shape=outs,
        in_specs=[any_spec] * 13 + [vmem, pl.BlockSpec(memory_space=pltpu.SMEM)] + [vmem] * 6,
        out_specs=[any_spec] * len(outs),
        scratch_shapes=scratch,
        compiler_params=pltpu.CompilerParams(
            collective_id=1, has_side_effects=True, vmem_limit_bytes=62 * MIB
        ),
        name="layer_back",
    )(*args)


def unpack_kernel(
    fin_d, fin_u, fin_o, fin_q, fin_v, layer, grad, layer_o, grad_o, down_o, up_o, out_o, qkv_o, *refs
):
    *vec_o, a_d, a_u, a_o, a_q, down, up, out, qkv, held, in_sem, out_sem = refs
    inward = [
        pltpu.make_async_copy(src, dst, in_sem.at[k])
        for k, (src, dst) in enumerate(
            ((fin_u, a_u), (fin_d, a_d), (fin_q, a_q), (fin_o, a_o), (layer, held.at[0]), (grad, held.at[1]))
        )
    ]
    outward = [
        pltpu.make_async_copy(src, dst, out_sem.at[k])
        for k, (src, dst) in enumerate(
            ((up, up_o), (down, down_o), (qkv, qkv_o), (out, out_o), (held.at[0], layer_o), (held.at[1], grad_o))
        )
    ]
    for copy in inward:
        copy.start()
    chunks, _, _ = a_d.shape
    part = a_u.shape[1]
    inward[0].wait()
    for c in range(chunks):
        for d in range(GROUPS):
            at = chunk_columns(up.shape[1], c, d)
            up[:, at : at + 128] = a_u[c, :, 128 * d : 128 * (d + 1)].astype(F32)
    outward[0].start()
    inward[1].wait()
    for c in range(chunks):
        down[128 * c : 128 * (c + 1)] = a_d[c].astype(F32)
    outward[1].start()
    inward[2].wait()
    for i in range(PAIRS):
        qkv[:, 384 * i : 384 * (i + 1)] = a_q[i].astype(F32)
    outward[2].start()
    inward[3].wait()
    out[...] = a_o[...].astype(F32)
    outward[3].start()
    for k in (4, 5):
        inward[k].wait()
        outward[k].start()
    for r in range(8):
        vec_o[r][...] = fin_v[r : r + 1, :part].reshape(part)
    vec_o[8][...] = jnp.concatenate([fin_v[8 + c : 9 + c] for c in range(chunks)], axis=1).reshape(128 * chunks)
    for copy in outward:
        copy.wait()


def unpack(fin_d, fin_u, fin_o, fin_q, fin_v, layer, grad):
    vmem = pl.BlockSpec(memory_space=pltpu.VMEM)
    any_spec = pl.BlockSpec(memory_space=pl.ANY)
    chunks, _, width = fin_d.shape
    part, span = fin_u.shape[1:]
    sds = jax.ShapeDtypeStruct
    large = [(128 * chunks, width), (part, span * chunks), (part, width), (part, PAIRS * fin_q.shape[2])]
    outs = [sds(layer.shape, BF), sds(grad.shape, BF)] + [sds(shape, F32) for shape in large]
    outs += [sds((part,), F32)] * 8 + [sds((128 * chunks,), F32)]
    return pl.pallas_call(
        unpack_kernel, out_shape=outs, in_specs=[any_spec] * 4 + [vmem] + [any_spec] * 2,
        out_specs=[any_spec] * 6 + [vmem] * 9,
        scratch_shapes=[
            *(pltpu.VMEM(ref.shape, BF) for ref in (fin_d, fin_u, fin_o, fin_q)),
            *(pltpu.VMEM(shape, F32) for shape in large),
            pltpu.VMEM((2, *layer.shape), BF),
            pltpu.SemaphoreType.DMA((6,)),
            pltpu.SemaphoreType.DMA((6,)),
        ],
        compiler_params=pltpu.CompilerParams(vmem_limit_bytes=60 * MIB),
        name="unpack",
    )(fin_d, fin_u, fin_o, fin_q, fin_v, layer, grad)


def local(
    tokens, cell_lengths, ln1_gain, ln1_shift, w_qkv, b_query, b_value, w_out, b_out,
    ln2_gain, ln2_shift, w_up, b_up, w_down, b_down, cotangent,
):
    bucket_count, local_slots, width = tokens.shape
    ff = w_up.shape[1]
    seq_count = lax.axis_size("seq")
    dp_count = lax.axis_size("dp")
    fast = dp_count == GROUPS
    rows = bucket_count * local_slots
    flat = tokens.reshape(rows, width)
    kn, vn, kt, xt, qn, qt, wp, att_t, lse = gather_attend(
        flat, cell_lengths, ln1_gain, ln1_shift, w_qkv, b_query, b_value, seq_count
    )
    layer_out, tokens_grad, *found = layer_back(
        fast, kn, vn, kt, xt, qn, qt, wp, att_t, flat, cotangent.reshape(rows, width), w_out, w_up, w_down,
        lse, cell_lengths, ln1_gain, b_out, ln2_gain, ln2_shift, b_up, b_down,
    )
    if fast:
        layer_out, tokens_grad, down, up, out, qkv, *vectors = unpack(*found, layer_out, tokens_grad)
    else:

        def summed(g):
            share = lax.psum_scatter(g, "dp", scatter_dimension=0, tiled=True)
            return lax.psum(share, "seq").astype(F32)

        g_down, g_up, g_out, g_qkv, packed = found
        g_qkv = g_qkv.reshape(CHUNKS, width, GROUPS * 128)[:, :, :768]
        g_qkv = jnp.moveaxis(g_qkv, 0, 1).reshape(width, 3 * width)
        g_down = jnp.moveaxis(g_down.reshape(CHUNKS, GROUPS, 128, width), 0, 1).reshape(ff, width)
        g_up = jnp.transpose(g_up.reshape(CHUNKS, width, GROUPS, 128), (1, 2, 0, 3)).reshape(width, ff)
        down, up, out, qkv = summed(g_down), summed(g_up), summed(g_out.reshape(width, width)), summed(g_qkv)
        packed = packed.reshape(GROUPS, 16, 128)
        vectors = [packed[:, r, : width // GROUPS].reshape(width) for r in range(8)]
        vectors.append(packed[:, 8 : 8 + CHUNKS].reshape(ff))
        together = jnp.concatenate([v.reshape(dp_count, -1) for v in vectors], axis=1)
        together = lax.psum(together, ("dp", "seq"))
        mine = lax.dynamic_index_in_dim(together, lax.axis_index("dp"), 0, keepdims=False)
        sizes = [v.shape[0] // dp_count for v in vectors]
        vectors = [mine[sum(sizes[:k]) : sum(sizes[: k + 1])] for k in range(len(sizes))]
    layer_out = layer_out.reshape(tokens.shape)
    tokens_grad = tokens_grad.reshape(tokens.shape)
    g1, s1, bq, bv, bo, g2, s2, bd, bu = vectors
    return layer_out, tokens_grad, g1, s1, qkv, bq, bv, out, bo, g2, s2, up, bu, down, bd


def solution(mesh):
    token_spec = P("dp", "seq", None)
    vector, matrix = P("dp"), P("dp", None)
    placed = (token_spec, P("dp", None)) + (P(),) * 13 + (token_spec,)
    return jax.shard_map(
        local,
        mesh=mesh,
        in_specs=placed,
        out_specs=(
            token_spec, token_spec, vector, vector, matrix, vector, vector, matrix, vector,
            vector, vector, matrix, vector, matrix, vector,
        ),
        check_vma=False,
    )
```

```python
from functools import partial

import jax
import jax.numpy as jnp
from jax import lax
from jax.experimental import pallas as pl
from jax.experimental.pallas import tpu as pltpu
from jax.sharding import PartitionSpec as P

HEADS = 12
HEAD = 64
PAIRS = 6
EPS = 1e-05
ROOT_HALF = 0.7071067811865476
BIG = 1e30
MESH = pl.DeviceIdType.MESH
F32 = jnp.float32
BF = jnp.bfloat16
MIB = 1024 * 1024


def normalize(values, gain, shift):
    average = jnp.mean(values, axis=-1, keepdims=True)
    centred = values - average
    variance = jnp.mean(centred * centred, axis=-1, keepdims=True)
    return centred * lax.rsqrt(variance + EPS) * gain + shift


def gelu_exact(values):
    return 0.5 * values * (1.0 + jax.scipy.special.erf(values * ROOT_HALF))


def mm(a, b):
    return jnp.dot(a, b, preferred_element_type=F32)


def mm_nt(a, b):
    return lax.dot_general(a, b, (((1,), (1,)), ((), ())), preferred_element_type=F32)


def cell_bounds(lens_ref, index):
    start = jnp.zeros(index.shape, jnp.int32)
    end = jnp.zeros(index.shape, jnp.int32)
    at = jnp.int32(0)
    for c in range(lens_ref.shape[1]):
        after = at + lens_ref[0, c]
        start = jnp.where(index == c, at, start)
        end = jnp.where(index == c, after, end)
        at = after
    return start, end


def key_codes(lens_ref, block, rows):
    lane = lax.broadcasted_iota(jnp.int32, (1, 128), 1) % 64
    start, end = cell_bounds(lens_ref, lane)
    ones = ((lane >= 8) & (lane < 11)).astype(F32)
    slot = lax.broadcasted_iota(jnp.int32, (rows, 128), 0) + block * rows
    hot = jnp.where((slot >= start) & (slot < end), 1.0, 0.0)
    return (hot + ones).astype(BF)


def query_codes(lens_ref, block, rows):
    cell = lax.broadcasted_iota(jnp.int32, (64, 1), 0)
    start, end = cell_bounds(lens_ref, cell)
    slot = lax.broadcasted_iota(jnp.int32, (64, rows), 1) + block * rows
    inside = (slot >= start) & (slot < end)
    return jnp.where(inside | (cell >= 8), 0.0, -BIG)


def lane_halves():
    lane = lax.broadcasted_iota(jnp.int32, (1, 128), 1)
    low = jnp.where(lane < 64, 1.0, 0.0).astype(BF)
    high = jnp.where(lane < 64, 0.0, 1.0).astype(BF)
    return low, high


def sort_weights(w_ref, wp):
    depth = w_ref.shape[0]
    lane = lax.broadcasted_iota(jnp.int32, (depth, 128), 1)
    low = lane < 64
    for i in range(PAIRS):
        t0, t1, t2 = (w_ref[:, 384 * i + 128 * j : 384 * i + 128 * (j + 1)].astype(F32) for j in range(3))
        at = slice(128 * i, 128 * (i + 1))
        wp[0, :, at] = jnp.where(low, t0, t1).astype(BF)
        wp[1, :, at] = pltpu.roll(jnp.where(low, t2, t0), 64, 1).astype(BF)
        wp[2, :, at] = jnp.where(low, t1, t2).astype(BF)


def gather_kernel(
    tok, lens, gain, shift, w_h, bq, bv,
    kn_o, vn_o, kt_o, xt_o, qn_o, qt_o, wp_o, att_o, lse_h,
    xr, w, wp, kn, vn, kt, xt, qn, qt, qta, vta, acc, top, att_t, lse_o, send, recv, in_sem, out_sem,
):
    rows, width = tok.shape
    span = rows // 2
    seq = lax.axis_size("seq")
    me = lax.axis_index("seq")
    has_left, has_right = me > 0, me < seq - 1
    at_end = (me == 0) | (me == seq - 1)

    barrier = pltpu.get_barrier_semaphore()

    @pl.when(has_left)
    def _():
        pl.semaphore_signal(barrier, inc=1, device_id={"seq": me - 1}, device_id_type=MESH)

    @pl.when(has_right)
    def _():
        pl.semaphore_signal(barrier, inc=1, device_id={"seq": me + 1}, device_id_type=MESH)

    own_tokens = pltpu.make_async_copy(tok, xr.at[me], in_sem.at[0])
    own_tokens.start()
    weights = pltpu.make_async_copy(w_h, w, in_sem.at[1])
    weights.start()

    @pl.when(at_end)
    def _():
        pl.semaphore_wait(barrier, 1)

    @pl.when(~at_end)
    def _():
        pl.semaphore_wait(barrier, 2)

    def copy(way, hop, quarter, block):
        at = pl.ds(quarter * (rows // 4), rows // 4)
        return pltpu.make_async_remote_copy(
            src_ref=tok.at[at] if hop == 0 else xr.at[block, at],
            dst_ref=xr.at[block, at],
            send_sem=send.at[way, hop, quarter],
            recv_sem=recv.at[way, hop, quarter],
            device_id={"seq": jnp.maximum(me - 1, 0) if way == 0 else jnp.minimum(me + 1, seq - 1)},
            device_id_type=MESH,
        )

    def can_send(way):
        return has_left if way == 0 else has_right

    def holds(way, hop):
        return me + hop < seq if way == 0 else me - hop >= 0

    def block_of(way, hop):
        return me + hop if way == 0 else me - hop

    for quarter in range(4):
        for way in range(2):
            @pl.when(can_send(way))
            def _():
                copy(way, 0, quarter, me).start()

    def normed(raw):
        return normalize(raw.astype(F32), gain[...].reshape(1, -1), shift[...].reshape(1, -1)).astype(BF)

    row16 = lax.broadcasted_iota(jnp.int32, (16, span), 0)
    for h in range(HEADS):
        vta[h, 64:] = jnp.where(row16 == 0, 1.0, 0.0).astype(BF)
    acc[...] = jnp.zeros_like(acc)
    top[...] = jnp.full_like(top, -3e38)
    codes = query_codes(lens, me, rows).astype(BF)
    low, high = lane_halves()
    own_tokens.wait()
    weights.wait()
    sort_weights(w, wp)
    keep_w = pltpu.make_async_copy(wp, wp_o, out_sem.at[4, 0])
    keep_w.start()
    q = ((mm(normed(xr[me]), wp[0]) + bq[...].reshape(1, -1)).astype(BF).astype(F32) * (HEAD**-0.5)).astype(BF)
    for i in range(PAIRS):
        pair = q[:, 128 * i : 128 * (i + 1)]
        qn[i] = pair
        turned = pair.T
        qt[i] = turned
        qta[2 * i, :64] = turned[:64]
        qta[2 * i, 64:] = codes
        qta[2 * i + 1, :64] = codes
        qta[2 * i + 1, 64:] = turned[64:]
    keep_q = pltpu.make_async_copy(qn, qn_o, out_sem.at[4, 1])
    keep_q.start()
    keep_qt = pltpu.make_async_copy(qt, qt_o, out_sem.at[4, 2])
    keep_qt.start()

    def keep_att(i):
        at = pl.ds(128 * i, 128)
        return pltpu.make_async_copy(att_t.at[at], att_o.at[at], out_sem.at[5, i])

    def keeps(step):
        block = block_at(step)
        return [
            pltpu.make_async_copy(src.at[block], dst.at[block], out_sem.at[step, k])
            for k, (src, dst) in enumerate(((kn, kn_o), (vn, vn_o), (kt, kt_o), (xt, xt_o)))
        ]

    def block_at(step):
        from_end = jnp.where(me == 0, step, seq - 1 - step)
        from_mid = jnp.where(step == 0, me, jnp.where(step == 1, me + 1, jnp.where(step == 2, me - 1, jnp.where(me == 1, seq - 1, 0))))
        return jnp.where(at_end, from_end, from_mid)

    def arrive(due, way, hop, quarter):
        @pl.when(due & holds(way, hop))
        def _():
            block = block_of(way, hop)
            copy(way, hop - 1, quarter, block).wait_recv()

            @pl.when(can_send(way))
            def _():
                copy(way, hop, quarter, block).start()

    def attend(step, part, span):
        block = block_at(step)
        at = pl.ds(pl.multiple_of(part * span, span), span)
        x = normed(xr[block, at])
        keys = mm(x, wp[1]).astype(BF)
        values = (mm(x, wp[2]) + bv[...].reshape(1, -1)).astype(BF)
        hot = key_codes(lens, block * (rows // span) + part, span)
        hot_low, hot_high = hot * low, hot * high
        xt[block, :, at] = x.T
        for i in range(PAIRS):
            cut = slice(128 * i, 128 * (i + 1))
            kn[block, i, at] = keys[:, cut]
            kt[block, i, :, at] = keys[:, cut].T
            vn[block, i, at] = values[:, cut]
            turned = values[:, cut].T
            vta[2 * i, :64, :span] = turned[:64]
            vta[2 * i + 1, :64, :span] = turned[64:]

        @pl.when(part == rows // span - 1)
        def _():
            for c in keeps(step):
                c.start()

        def one_pair(i, carry):
            pair = kn[block, i, at]
            scores = [
                mm(pair * low + hot_high, qta[2 * i]),
                mm(pair * high + hot_low, qta[2 * i + 1]),
            ]
            for j in range(2):
                h = 2 * i + j
                before = top[h]
                now = jnp.maximum(before, jnp.max(scores[j], axis=0, keepdims=True))
                raised = jnp.exp(scores[j] - now).astype(BF)
                top[h] = now
                acc[h] = acc[h] * jnp.exp(before - now) + mm(vta[h, :, :span], raised)
            return carry

        lax.fori_loop(0, PAIRS, one_pair, 0)

    def half_step(turn, carry):
        for hop in range(1, 3):
            for quarter in range(4):
                first = jnp.where(at_end, 2 * hop, 2 * hop if hop == 1 else -2)
                for way in range(2):
                    arrive(turn == first + quarter // 2, way, hop, quarter)
        attend(turn // 2, turn % 2, rows // 2)
        return carry

    def last_step(turn, carry):
        for hop in range(2, 4):
            for quarter in range(4):
                due = (turn == quarter) & (at_end if hop == 3 else ~at_end)
                for way in range(2):
                    arrive(due, way, hop, quarter)
        attend(seq - 1, turn, rows // 4)
        return carry

    lax.fori_loop(0, 2 * (seq - 1), half_step, 0)
    lax.fori_loop(0, 4, last_step, 0)

    for i in range(PAIRS):
        for j in range(2):
            h = 2 * i + j
            total = acc[h, 64:65]
            lse_o[h : h + 1] = top[h] + jnp.log(total)
            att_t[64 * h : 64 * (h + 1)] = (acc[h, :64] * (1.0 / total)).astype(BF)
        keep_att(i).start()
    lse_o[HEADS:] = jnp.zeros((16 - HEADS, rows), F32)
    keep_lse = pltpu.make_async_copy(lse_o, lse_h, out_sem.at[4, 4])
    keep_lse.start()

    for way in range(2):
        for hop in range(3):
            for quarter in range(4):
                @pl.when(can_send(way) & holds(way, hop))
                def _():
                    copy(way, hop, quarter, block_of(way, hop)).wait_send()

    keep_w.wait()
    keep_q.wait()
    keep_qt.wait()
    for i in range(PAIRS):
        keep_att(i).wait()
    keep_lse.wait()
    for step in range(4):
        for c in keeps(step):
            c.wait()


def gather_attend(tokens, lens, gain, shift, w, bq, bv, seq):
    rows, width = tokens.shape
    any_spec = pl.BlockSpec(memory_space=pl.ANY)
    vmem = pl.BlockSpec(memory_space=pltpu.VMEM)
    sds = jax.ShapeDtypeStruct
    outs = [
        sds((seq, PAIRS, rows, 128), BF),
        sds((seq, PAIRS, rows, 128), BF),
        sds((seq, PAIRS, 128, rows), BF),
        sds((seq, width, rows), BF),
        sds((PAIRS, rows, 128), BF),
        sds((PAIRS, 128, rows), BF),
        sds((3, width, width), BF),
        sds((width, rows), BF),
        sds((16, rows), F32),
    ]
    return pl.pallas_call(
        gather_kernel,
        out_shape=outs,
        in_specs=[any_spec, pl.BlockSpec(memory_space=pltpu.SMEM), vmem, vmem, any_spec, vmem, vmem],
        out_specs=[any_spec] * 9,
        scratch_shapes=[
            pltpu.VMEM((seq, rows, width), BF),
            pltpu.VMEM((width, 3 * width), BF),
            pltpu.VMEM((3, width, width), BF),
            pltpu.VMEM((seq, PAIRS, rows, 128), BF),
            pltpu.VMEM((seq, PAIRS, rows, 128), BF),
            pltpu.VMEM((seq, PAIRS, 128, rows), BF),
            pltpu.VMEM((seq, width, rows), BF),
            pltpu.VMEM((PAIRS, rows, 128), BF),
            pltpu.VMEM((PAIRS, 128, rows), BF),
            pltpu.VMEM((HEADS, 128, rows), BF),
            pltpu.VMEM((HEADS, 80, rows // 2), BF),
            pltpu.VMEM((HEADS, 80, rows), F32),
            pltpu.VMEM((HEADS, 1, rows), F32),
            pltpu.VMEM((width, rows), BF),
            pltpu.VMEM((16, rows), F32),
            pltpu.SemaphoreType.DMA((2, 4, 4)),
            pltpu.SemaphoreType.DMA((2, 4, 4)),
            pltpu.SemaphoreType.DMA((2,)),
            pltpu.SemaphoreType.DMA((6, 6)),
        ],
        compiler_params=pltpu.CompilerParams(
            collective_id=0, has_side_effects=True, vmem_limit_bytes=58 * MIB
        ),
        name="gather_attend",
    )(tokens, lens, gain, shift, w, bq, bv)


def three_parts(values):
    high = values.astype(BF).astype(F32)
    middle = (values - high).astype(BF).astype(F32)
    return high, middle, values - high - middle


def add_parts(total, other, parts=1, step=32):
    depth = total.shape[-2] // step

    def some(k, carry):
        at = (pl.ds(pl.multiple_of(k % depth * step, step), step),)
        if len(total.shape) == 3:
            at = (k // depth, *at)
        total[at] = total[at] + other[at]
        return carry

    lax.fori_loop(0, parts * depth, some, 0)


def dp_place():
    dp = lax.axis_index("dp")
    core, x, y = dp % 2, (dp // 2) % 2, dp // 4
    return (core, x, y), (dp + 1 - 2 * core, dp + 2 - 4 * x, dp + 4 - 8 * y)


class DpSum:
    def __init__(self, first, stage, one, two, three, send, recv):
        self.first, self.stage, self.one, self.two, self.three = first, stage, one, two, three
        (self.core, self.x, self.y), (self.to_core, self.to_x, self.to_y) = dp_place()
        self.send, self.recv = send, recv
        self.step = min(32, three.shape[-2])

    def copy(self, phase):
        x_first = self.first == "x"
        if phase == 0:
            src, dst, to = self.stage.at[:, :, 1 - self.core], self.one, self.to_core
        elif phase == 1:
            src = self.one.at[:, 1 - self.x] if x_first else self.one.at[1 - self.y]
            dst, to = self.two, self.to_x if x_first else self.to_y
        else:
            src = self.two.at[1 - self.y] if x_first else self.two.at[1 - self.x]
            dst, to = self.three, self.to_y if x_first else self.to_x
        return pltpu.make_async_remote_copy(
            src_ref=src, dst_ref=dst, send_sem=self.send.at[phase], recv_sem=self.recv.at[phase],
            device_id={"dp": to}, device_id_type=MESH,
        )

    def start(self, phase):
        self.copy(phase).start()

    def finish(self, phase):
        self.copy(phase).wait_recv()
        x_first = self.first == "x"
        if phase == 0:
            for y in range(2):
                add_parts(self.one.at[y], self.stage.at[y, :, self.core], 2, self.step)
        elif phase == 1:
            add_parts(self.two, self.one.at[:, self.x] if x_first else self.one.at[self.y], 2, self.step)
        else:
            add_parts(self.three, self.two.at[self.y] if x_first else self.two.at[self.x], 1, self.step)

    def wait_sends(self, phases):
        for phase in phases:
            self.copy(phase).wait_send()


class SeqSum:
    def __init__(self, part, total, swapped, send, recv):
        self.part, self.total, self.swapped = part, total, swapped
        self.send, self.recv = send, recv
        me = lax.axis_index("seq")
        self.end = (me == 0) | (me == 3)
        self.partner = jnp.where(me < 2, 1 - me, 5 - me)
        self.other = 3 - me

    def copy(self, phase):
        src, dst, to = (
            (self.part, self.total, self.partner),
            (self.part, self.swapped, self.other),
            (self.total, self.total, self.partner),
        )[phase]
        return pltpu.make_async_remote_copy(
            src_ref=src, dst_ref=dst, send_sem=self.send.at[phase], recv_sem=self.recv.at[phase],
            device_id={"seq": to}, device_id_type=MESH,
        )

    def ends_send(self):
        @pl.when(self.end)
        def _():
            self.copy(0).start()

    def middles_swap(self):
        @pl.when(~self.end)
        def _():
            self.copy(0).wait_recv()
            add_parts(self.part, self.total, 1, min(32, self.part.shape[-2]))
            self.copy(1).start()

    def middles_send(self):
        @pl.when(~self.end)
        def _():
            self.copy(1).wait_recv()
            depth = min(32, self.part.shape[-2])

            def some(k, carry):
                at = pl.ds(pl.multiple_of(k * depth, depth), depth)
                self.total[at] = self.part[at] + self.swapped[at]
                return carry

            lax.fori_loop(0, self.part.shape[-2] // depth, some, 0)
            self.copy(2).start()

    def finish(self):
        @pl.when(self.end)
        def _():
            self.copy(0).wait_send()
            self.copy(2).wait_recv()

        @pl.when(~self.end)
        def _():
            self.copy(1).wait_send()
            self.copy(2).wait_send()


CHUNKS = 3
GROUPS = 8


def chunk_columns(ff, c, d):
    return (ff // GROUPS) * d + 128 * c


def place_of(d):
    return d // 4, (d // 2) % 2, d % 2


def layer_back_kernel(fast, *refs):
    (
        kn_h, vn_h, kt_h, xt_h, qn_h, qt_h, wp_h, att_h, tok_h, cot_h, w_out_h, w_up_h, w_down_h,
        lse, lens, gain_one, b_out, gain, shift, b_up, b_down, *refs,
    ) = refs
    layer_o, tok_o, *refs = refs
    if fast:
        fin_d_o, fin_u_o, fin_o_o, fin_q_o, fin_v_o, *refs = refs
    else:
        gd_o, gu_o, go_o, gq_o, stage_v_o, *refs = refs
    (
        stage_d, stage_u, stage_o, stage_v, sums, vec_up, d_att, dta, d_mid, rx, kn, vn, kt, qta, qn,
        ff_sem, in_sem, load_sem, out_sem, dsend, drecv, *refs,
    ) = refs
    rows, width = tok_h.shape
    ff = w_up_h.shape[1]
    span = GROUPS * 128
    part_w = width // GROUPS
    seq = lax.axis_size("seq")
    me = lax.axis_index("seq")
    has_left, has_right = me > 0, me < seq - 1
    at_end = (me == 0) | (me == seq - 1)
    half_rows = rows // 2

    barrier = pltpu.get_barrier_semaphore()

    @pl.when(has_left)
    def _():
        pl.semaphore_signal(barrier, inc=1, device_id={"seq": me - 1}, device_id_type=MESH)

    @pl.when(has_right)
    def _():
        pl.semaphore_signal(barrier, inc=1, device_id={"seq": me + 1}, device_id_type=MESH)

    if fast:
        for to in dp_place()[1]:
            pl.semaphore_signal(barrier, inc=1, device_id={"dp": to}, device_id_type=MESH)
    greeted = 3 if fast else 0

    def meet():
        @pl.when(at_end)
        def _():
            pl.semaphore_wait(barrier, greeted + 1)

        @pl.when(~at_end)
        def _():
            pl.semaphore_wait(barrier, greeted + 2)

    if fast:
        (
            one_d, one_u, one_o, two_d, two_u, two_o, three_d, three_u, three_o,
            one_q, two_q, three_q, one_v, two_v, three_v,
            zx_d, fin_d, zx_u, fin_u, zx_o, fin_o, zx_q, fin_q, zx_v, fin_v,
            psend, precv, zsend, zrecv,
        ) = refs
        rs_d = [
            DpSum("x", stage_d.at[c], one_d.at[c], two_d.at[c], three_d.at[c], psend.at[c], precv.at[c])
            for c in range(CHUNKS)
        ]
        rs_u = [
            DpSum("y", stage_u.at[c], one_u.at[c], two_u.at[c], three_u.at[c], psend.at[3 + c], precv.at[3 + c])
            for c in range(CHUNKS)
        ]
        rs_o = DpSum("x", stage_o, one_o, two_o, three_o, psend.at[6], precv.at[6])
        rs_v = DpSum("x", stage_v, one_v, two_v, three_v, psend.at[7], precv.at[7])

        def couple(c):
            found = []
            for k in range(2):
                tile = 2 * c + k
                staged = stage_u.at[c, :, :, :, :, pl.ds(384 * k, 384)]
                found.append(
                    DpSum(
                        "xy"[k], staged, one_q.at[tile], two_q.at[tile], three_q.at[tile],
                        psend.at[8 + tile], precv.at[8 + tile],
                    )
                )
            return found

        ar_d = [
            SeqSum(three_d.at[c], fin_d.at[c], zx_d.at[c], zsend.at[c], zrecv.at[c]) for c in range(CHUNKS)
        ]
        ar_u = [
            SeqSum(three_u.at[c], fin_u.at[c], zx_u.at[c], zsend.at[3 + c], zrecv.at[3 + c])
            for c in range(CHUNKS)
        ]
        ar_o = SeqSum(three_o, fin_o, zx_o, zsend.at[6], zrecv.at[6])
        ar_v = SeqSum(three_v, fin_v, zx_v, zsend.at[7], zrecv.at[7])
        ar_q = [
            SeqSum(three_q.at[c], fin_q.at[c], zx_q.at[c], zsend.at[8 + c], zrecv.at[8 + c])
            for c in range(PAIRS)
        ]

    def turn(*found):
        for unit_sum in found:
            unit_sum.finish(1)
            unit_sum.start(2)

    def close(*found):
        for unit_sum in found:
            unit_sum.finish(2)

    def per_row(ref):
        return ref[...].reshape(1, -1)

    stage_v[...] = jnp.zeros_like(stage_v)
    sums[...] = jnp.zeros_like(sums)

    def block_at(step):
        b0 = jnp.where(me < 2, seq - 1, 0)
        b1 = jnp.where(me < 2, seq - 2, 1)
        b2 = jnp.where(me == 0, 1, jnp.where(me == 1, 0, jnp.where(me == 2, 3, 2)))
        return jnp.where(step == 0, b0, jnp.where(step == 1, b1, jnp.where(step == 2, b2, me)))

    def loads(step):
        block, slot = block_at(step), step % 2
        return [
            pltpu.make_async_copy(kn_h.at[block], kn.at[slot], in_sem.at[slot, 0]),
            pltpu.make_async_copy(vn_h.at[block], vn.at[slot], in_sem.at[slot, 1]),
            pltpu.make_async_copy(kt_h.at[block], kt.at[slot], in_sem.at[slot, 2]),
        ]

    fills = [pltpu.make_async_copy(qn_h, qn, load_sem.at[HEADS])]
    for h in range(HEADS):
        own = pl.ds(64 * (h % 2), 64)
        fills.append(pltpu.make_async_copy(qt_h.at[h // 2, own], qta.at[h, own], load_sem.at[h]))

    def feed_forward(tok, att_t, cot, w_out, wu, wd, d_norm, bias):
        first = [
            pltpu.make_async_copy(src, dst, ff_sem.at[2, k // GROUPS, k % GROUPS])
            for k, (src, dst) in enumerate(((att_h, att_t), (w_out_h, w_out), (tok_h, tok), (cot_h, cot)))
        ]

        def weights(c):
            found = []
            for d in range(GROUPS):
                at = pl.ds(chunk_columns(ff, c, d), 128)
                to = pl.ds(128 * d, 128)
                found.append(pltpu.make_async_copy(w_up_h.at[:, at], wu.at[c % 2, :, to], ff_sem.at[0, c, d]))
                found.append(pltpu.make_async_copy(w_down_h.at[at], wd.at[c % 2, to], ff_sem.at[1, c, d]))
            return found

        for copy in (*first[:3], *weights(0), *first[3:], *weights(1), *loads(0), *fills):
            copy.start()
        codes = query_codes(lens, me, rows)[:16]
        row16 = lax.broadcasted_iota(jnp.int32, (16, rows), 0)
        for h in range(HEADS):
            other = 64 * (1 - h % 2)
            extra = codes
            for r, part in enumerate(three_parts(-lse[h : h + 1])):
                extra = jnp.where(row16 == 8 + r, part, extra)
            qta[h, other : other + 16] = extra.astype(BF)
            qta[h, other + 16 : other + 64] = jnp.zeros((48, rows), BF)
        meet()
        for copy in first[:3]:
            copy.wait()
        middle = tok[...].astype(F32) + mm(att_t[...].T, w_out[...]) + per_row(b_out)
        average = jnp.mean(middle, axis=-1, keepdims=True)
        centred = middle - average
        scale = lax.rsqrt(jnp.mean(centred * centred, axis=-1, keepdims=True) + EPS)
        unit = centred * scale
        normed = (unit * per_row(gain) + per_row(shift)).astype(BF)
        normed_t = normed.T
        for copy in first[3:]:
            copy.wait()
        d_out = cot[...]
        for c in range(CHUNKS):
            for d in range(GROUPS):
                at = chunk_columns(ff, c, d)
                bias[c : c + 1, 128 * d : 128 * (d + 1)] = b_up[at : at + 128].reshape(1, 128)
        d_mid[...] = middle + per_row(b_down)
        d_norm[...] = jnp.zeros_like(d_norm)

        def one_chunk(c, carry):
            for copy in weights(c):
                copy.wait()
            slot = c % 2
            upper = mm(normed, wu[slot]) + bias[pl.ds(c, 1)]
            cdf = 0.5 * (1.0 + lax.erf(upper * ROOT_HALF))
            hidden = (upper * cdf).astype(BF)
            slope = cdf + upper * (jnp.exp(-0.5 * upper * upper) * 0.3989422804014327)
            d_upper = (mm_nt(d_out, wd[slot]) * slope).astype(BF)
            vec_up[pl.ds(c, 1)] = jnp.sum(d_upper.astype(F32), axis=0, keepdims=True)
            if fast:

                @pl.when(c == 1)
                def _():
                    for unit_sum in (rs_d[0], rs_u[0]):
                        unit_sum.finish(0)
                        unit_sum.start(1)

                @pl.when(c == 2)
                def _():
                    for unit_sum in (rs_d[1], rs_u[1]):
                        unit_sum.finish(0)

            g_down = mm(hidden.T, d_out).astype(BF)
            g_up = mm(normed_t, d_upper).astype(BF)
            for d in range(GROUPS):
                stage_d[(c, *place_of(d))] = g_down[128 * d : 128 * (d + 1)]
                stage_u[(c, *place_of(d))] = g_up[96 * d : 96 * (d + 1)]
            if fast:
                for k in range(CHUNKS):

                    @pl.when(c == k)
                    def _():
                        rs_d[k].start(0)
                        rs_u[k].start(0)
                        if k == 2:
                            turn(rs_d[0], rs_u[0])
                            rs_d[1].start(1)
                            rs_u[1].start(1)

            d_mid[...] += mm(hidden, wd[slot])
            d_norm[...] += mm_nt(d_upper, wu[slot])

            @pl.when(c == 0)
            def _():
                for copy in weights(2):
                    copy.start()

            return carry

        lax.fori_loop(0, CHUNKS, one_chunk, 0)
        d_normed = d_norm[...]
        tok[...] = d_mid[...].astype(BF)
        keep_layer = pltpu.make_async_copy(tok, layer_o, out_sem.at[5])
        keep_layer.start()
        sums[7:8] = jnp.sum(d_out.astype(F32), axis=0, keepdims=True)
        sums[5:6] = jnp.sum(d_normed * unit, axis=0, keepdims=True)
        sums[6:7] = jnp.sum(d_normed, axis=0, keepdims=True)
        scaled = d_normed * per_row(gain)
        d_middle = d_out.astype(F32) + scale * (
            scaled
            - jnp.mean(scaled, axis=-1, keepdims=True)
            - unit * jnp.mean(scaled * unit, axis=-1, keepdims=True)
        )
        d_mid[...] = d_middle
        d_branch = d_middle.astype(BF)
        sums[4:5] = jnp.sum(d_branch.astype(F32), axis=0, keepdims=True)
        g_out = mm(att_t[...], d_branch).astype(BF)
        for d in range(GROUPS):
            stage_o[place_of(d)] = g_out[96 * d : 96 * (d + 1)]
        if fast:
            rs_o.start(0)
            close(rs_d[0], rs_u[0])
            ar_d[0].ends_send()
            ar_u[0].ends_send()
        d_attended = mm_nt(d_branch, w_out[...]).astype(BF)
        d_att[...] = d_attended
        turned = d_attended.T
        product = turned.astype(F32) * att_t[...].astype(F32)
        row16 = lax.broadcasted_iota(jnp.int32, (16, rows), 0)
        for h in range(HEADS):
            own, other = 64 * (h % 2), 64 * (1 - h % 2)
            dta[h, own : own + 64] = turned[64 * h : 64 * (h + 1)]
            delta = jnp.sum(product[64 * h : 64 * (h + 1)], axis=0, keepdims=True)
            extra = jnp.zeros((16, rows), F32)
            for r, part in enumerate(three_parts(-delta)):
                extra = jnp.where(row16 == r, part, extra)
            dta[h, other : other + 16] = extra.astype(BF)
            dta[h, other + 16 : other + 64] = jnp.zeros((48, rows), BF)
        if not fast:
            keep = [
                pltpu.make_async_copy(stage_d, gd_o, out_sem.at[0]),
                pltpu.make_async_copy(stage_u, gu_o, out_sem.at[1]),
                pltpu.make_async_copy(stage_o, go_o, out_sem.at[2]),
            ]
            for copy in keep:
                copy.start()
            for copy in keep:
                copy.wait()
        keep_layer.wait()

    pl.run_scoped(
        feed_forward,
        pltpu.VMEM((rows, width), BF),
        pltpu.VMEM((width, rows), BF),
        pltpu.VMEM((rows, width), BF),
        pltpu.VMEM((width, width), BF),
        pltpu.VMEM((2, width, span), BF),
        pltpu.VMEM((2, span, width), BF),
        pltpu.VMEM((rows, width), F32),
        pltpu.VMEM((8, span), F32),
    )

    def dx_stage(step, half):
        return stage_d.at[step // 2, step % 2, half]

    def dx_copy(way, step, block, half):
        return pltpu.make_async_remote_copy(
            src_ref=dx_stage(step, half), dst_ref=rx.at[block + way, half],
            send_sem=dsend.at[way, block, half], recv_sem=drecv.at[way, block, half],
            device_id={"seq": jnp.maximum(me - 1, 0) if way == 0 else jnp.minimum(me + 1, seq - 1)}, device_id_type=MESH,
        )

    def store_dx(step, half, value):
        for k in range(2):
            stage_d[step // 2, step % 2, half, k] = value[128 * k : 128 * (k + 1)]

    def relay_at(place, way, step, half):
        @pl.when(me == place)
        def _():
            block = block_at(step)
            dx_copy(way, step, block, half).wait_recv()
            add_parts(dx_stage(step, half), rx.at[block + way, half], 2)
            dx_copy(way, step, block, half).start()

    def relay_far(step, half):
        relay_at(1, 1, step, half)
        relay_at(2, 0, step, half)

    def relay_near(half):
        relay_at(1, 0, 2, half)
        relay_at(2, 1, 2, half)

    def send_dx(step, half):
        block = block_at(step)

        @pl.when(me == 0)
        def _():
            dx_copy(1, step, block, half).start()

        @pl.when(me == seq - 1)
        def _():
            dx_copy(0, step, block, half).start()

    def attention(xt, dqt, gk, gv, dk, dv, dq, wp, hot_ref):
        def load_x(step):
            return pltpu.make_async_copy(xt_h.at[block_at(step)], xt, in_sem.at[0, 3])

        load_wp = pltpu.make_async_copy(wp_h, wp, load_sem.at[HEADS + 1])
        for copy in (load_x(0), load_wp):
            copy.start()
        low, high = lane_halves()
        dqt[...] = jnp.zeros_like(dqt)
        lane = lax.broadcasted_iota(jnp.int32, (1, 128), 1)
        v_low = jnp.where(lane < 3, 1.0, 0.0).astype(BF)
        v_high = jnp.where((lane >= 64) & (lane < 67), 1.0, 0.0).astype(BF)
        if fast:
            for unit_sum in rs_d:
                unit_sum.wait_sends((0,))
        for copy in fills:
            copy.wait()

        def hooks(g):
            if not fast:
                return

            def at(when, action):
                @pl.when(g == when)
                def _():
                    action()

            def second():
                turn(rs_d[1], rs_u[1])
                for unit_sum in (rs_d[2], rs_u[2], rs_o):
                    unit_sum.finish(0)
                    unit_sum.start(1)

            at(6, lambda: (second(), ar_d[0].middles_swap(), ar_u[0].middles_swap()))
            at(12, lambda: (close(rs_d[1], rs_u[1]), ar_d[1].ends_send(), ar_u[1].ends_send()))
            at(14, lambda: relay_far(0, 0))
            at(16, lambda: (ar_d[0].middles_send(), ar_u[0].middles_send()))
            at(17, lambda: turn(rs_d[2], rs_u[2]))
            at(20, lambda: relay_far(0, 1))
            at(21, lambda: (turn(rs_o), close(rs_d[2], rs_u[2])))
            at(23, lambda: (close(rs_o), [unit.ends_send() for unit in (ar_d[2], ar_u[2], ar_o)]))

        def products(slot, i, part=slice(None)):
            at = pl.ds(pl.multiple_of(i * 128, 128), 128)
            keys, values = kn[slot, i, part], vn[slot, i, part]
            q_pair, d_pair = qn[i], d_att[:, at]
            hot = hot_ref[part]
            scores = [
                mm(keys * low + hot * high, qta[2 * i]),
                mm(keys * high + hot * low, qta[2 * i + 1]),
            ]
            slopes = [
                mm(values * low + v_high, dta[2 * i]),
                mm(values * high + v_low, dta[2 * i + 1]),
            ]
            d_keys = jnp.zeros((keys.shape[0], 128), F32)
            d_values = jnp.zeros((keys.shape[0], 128), F32)
            for j in range(2):
                h = 2 * i + j
                mask = low if j == 0 else high
                probs = jnp.exp(scores[j])
                d_scores = (probs * slopes[j]).astype(BF)
                d_values = d_values + mm(probs.astype(BF), d_pair * mask)
                d_keys = d_keys + mm(d_scores, q_pair * mask)
                dqt[h] += mm(kt[slot, i, 64 * j : 64 * (j + 1), part], d_scores)
            dk[part, at] = d_keys.astype(BF)
            dv[part, at] = d_values.astype(BF)

        def enter(step):
            for copy in loads(step):
                copy.wait()
            hot_ref[...] = key_codes(lens, block_at(step), rows)

        enter(0)
        for copy in loads(1):
            copy.start()

        def one_half(half, carry):
            part = pl.ds(pl.multiple_of(half * half_rows, half_rows), half_rows)

            def one_pair(i, carry):
                hooks(half * PAIRS + i)
                products(0, i, part)
                return carry

            lax.fori_loop(0, PAIRS, one_pair, 0)

            @pl.when(half == 0)
            def _():
                load_wp.wait()

            store_dx(0, half, (mm_nt(dk[part], wp[1]) + mm_nt(dv[part], wp[2])).astype(BF))
            send_dx(0, half)
            return carry

        lax.fori_loop(0, 2, one_half, 0)
        load_x(0).wait()
        gk[...] = mm(xt[...], dk[...])
        gv[...] = mm(xt[...], dv[...])
        load_x(1).start()
        sums[3:4] = jnp.sum(dv[...].astype(F32), axis=0, keepdims=True)

        def one_step(step, carry):
            slot = step % 2
            enter(step)
            for copy in loads(step + 1):
                copy.start()

            def one_pair(i, carry):
                hooks((step + 1) * PAIRS + i)
                products(slot, i)
                return carry

            lax.fori_loop(0, PAIRS, one_pair, 0)
            dx = (mm_nt(dk[...], wp[1]) + mm_nt(dv[...], wp[2])).astype(BF)
            for half in range(2):
                store_dx(step, half, dx[half * half_rows : (half + 1) * half_rows])
                send_dx(step, half)
            load_x(step).wait()
            gk[...] += mm(xt[...], dk[...])
            gv[...] += mm(xt[...], dv[...])
            load_x(step + 1).start()
            sums[3:4] += jnp.sum(dv[...].astype(F32), axis=0, keepdims=True)
            return carry

        lax.fori_loop(1, seq - 1, one_step, 0)

        last = (seq - 1) % 2
        enter(seq - 1)
        load_x(seq - 1).wait()
        lane_w = lax.broadcasted_iota(jnp.int32, (width, 128), 1)
        lo = lane_w < 64
        if fast:
            for unit_sum in rs_u:
                unit_sum.wait_sends((0,))

        def one_couple(c, carry):
            if fast:

                @pl.when(c == 0)
                def _():
                    relay_near(0)
                    ar_d[1].middles_swap()
                    ar_u[1].middles_swap()

                @pl.when(c == 1)
                def _():
                    relay_near(1)
                    relay_far(1, 0)

                @pl.when(c == 2)
                def _():
                    relay_far(1, 1)
                    ar_d[1].middles_send()
                    ar_u[1].middles_send()

                @pl.when(c >= 1)
                def _():
                    for unit in couple(c - 1):
                        unit.finish(0)
                        unit.start(1)

                @pl.when(c >= 2)
                def _():
                    turn(*couple(c - 2))


            def one_pair(k, carry):
                products(last, 2 * c + k)
                return carry

            lax.fori_loop(0, 2, one_pair, 0)
            at = pl.ds(pl.multiple_of(c * 256, 256), 256)
            turned = dqt[pl.ds(4 * c, 4)].reshape(256, rows) * (HEAD**-0.5)
            dq_part = turned.T.astype(BF)
            dq[:, at] = dq_part
            x_t = xt[...]
            gq_part = mm(x_t, dq_part)
            gk_part = gk[:, at] + mm(x_t, dk[:, at])
            gv_part = gv[:, at] + mm(x_t, dv[:, at])
            for k in range(2):
                cut = slice(128 * k, 128 * (k + 1))
                q_tile, v_tile = gq_part[:, cut], gv_part[:, cut]
                k_tile = pltpu.roll(gk_part[:, cut], 64, 1)
                tiles = jnp.where(lo, q_tile, k_tile), jnp.where(lo, v_tile, q_tile), jnp.where(lo, k_tile, v_tile)
                for j, tile in enumerate(tiles):
                    tile = tile.astype(BF)
                    to = slice(384 * k + 128 * j, 384 * k + 128 * (j + 1))
                    for d in range(GROUPS):
                        stage_u[(c, *place_of(d), slice(None), to)] = tile[part_w * d : part_w * (d + 1)]
            if fast:
                for unit in couple(c):
                    unit.start(0)
            return carry

        lax.fori_loop(0, PAIRS // 2, one_couple, 0)
        if not fast:
            for step in range(2):
                for half in range(2):
                    relay_far(step, half)
            relay_near(0)
            relay_near(1)
        dx_own = gk.at[pl.ds(0, rows)]
        dx_own[...] = mm_nt(dk[...], wp[1]) + mm_nt(dv[...], wp[2]) + mm_nt(dq[...], wp[0])
        sums[3:4] += jnp.sum(dv[...].astype(F32), axis=0, keepdims=True)
        sums[2:3] = jnp.sum(dq[...].astype(F32), axis=0, keepdims=True)
        load_tok = pltpu.make_async_copy(tok_h, dv, load_sem.at[HEADS + 2])
        load_tok.start()
        if fast:
            for unit in couple(2):
                unit.finish(0)
                unit.start(1)
            turn(*couple(1))
            close(*couple(0))
            ar_d[2].middles_swap()
            turn(*couple(2))
            ar_u[2].middles_swap()
            close(*couple(1), *couple(2))
            ar_o.middles_swap()
            for unit in ar_q:
                unit.ends_send()
            ar_d[2].middles_send()
            ar_u[2].middles_send()

        load_tok.wait()
        for way, there in ((0, has_right), (1, has_left)):
            @pl.when(there)
            def _():
                for half in range(2):
                    dx_copy(way, 0, me, half).wait_recv()

                def some(k, carry):
                    at = pl.ds(pl.multiple_of(k * 32, 32), 32)
                    piece = rx[me + way, k // 8, k // 4 % 2, pl.ds(pl.multiple_of(k % 4 * 32, 32), 32)]
                    dx_own[at] += piece.astype(F32)
                    return carry

                lax.fori_loop(0, rows // 32, some, 0)

        values = dv[...].astype(F32)
        centred = values - jnp.mean(values, axis=-1, keepdims=True)
        scale = lax.rsqrt(jnp.mean(centred * centred, axis=-1, keepdims=True) + EPS)
        unit_rows = centred * scale
        d_normed = dx_own[...]
        sums[0:1] = jnp.sum(d_normed * unit_rows, axis=0, keepdims=True)
        sums[1:2] = jnp.sum(d_normed, axis=0, keepdims=True)
        rows8 = sums[...]
        for d in range(GROUPS):
            y, x, core = place_of(d)
            stage_v[y, x, core, 0:8, 0:part_w] = rows8[:, part_w * d : part_w * (d + 1)]
            stage_v[y, x, core, 8 : 8 + CHUNKS] = vec_up[0:CHUNKS, 128 * d : 128 * (d + 1)]
        if fast:
            rs_v.start(0)
        if fast:
            ar_o.middles_send()
            ar_q[0].middles_swap()
        scaled = d_normed * per_row(gain_one)
        dk[...] = (
            d_mid[...]
            + scale
            * (
                scaled
                - jnp.mean(scaled, axis=-1, keepdims=True)
                - unit_rows * jnp.mean(scaled * unit_rows, axis=-1, keepdims=True)
            )
        ).astype(BF)
        keep = [pltpu.make_async_copy(dk, tok_o, out_sem.at[6])]
        keep[0].start()
        if fast:
            ar_q[1].middles_swap()
            rs_v.finish(0)
            rs_v.start(1)
            ar_q[2].middles_swap()
            ar_q[0].middles_send()
            rs_v.finish(1)
            rs_v.start(2)
            ar_q[3].middles_swap()
            ar_q[1].middles_send()
            rs_v.finish(2)
            ar_v.ends_send()
            ar_q[4].middles_swap()
            ar_q[2].middles_send()
            ar_q[5].middles_swap()
            ar_q[3].middles_send()
            ar_v.middles_swap()
            ar_q[4].middles_send()
            ar_q[5].middles_send()
            ar_v.middles_send()
            done = ((ar_d, fin_d, fin_d_o), (ar_u, fin_u, fin_u_o), ((ar_o,), fin_o, fin_o_o), (ar_q, fin_q, fin_q_o), ((ar_v,), fin_v, fin_v_o))
            for k, (units, src, dst) in enumerate(done):
                for unit in units:
                    unit.finish()
                keep.append(pltpu.make_async_copy(src, dst, out_sem.at[k]))
                keep[-1].start()
            for unit in (*rs_d, *rs_u):
                unit.wait_sends((1, 2))
            for unit in (rs_o, rs_v, *couple(0), *couple(1), *couple(2)):
                unit.wait_sends((0, 1, 2))
        else:
            for k, (src, dst) in enumerate(((stage_u, gq_o), (stage_v, stage_v_o))):
                keep.append(pltpu.make_async_copy(src, dst, out_sem.at[k]))
                keep[-1].start()
        for copy in keep:
            copy.wait()

        for place, first, second in ((0, 1, 1), (1, 1, 0), (2, 0, 1), (3, 0, 0)):
            @pl.when(me == place)
            def _():
                for step, way in enumerate((first, first, second)):
                    for half in range(2):
                        dx_copy(way, step, block_at(step), half).wait_send()

    pl.run_scoped(
        attention,
        pltpu.VMEM((width, rows), BF),
        pltpu.VMEM((HEADS, HEAD, rows), F32),
        pltpu.VMEM((width, width), F32),
        pltpu.VMEM((width, width), F32),
        pltpu.VMEM((rows, width), BF),
        pltpu.VMEM((rows, width), BF),
        pltpu.VMEM((rows, width), BF),
        pltpu.VMEM((3, width, width), BF),
        pltpu.VMEM((rows, 128), BF),
    )


def layer_back(fast, *args):
    kn, wp = args[0], args[6]
    seq, _, rows, _ = kn.shape
    width = wp.shape[1]
    span = GROUPS * 128
    part = width // GROUPS
    any_spec = pl.BlockSpec(memory_space=pl.ANY)
    vmem = pl.BlockSpec(memory_space=pltpu.VMEM)
    sds = jax.ShapeDtypeStruct
    cube = (2, 2, 2)
    outs = [sds((rows, width), BF), sds((rows, width), BF)]
    if fast:
        outs += [
            sds((CHUNKS, 128, width), BF), sds((CHUNKS, part, span), BF), sds((part, width), BF),
            sds((PAIRS, part, 384), BF), sds((16, 128), F32),
        ]
    else:
        outs += [
            sds((CHUNKS, *cube, 128, width), BF), sds((CHUNKS, *cube, part, span), BF), sds((*cube, part, width), BF),
            sds((CHUNKS, *cube, part, span), BF), sds((*cube, 16, 128), F32),
        ]
    scratch = [
        pltpu.VMEM((CHUNKS, *cube, 128, width), BF),
        pltpu.VMEM((CHUNKS, *cube, part, span), BF),
        pltpu.VMEM((*cube, part, width), BF),
        pltpu.VMEM((*cube, 16, 128), F32),
        pltpu.VMEM((8, width), F32),
        pltpu.VMEM((8, span), F32),
        pltpu.VMEM((rows, width), BF),
        pltpu.VMEM((HEADS, 128, rows), BF),
        pltpu.VMEM((rows, width), F32),
        pltpu.VMEM((seq + 1, 2, 2, 128, width), BF),
        pltpu.VMEM((2, PAIRS, rows, 128), BF),
        pltpu.VMEM((2, PAIRS, rows, 128), BF),
        pltpu.VMEM((2, PAIRS, 128, rows), BF),
        pltpu.VMEM((HEADS, 128, rows), BF),
        pltpu.VMEM((PAIRS, rows, 128), BF),
        pltpu.SemaphoreType.DMA((3, CHUNKS, GROUPS)),
        pltpu.SemaphoreType.DMA((2, 4)),
        pltpu.SemaphoreType.DMA((HEADS + 3,)),
        pltpu.SemaphoreType.DMA((7,)),
        pltpu.SemaphoreType.DMA((2, 4, 2)),
        pltpu.SemaphoreType.DMA((2, 4, 2)),
    ]
    if fast:
        d, u, o, q = (128, width), (part, span), (part, width), (part, 384)
        scratch += [
            pltpu.VMEM(shape, BF)
            for shape in (
                (CHUNKS, 2, 2, *d), (CHUNKS, 2, 2, *u), (2, 2, *o), (CHUNKS, 2, *d), (CHUNKS, 2, *u), (2, *o),
                (CHUNKS, *d), (CHUNKS, *u), o, (PAIRS, 2, 2, *q), (PAIRS, 2, *q), (PAIRS, *q),
            )
        ]
        scratch += [pltpu.VMEM((2, 2, 16, 128), F32), pltpu.VMEM((2, 16, 128), F32), pltpu.VMEM((16, 128), F32)]
        for shape in ((CHUNKS, *d), (CHUNKS, *u), o, (PAIRS, *q)):
            scratch += [pltpu.VMEM(shape, BF)] * 2
        scratch += [pltpu.VMEM((16, 128), F32)] * 2
        scratch += [pltpu.SemaphoreType.DMA((14, 3))] * 4
    return pl.pallas_call(
        partial(layer_back_kernel, fast),
        out_shape=outs,
        in_specs=[any_spec] * 13 + [vmem, pl.BlockSpec(memory_space=pltpu.SMEM)] + [vmem] * 6,
        out_specs=[any_spec] * len(outs),
        scratch_shapes=scratch,
        compiler_params=pltpu.CompilerParams(
            collective_id=1, has_side_effects=True, vmem_limit_bytes=62 * MIB
        ),
        name="layer_back",
    )(*args)


def unpack_kernel(
    fin_d, fin_u, fin_o, fin_q, fin_v, layer, grad, layer_o, grad_o, down_o, up_o, out_o, qkv_o, *refs
):
    *vec_o, a_d, a_u, a_o, a_q, down, up, out, qkv, held, in_sem, out_sem = refs
    inward = [
        pltpu.make_async_copy(src, dst, in_sem.at[k])
        for k, (src, dst) in enumerate(
            ((fin_u, a_u), (fin_d, a_d), (fin_q, a_q), (fin_o, a_o), (layer, held.at[0]), (grad, held.at[1]))
        )
    ]
    outward = [
        pltpu.make_async_copy(src, dst, out_sem.at[k])
        for k, (src, dst) in enumerate(
            ((up, up_o), (down, down_o), (qkv, qkv_o), (out, out_o), (held.at[0], layer_o), (held.at[1], grad_o))
        )
    ]
    for copy in inward:
        copy.start()
    chunks, _, _ = a_d.shape
    part = a_u.shape[1]
    inward[0].wait()
    for c in range(chunks):
        for d in range(GROUPS):
            at = chunk_columns(up.shape[1], c, d)
            up[:, at : at + 128] = a_u[c, :, 128 * d : 128 * (d + 1)].astype(F32)
    outward[0].start()
    inward[1].wait()
    for c in range(chunks):
        down[128 * c : 128 * (c + 1)] = a_d[c].astype(F32)
    outward[1].start()
    inward[2].wait()
    for i in range(PAIRS):
        qkv[:, 384 * i : 384 * (i + 1)] = a_q[i].astype(F32)
    outward[2].start()
    inward[3].wait()
    out[...] = a_o[...].astype(F32)
    outward[3].start()
    for k in (4, 5):
        inward[k].wait()
        outward[k].start()
    for r in range(8):
        vec_o[r][...] = fin_v[r : r + 1, :part].reshape(part)
    vec_o[8][...] = jnp.concatenate([fin_v[8 + c : 9 + c] for c in range(chunks)], axis=1).reshape(128 * chunks)
    for copy in outward:
        copy.wait()


def unpack(fin_d, fin_u, fin_o, fin_q, fin_v, layer, grad):
    vmem = pl.BlockSpec(memory_space=pltpu.VMEM)
    any_spec = pl.BlockSpec(memory_space=pl.ANY)
    chunks, _, width = fin_d.shape
    part, span = fin_u.shape[1:]
    sds = jax.ShapeDtypeStruct
    large = [(128 * chunks, width), (part, span * chunks), (part, width), (part, PAIRS * fin_q.shape[2])]
    outs = [sds(layer.shape, BF), sds(grad.shape, BF)] + [sds(shape, F32) for shape in large]
    outs += [sds((part,), F32)] * 8 + [sds((128 * chunks,), F32)]
    return pl.pallas_call(
        unpack_kernel, out_shape=outs, in_specs=[any_spec] * 4 + [vmem] + [any_spec] * 2,
        out_specs=[any_spec] * 6 + [vmem] * 9,
        scratch_shapes=[
            *(pltpu.VMEM(ref.shape, BF) for ref in (fin_d, fin_u, fin_o, fin_q)),
            *(pltpu.VMEM(shape, F32) for shape in large),
            pltpu.VMEM((2, *layer.shape), BF),
            pltpu.SemaphoreType.DMA((6,)),
            pltpu.SemaphoreType.DMA((6,)),
        ],
        compiler_params=pltpu.CompilerParams(vmem_limit_bytes=60 * MIB),
        name="unpack",
    )(fin_d, fin_u, fin_o, fin_q, fin_v, layer, grad)


def local(
    tokens, cell_lengths, ln1_gain, ln1_shift, w_qkv, b_query, b_value, w_out, b_out,
    ln2_gain, ln2_shift, w_up, b_up, w_down, b_down, cotangent,
):
    bucket_count, local_slots, width = tokens.shape
    ff = w_up.shape[1]
    seq_count = lax.axis_size("seq")
    dp_count = lax.axis_size("dp")
    fast = dp_count == GROUPS
    rows = bucket_count * local_slots
    flat = tokens.reshape(rows, width)
    kn, vn, kt, xt, qn, qt, wp, att_t, lse = gather_attend(
        flat, cell_lengths, ln1_gain, ln1_shift, w_qkv, b_query, b_value, seq_count
    )
    layer_out, tokens_grad, *found = layer_back(
        fast, kn, vn, kt, xt, qn, qt, wp, att_t, flat, cotangent.reshape(rows, width), w_out, w_up, w_down,
        lse, cell_lengths, ln1_gain, b_out, ln2_gain, ln2_shift, b_up, b_down,
    )
    if fast:
        layer_out, tokens_grad, down, up, out, qkv, *vectors = unpack(*found, layer_out, tokens_grad)
    else:

        def summed(g):
            share = lax.psum_scatter(g, "dp", scatter_dimension=0, tiled=True)
            return lax.psum(share, "seq").astype(F32)

        g_down, g_up, g_out, g_qkv, packed = found
        g_qkv = g_qkv.reshape(CHUNKS, width, GROUPS * 128)[:, :, :768]
        g_qkv = jnp.moveaxis(g_qkv, 0, 1).reshape(width, 3 * width)
        g_down = jnp.moveaxis(g_down.reshape(CHUNKS, GROUPS, 128, width), 0, 1).reshape(ff, width)
        g_up = jnp.transpose(g_up.reshape(CHUNKS, width, GROUPS, 128), (1, 2, 0, 3)).reshape(width, ff)
        down, up, out, qkv = summed(g_down), summed(g_up), summed(g_out.reshape(width, width)), summed(g_qkv)
        packed = packed.reshape(GROUPS, 16, 128)
        vectors = [packed[:, r, : width // GROUPS].reshape(width) for r in range(8)]
        vectors.append(packed[:, 8 : 8 + CHUNKS].reshape(ff))
        together = jnp.concatenate([v.reshape(dp_count, -1) for v in vectors], axis=1)
        together = lax.psum(together, ("dp", "seq"))
        mine = lax.dynamic_index_in_dim(together, lax.axis_index("dp"), 0, keepdims=False)
        sizes = [v.shape[0] // dp_count for v in vectors]
        vectors = [mine[sum(sizes[:k]) : sum(sizes[: k + 1])] for k in range(len(sizes))]
    layer_out = layer_out.reshape(tokens.shape)
    tokens_grad = tokens_grad.reshape(tokens.shape)
    g1, s1, bq, bv, bo, g2, s2, bd, bu = vectors
    return layer_out, tokens_grad, g1, s1, qkv, bq, bv, out, bo, g2, s2, up, bu, down, bd


def solution(mesh):
    token_spec = P("dp", "seq", None)
    vector, matrix = P("dp"), P("dp", None)
    placed = (token_spec, P("dp", None)) + (P(),) * 13 + (token_spec,)
    return jax.shard_map(
        local,
        mesh=mesh,
        in_specs=placed,
        out_specs=(
            token_spec, token_spec, vector, vector, matrix, vector, vector, matrix, vector,
            vector, vector, matrix, vector, matrix, vector,
        ),
        check_vma=False,
    )
```
